32 devices in a mesh: dp: 4 (over x, core), seq: 8 (over z, y).
Axes of the slice: x: 2, y: 2, z: 4, core: 2. Of those that a mesh axis runs over, the one named last changes fastest.
Arguments:
- tokens: bfloat16 [16384, 1024], P(('dp', 'seq')), may hold values from -6 to 6
- mixer_gain: bfloat16 [1024], P('seq'), may hold values from 0.099609375 to 1.8984375
- in_weight: bfloat16 [1024, 3072], P('seq', 'dp'), may hold values from -0.1875 to 0.1875
- conv_weight: bfloat16 [3, 1024], P(None, 'seq'), may hold values from -3.5 to 3.5
- out_weight: bfloat16 [1024, 1024], P('seq', 'dp'), may hold values from -0.1875 to 0.1875
- feed_gain: bfloat16 [1024], P('seq'), may hold values from 0.099609375 to 1.8984375
- gate_weight: bfloat16 [1024, 4608], P('seq', 'dp'), may hold values from -0.1875 to 0.1875
- up_weight: bfloat16 [1024, 4608], P('seq', 'dp'), may hold values from -0.1875 to 0.1875
- down_weight: bfloat16 [4608, 1024], P('seq', 'dp'), may hold values from -0.09375 to 0.09375
- lengths: int32 [4, 1], P('dp'), may hold values from 1024 to 4096, as said below
- cotangent: bfloat16 [16384, 1024], P(('dp', 'seq')), may hold values from -6 to 6
Outputs:
- output: bfloat16 [16384, 1024], P(('dp', 'seq'))
- grad_tokens: bfloat16 [16384, 1024], P(('dp', 'seq'))
- grad_mixer_gain: float32 [1024], P('seq')
- grad_in_weight: float32 [1024, 3072], P('seq', 'dp')
- grad_conv_weight: float32 [3, 1024], P(None, 'seq')
- grad_out_weight: float32 [1024, 1024], P('seq', 'dp')
- grad_feed_gain: float32 [1024], P('seq')
- grad_gate_weight: float32 [1024, 4608], P('seq', 'dp')
- grad_up_weight: float32 [1024, 4608], P('seq', 'dp')
- grad_down_weight: float32 [4608, 1024], P('seq', 'dp')
The draws below stay inside these ranges and needn't reach their ends.
Inputs may be any that keep to these rules, and one draw needn't show every extreme that they name: `lengths`: each slot of 4096 rows holds one sequence from its first row on, padding after it; at least one slot of the batch is full.
All inputs are finite; a program needn't handle non-finite values.
Results may differ from the reference program's by a relative error of at most 0.0097.
Values may be sent and summed in bfloat16 or wider, within the bound.
No kernel may reach another device: no remote copies, remote signals or barrier semaphores. Data moves between devices by JAX's collectives and lax.ppermute only.
A program may use at most 256 MiB of HBM per device.

```python
import jax
import jax.numpy as jnp
from jax import lax

MODEL_WIDTH = 1024
FF = 4608
TOKEN_SLOTS = 4096
SEQUENCE_SLOTS = 1
TOKENS = 16384
N_DP = 4


def draw_lengths(key, part):
    offset_start = jax.random.randint(key, (N_DP, SEQUENCE_SLOTS), TOKEN_SLOTS // 4, TOKEN_SLOTS + 1)
    picked_slots = jax.random.randint(jax.random.fold_in(key, 7), (), 0, N_DP * SEQUENCE_SLOTS)
    flattened_indices = jnp.arange(N_DP * SEQUENCE_SLOTS, dtype=jnp.int32).reshape(N_DP, SEQUENCE_SLOTS)
    return jnp.where(flattened_indices == picked_slots, TOKEN_SLOTS, offset_start).astype(jnp.int32)


def block_scale(own_key, dims, pieces, low, largest):
    level = 1.0
    for position, shards_of in pieces:
        steps = jax.random.uniform(jax.random.fold_in(jax.random.fold_in(own_key, 6), position), (shards_of,), jnp.float32, low / len(pieces), largest / len(pieces))
        level = level * jnp.repeat(jnp.exp(steps), dims[position] // shards_of).reshape((-1,) + (1,) * (len(dims) - 1 - position))
    return level


def scatter_about(own_key, shape, spread, limit, shards=(), kind=jnp.bfloat16):
    values = spread * jax.random.normal(own_key, shape, jnp.float32)
    if shards:
        values = values * block_scale(own_key, shape, shards, -0.22, 0.18)
    return jnp.clip(values, -limit, limit).astype(kind)


def setup_inputs(seed: int = 0) -> dict:
    seeds = jax.random.split(jax.random.key(seed), 12)
    return {
        "tokens": scatter_about(seeds[0], (TOKENS, MODEL_WIDTH), 1.0, 6.0, ((0, 32),)),
        "mixer_gain": jnp.clip(1.0 + 0.18 * jax.random.normal(seeds[1], (MODEL_WIDTH,), jnp.float32), 0.099609375, 1.8984375).astype(jnp.bfloat16),
        "in_weight": scatter_about(seeds[2], (MODEL_WIDTH, 3 * MODEL_WIDTH), MODEL_WIDTH ** -0.5, 0.1875, ((0, 8), (1, 4))),
        "conv_weight": scatter_about(seeds[3], (3, MODEL_WIDTH), 3 ** -0.5, 3.5, ((1, 8),)),
        "out_weight": scatter_about(seeds[4], (MODEL_WIDTH, MODEL_WIDTH), MODEL_WIDTH ** -0.5, 0.1875, ((0, 8), (1, 4))),
        "feed_gain": jnp.clip(1.0 + 0.18 * jax.random.normal(seeds[5], (MODEL_WIDTH,), jnp.float32), 0.099609375, 1.8984375).astype(jnp.bfloat16),
        "gate_weight": scatter_about(seeds[6], (MODEL_WIDTH, FF), MODEL_WIDTH ** -0.5, 0.1875, ((0, 8), (1, 4))),
        "up_weight": scatter_about(seeds[7], (MODEL_WIDTH, FF), MODEL_WIDTH ** -0.5, 0.1875, ((0, 8), (1, 4))),
        "down_weight": scatter_about(seeds[8], (FF, MODEL_WIDTH), FF ** -0.5, 0.09375, ((0, 8), (1, 4))),
        "lengths": draw_lengths(jax.random.fold_in(seeds[11], 71), 0),
        "cotangent": scatter_about(seeds[10], (TOKENS, MODEL_WIDTH), 1.0, 6.0, ((0, 32),)),
    }


norm_eps = 1e-05

@jax.custom_vjp
def low(v):
    return lax.optimization_barrier(v.astype(jnp.bfloat16)).astype(jnp.float32)

@jax.custom_vjp
def low_back(v):
    return v

def low_keep(v):
    return (low(v), None)

def low_pass(kept, grad):
    return (grad,)

def back_keep(v):
    return (v, None)

def back_low(kept, grad):
    return (low(grad),)
low.defvjp(low_keep, low_pass)
low_back.defvjp(back_keep, back_low)

def highest(left_side, right_side):
    return jnp.dot(left_side, right_side, precision=lax.Precision.HIGHEST)

def slot_forward(params, slot_rows, length):
    gain_one, weight_in, conv_taps, weight_out, gain_two, weight_gate, weight_up, weight_down = params
    live_mask = (jnp.arange(TOKEN_SLOTS, dtype=jnp.int32) < length).astype(jnp.float32)[:, None]
    scale_one = lax.rsqrt(lax.optimization_barrier(jnp.mean(slot_rows * slot_rows, axis=1, keepdims=True)) + norm_eps)
    normed_one = low(slot_rows * scale_one * gain_one)
    projected = low_back(highest(normed_one, weight_in))
    b_part = projected[:, :MODEL_WIDTH]
    c_part = projected[:, MODEL_WIDTH:2 * MODEL_WIDTH]
    x_part = projected[:, 2 * MODEL_WIDTH:]
    mixed_in = low(b_part * x_part)
    padded = jnp.pad(mixed_in, ((2, 0), (0, 0)))
    conv_out = conv_taps[0] * padded[:-2] + conv_taps[1] * padded[1:-1] + conv_taps[2] * padded[2:]
    gated = low(c_part * conv_out)
    hidden = slot_rows + low_back(highest(gated, weight_out))
    scale_two = lax.rsqrt(lax.optimization_barrier(jnp.mean(hidden * hidden, axis=1, keepdims=True)) + norm_eps)
    normed_two = low(hidden * scale_two * gain_two)
    gate_val = low_back(highest(normed_two, weight_gate))
    up_val = low_back(highest(normed_two, weight_up))
    activated = low(jax.nn.silu(gate_val) * up_val)
    return live_mask * (hidden + highest(activated, weight_down))

def reference(tokens, mixer_gain, in_weight, conv_weight, out_weight, feed_gain, gate_weight, up_weight, down_weight, lengths, cotangent):
    params = tuple((weight.astype(jnp.float32) for weight in (mixer_gain, in_weight, conv_weight, out_weight, feed_gain, gate_weight, up_weight, down_weight)))
    per_slot_input = tokens.astype(jnp.float32).reshape(N_DP * SEQUENCE_SLOTS, TOKEN_SLOTS, MODEL_WIDTH)
    per_slot_gradients = cotangent.astype(jnp.float32).reshape(N_DP * SEQUENCE_SLOTS, TOKEN_SLOTS, MODEL_WIDTH)
    per_slot_length = lengths.reshape(N_DP * SEQUENCE_SLOTS).astype(jnp.int32)
    checked = jax.checkpoint(slot_forward)

    def visit(totals, slot_item):
        slot_rows, length, grad_rows = slot_item
        result, pullback = jax.vjp(lambda weights, inputs: checked(weights, inputs, length), params, slot_rows)
        grad_params, grad_inputs = pullback(grad_rows)
        totals = jax.tree.map(lambda first, second: first + second, totals, grad_params)
        return (totals, (result, grad_inputs))
    starting = jax.tree.map(jnp.zeros_like, params)
    totals, (results, grad_rows_all) = lax.scan(visit, starting, (per_slot_input, per_slot_length, per_slot_gradients))
    output = results.reshape(TOKENS, MODEL_WIDTH).astype(jnp.bfloat16)
    grad_tokens = grad_rows_all.reshape(TOKENS, MODEL_WIDTH).astype(jnp.bfloat16)
    return (output, grad_tokens, totals[0], totals[1], totals[2], totals[3], totals[4], totals[5], totals[6], totals[7])
```

```python
import functools

import jax
import jax.numpy as jnp
from jax import lax
from jax.experimental import pallas as pl
from jax.experimental.pallas import tpu as pltpu
from jax.sharding import PartitionSpec as P

SLOT_MAX = 8192
HALO = 16
SMALL_ROWS = 16

norm_eps = 1e-05


def multiply(left_side, right_side):
    return jnp.dot(left_side, right_side, preferred_element_type=jnp.float32)


def against(left_side, right_side):
    return lax.dot_general(
        left_side, right_side, (((1,), (1,)), ((), ())), preferred_element_type=jnp.float32
    )


def outer_sum(left_side, right_side):
    return lax.dot_general(
        left_side, right_side, (((0,), (0,)), ((), ())), preferred_element_type=jnp.float32
    )


def rms_forward(values, gain_row):
    scales = lax.rsqrt(jnp.mean(values * values, axis=1, keepdims=True) + norm_eps)
    return (scales, values * scales * gain_row)


def rms_backward(values, scales, gain_row, grad_normed):
    weighted = grad_normed * gain_row
    grad_gain = jnp.sum(grad_normed * values * scales, axis=0)
    inner_mean = jnp.mean(weighted * values, axis=1, keepdims=True)
    return (scales * weighted - values * scales * scales * scales * inner_mean, grad_gain)


def swap(shard, step):
    axis, bit = step
    count = lax.axis_size(axis)
    return lax.ppermute(shard, axis, [(i, i ^ bit) for i in range(count)])


def exchange_gather(block, steps):
    stack = block[None]
    for step in steps[:-1]:
        stack = jnp.concatenate([stack, swap(stack, step)], axis=0)
    return [stack, swap(stack, steps[-1])]


def exchange_scatter(keep, send, steps):
    for step in reversed(steps):
        total = keep.astype(jnp.float32) + swap(send, step).astype(jnp.float32)
        half = total.shape[0] // 2
        if half:
            keep = total[:half].astype(jnp.bfloat16)
            send = total[half:].astype(jnp.bfloat16)
    return total[0]


def masks_at(position, steps):
    masks = {"dp": 0, "seq": 0}
    for place, (axis, bit) in enumerate(steps):
        masks[axis] = masks[axis] + ((position >> place) & 1) * bit
    return masks["dp"], masks["seq"]


def move_blocks(ids, sources, out_shapes, moves):
    def kernel(ids_ref, *refs):
        ins, outs, sems = refs[: len(sources)], refs[len(sources) : -1], refs[-1]
        own_dp, own_seq = ids_ref[0], ids_ref[1]
        for source, target, first, count, steps, views in moves:

            def start(position, carry):
                mask_dp, mask_seq = masks_at(position + first, steps)
                for view in views:
                    a, b = view(
                        ins[source],
                        outs[target],
                        position,
                        own_dp ^ mask_dp,
                        own_seq ^ mask_seq,
                    )
                    pltpu.make_async_copy(a, b, sems.at[target]).start()
                return carry

            lax.fori_loop(0, count, start, 0)
        for place, out in enumerate(outs):
            pltpu.make_async_copy(out, out, sems.at[place]).wait()

    return pl.pallas_call(
        kernel,
        out_shape=out_shapes,
        grid_spec=pltpu.PrefetchScalarGridSpec(
            num_scalar_prefetch=1,
            in_specs=[pl.BlockSpec(memory_space=pl.ANY)] * len(sources),
            out_specs=[pl.BlockSpec(memory_space=pl.ANY)] * len(out_shapes),
            scratch_shapes=[pltpu.SemaphoreType.DMA((len(out_shapes),))],
            grid=(),
        ),
    )(ids, *sources)


def tile_of(ref, row, rows, col, cols):
    return ref.at[pl.ds(pl.multiple_of(row * rows, rows), rows), pl.ds(pl.multiple_of(col * cols, cols), cols)]


def assembled(ids, stacks, steps, shape, view):
    sources, moves = [], []
    for piece, parts in enumerate(stacks):
        first = 0
        for part in parts:
            moves.append(
                (
                    len(sources),
                    0,
                    first,
                    part.shape[0],
                    steps[piece],
                    [lambda a, b, at, dp, seq, piece=piece: (a.at[at], view(b, piece, dp, seq))],
                )
            )
            sources.append(part)
            first += part.shape[0]
    return move_blocks(ids, sources, [jax.ShapeDtypeStruct(shape, jnp.bfloat16)], moves)[0]


def blocks_of(ids, whole, steps, block, view):
    shapes, moves = [], []
    for piece, order in enumerate(steps):
        half = 2 ** (len(order) - 1)
        for first in (0, half):
            moves.append(
                (
                    0,
                    len(shapes),
                    first,
                    half,
                    order,
                    [lambda a, b, at, dp, seq, piece=piece: (view(a, piece, dp, seq), b.at[at])],
                )
            )
            shapes.append(jax.ShapeDtypeStruct((half, *block), jnp.bfloat16))
    parts = move_blocks(ids, [whole], shapes, moves)
    return [(parts[2 * i], parts[2 * i + 1]) for i in range(len(steps))]


def dp_gather(block, steps):
    blocks = [block]
    for step in steps:
        blocks = blocks + [swap(b, step) for b in blocks]
    return blocks


def dp_scatter(parts, steps):
    for step in reversed(steps):
        half = len(parts) // 2
        parts = [
            keep + swap(send.astype(jnp.bfloat16), step).astype(jnp.float32)
            for keep, send in zip(parts[:half], parts[half:])
        ]
    return parts[0]


def bits_below(count):
    return [1 << i for i in range(count.bit_length() - 1)]


def per_device(
    tokens,
    mixer_gain,
    in_weight,
    conv_weight,
    out_weight,
    feed_gain,
    gate_weight,
    up_weight,
    down_weight,
    lengths,
    cotangent,
):
    n_dp, n_seq = lax.axis_size("dp"), lax.axis_size("seq")
    tok_rows, features = tokens.shape
    slot_size = min(SLOT_MAX, tok_rows * n_seq)
    own_dp, own_seq = lax.axis_index("dp"), lax.axis_index("seq")
    ids = jnp.stack([own_dp, own_seq]).astype(jnp.int32)

    seq_bits = bits_below(n_seq)
    along_y = seq_bits[: len(seq_bits) // 2]
    ys = [("seq", b) for b in reversed(along_y)]
    zs = [("seq", b) for b in reversed(seq_bits[len(along_y) :])]
    core = [("dp", 1)]
    xs = [("dp", b) for b in reversed(bits_below(n_dp)[1:])]
    in_orders = [zs + xs + ys + core, zs + ys + xs + core, zs[:1] + ys + xs + zs[1:] + core]
    out_order = zs + ys + xs + core
    gate_order, up_order, down_order = zs + ys, zs + ys, zs[:1] + ys + zs[1:]
    token_order = xs + core

    position = own_seq * tok_rows + jnp.arange(tok_rows, dtype=jnp.int32)
    in_slot = position % slot_size
    slot_index = position // slot_size
    slot_ids = jnp.arange(lengths.shape[1], dtype=jnp.int32)
    slot_length = jnp.sum(
        jnp.where(slot_index[:, None] == slot_ids[None, :], lengths[0][None, :], 0), axis=1
    )
    live_mask = (in_slot < slot_length).astype(jnp.float32)[:, None]
    tap_masks = [(in_slot >= 2 - tap_index).astype(jnp.float32)[:, None] for tap_index in range(3)]

    in_rows, in_cols = in_weight.shape[0], in_weight.shape[1] // 3
    out_rows, out_cols = out_weight.shape
    small = jnp.concatenate([mixer_gain[None], feed_gain[None], conv_weight], axis=0)
    small = jnp.pad(small, ((0, SMALL_ROWS - small.shape[0]), (0, out_cols - small.shape[1])))
    out_block = jnp.concatenate([out_weight, small], axis=0)
    before = lax.ppermute(
        tokens[tok_rows - HALO :], "seq", [(i, i + 1) for i in range(n_seq - 1)]
    )
    in_stacks = []
    for piece, order in enumerate(in_orders):
        shard = in_weight[:, piece * in_cols : (piece + 1) * in_cols]
        in_stacks.append(exchange_gather(shard, order))
    out_stacks = exchange_gather(out_block, out_order)

    def in_view(ref, piece, dp, seq):
        return tile_of(ref, seq, in_rows, dp * 3 + piece, in_cols)

    weight_in = assembled(ids, in_stacks, in_orders, (features, 3 * features), in_view)
    out_moves, first = [], 0
    for source, part in enumerate(out_stacks):
        out_moves.append(
            (
                source,
                0,
                first,
                part.shape[0],
                out_order,
                [
                    lambda a, b, at, dp, seq: (
                        a.at[at, pl.ds(0, out_rows)],
                        tile_of(b, seq, out_rows, dp, out_cols),
                    )
                ],
            )
        )
        out_moves.append(
            (
                source,
                1,
                first,
                part.shape[0],
                out_order,
                [
                    lambda a, b, at, dp, seq: (
                        a.at[at, pl.ds(out_rows, SMALL_ROWS)],
                        b.at[dp, seq],
                    )
                ],
            )
        )
        first += part.shape[0]
    weight_out, smalls = move_blocks(
        ids,
        out_stacks,
        [
            jax.ShapeDtypeStruct((features, features), jnp.bfloat16),
            jax.ShapeDtypeStruct((n_dp, n_seq, SMALL_ROWS, out_cols), jnp.bfloat16),
        ],
        out_moves,
    )
    smalls = smalls[0, :, :5, : mixer_gain.shape[0]].astype(jnp.float32)
    smalls = smalls.transpose(1, 0, 2).reshape(5, features)
    gain_one, gain_two, conv_taps = smalls[0], smalls[1], smalls[2:]

    ratio = n_seq // n_dp
    home = [
        (e * n_seq + s, (s // ratio) * n_seq + e * ratio + s % ratio)
        for e in range(n_dp)
        for s in range(n_seq)
    ]
    down_shard = lax.ppermute(down_weight, ("dp", "seq"), home)
    hidden_units = gate_weight.shape[1]
    gate_rows = gate_weight.shape[0]
    down_rows, down_cols = down_weight.shape
    gate_stacks = exchange_gather(gate_weight, gate_order)
    up_stacks = exchange_gather(up_weight, up_order)
    down_stacks = exchange_gather(down_shard, down_order)

    def gate_view(ref, piece, dp, seq):
        return ref.at[pl.ds(pl.multiple_of(seq * gate_rows, gate_rows), gate_rows)]

    def down_view(ref, piece, dp, seq):
        return tile_of(ref, seq % ratio, down_rows, seq // ratio, down_cols)

    wide = (features, hidden_units)
    weight_gate = assembled(ids, [gate_stacks], [gate_order], wide, gate_view)
    weight_up = assembled(ids, [up_stacks], [up_order], wide, gate_view)
    weight_down = assembled(ids, [down_stacks], [down_order], (hidden_units, features), down_view)

    residual = tokens.astype(jnp.float32)
    extended_rows = jnp.concatenate([before, tokens], axis=0).astype(jnp.float32)
    scale_ext, normed_ext = rms_forward(extended_rows, gain_one)
    normed_ext = normed_ext.astype(jnp.bfloat16)
    scale_one, normed_one = scale_ext[HALO:], normed_ext[HALO:]
    projected = multiply(normed_ext, weight_in)
    mixed_ext = projected[:, :features] * projected[:, 2 * features :]
    b_part = projected[HALO:, :features]
    c_part = projected[HALO:, features : 2 * features]
    x_part = projected[HALO:, 2 * features :]
    extended = mixed_ext[HALO - 2 :].astype(jnp.bfloat16).astype(jnp.float32)
    conv_out = sum(
        (
            tap_masks[tap_index] * conv_taps[tap_index] * extended[tap_index : tap_index + tok_rows]
            for tap_index in range(3)
        )
    )
    gated = (c_part * conv_out).astype(jnp.bfloat16)
    hidden = residual + multiply(gated, weight_out)
    scale_two, normed_mid = rms_forward(hidden, gain_two)
    normed_two = normed_mid.astype(jnp.bfloat16)

    grad_final = (live_mask * cotangent.astype(jnp.float32)).astype(jnp.bfloat16)
    final_all = jnp.concatenate(dp_gather(grad_final, token_order), axis=0)
    normed_all = jnp.concatenate(dp_gather(normed_two, token_order), axis=0)

    def split_rows(v):
        return [v[i * tok_rows : (i + 1) * tok_rows] for i in range(n_dp)]

    gate_val = multiply(normed_all, weight_gate)
    up_val = multiply(normed_all, weight_up)
    sigmoid_gate = jax.nn.sigmoid(gate_val)
    silu_gate = gate_val * sigmoid_gate
    activated = (silu_gate * up_val).astype(jnp.bfloat16)
    feed_out = dp_scatter(split_rows(multiply(activated, weight_down)), token_order)
    output = (live_mask * (hidden + feed_out)).astype(jnp.bfloat16)
    grad_down = outer_sum(activated, final_all).astype(jnp.bfloat16)
    grad_act = against(final_all, weight_down)
    grad_gate = (grad_act * up_val * sigmoid_gate * (1.0 + gate_val * (1.0 - sigmoid_gate))).astype(
        jnp.bfloat16
    )
    grad_up = (grad_act * silu_gate).astype(jnp.bfloat16)
    grad_norm_parts = against(grad_gate, weight_gate) + against(grad_up, weight_up)
    grad_norm_two = dp_scatter(split_rows(grad_norm_parts), token_order)
    grad_gate_w = outer_sum(normed_all, grad_gate).astype(jnp.bfloat16)
    grad_up_w = outer_sum(normed_all, grad_up).astype(jnp.bfloat16)

    def scattered(whole, order, block, view):
        ((keep, send),) = blocks_of(ids, whole, [order], block, view)
        return exchange_scatter(keep, send, order)

    own_down = scattered(grad_down, down_order, down_weight.shape, down_view)
    own_down = lax.ppermute(
        own_down.astype(jnp.bfloat16), ("dp", "seq"), [(b, a) for a, b in home]
    ).astype(jnp.float32)
    own_gate = scattered(grad_gate_w, gate_order, gate_weight.shape, gate_view)
    own_up = scattered(grad_up_w, up_order, up_weight.shape, gate_view)

    grad_from_norm, grad_gain_two = rms_backward(hidden, scale_two, gain_two, grad_norm_two)
    grad_hidden = grad_final.astype(jnp.float32) + grad_from_norm
    grad_branch = grad_hidden.astype(jnp.bfloat16)
    grad_out_w = outer_sum(gated, grad_branch).astype(jnp.bfloat16)

    def out_view(ref, piece, dp, seq):
        return tile_of(ref, seq, out_rows, dp, out_cols)

    own_out = scattered(grad_out_w, out_order, out_weight.shape, out_view)
    grad_gated = against(grad_branch, weight_out)
    grad_conv = grad_gated * c_part
    grad_c = grad_gated * conv_out
    grad_taps = [tap_masks[tap_index] * grad_conv for tap_index in range(3)]
    grad_conv_w = jnp.stack(
        [
            jnp.sum(grad_taps[tap_index] * extended[tap_index : tap_index + tok_rows], axis=0)
            for tap_index in range(3)
        ]
    )
    grad_extended = sum(
        (
            jnp.pad(
                grad_taps[tap_index] * conv_taps[tap_index], ((tap_index, 2 - tap_index), (0, 0))
            )
            for tap_index in range(3)
        )
    )
    returned = lax.ppermute(grad_extended[:2], "seq", [(i + 1, i) for i in range(n_seq - 1)])
    grad_mixed = grad_extended[2:] + jnp.pad(returned, ((tok_rows - 2, 0), (0, 0)))
    grad_proj = jnp.concatenate([grad_mixed * x_part, grad_c, grad_mixed * b_part], axis=1).astype(
        jnp.bfloat16
    )
    grad_in_w = outer_sum(normed_one, grad_proj).astype(jnp.bfloat16)
    in_parts = blocks_of(ids, grad_in_w, in_orders, (in_rows, in_cols), in_view)
    own_in = jnp.concatenate(
        [exchange_scatter(keep, send, order) for (keep, send), order in zip(in_parts, in_orders)],
        axis=1,
    )
    grad_norm_one = against(grad_proj, weight_in)
    grad_from_first, grad_gain_one = rms_backward(residual, scale_one, gain_one, grad_norm_one)
    grad_tokens = (grad_hidden + grad_from_first).astype(jnp.bfloat16)

    sums = jnp.concatenate([grad_gain_one[None], grad_gain_two[None], grad_conv_w], axis=0)
    sums = jnp.pad(sums, ((0, 3), (0, 0)))
    for step in zs + ys + xs + core:
        sums = sums + swap(sums, step)
    columns = mixer_gain.shape[0]
    own_sums = lax.dynamic_slice(sums, (0, own_seq * columns), (8, columns))
    return (
        output,
        grad_tokens,
        own_sums[0],
        own_in,
        own_sums[2:5],
        own_out,
        own_sums[1],
        own_gate,
        own_up,
        own_down,
    )


def solution(mesh):
    in_specs = (
        P(("dp", "seq"), None),
        P("seq"),
        P("seq", "dp"),
        P(None, "seq"),
        P("seq", "dp"),
        P("seq"),
        P("seq", "dp"),
        P("seq", "dp"),
        P("seq", "dp"),
        P("dp", None),
        P(("dp", "seq"), None),
    )
    out_specs = (
        P(("dp", "seq"), None),
        P(("dp", "seq"), None),
        P("seq"),
        P("seq", "dp"),
        P(None, "seq"),
        P("seq", "dp"),
        P("seq"),
        P("seq", "dp"),
        P("seq", "dp"),
        P("seq", "dp"),
    )
    return jax.shard_map(
        per_device, mesh=mesh, in_specs=in_specs, out_specs=out_specs, check_vma=False
    )
```

```python
import functools

import jax
import jax.numpy as jnp
from jax import lax
from jax.experimental import pallas as pl
from jax.experimental.pallas import tpu as pltpu
from jax.sharding import PartitionSpec as P

SLOT_MAX = 8192
HALO = 16
SMALL_ROWS = 16
VMEM_BYTES = 16 << 20

norm_eps = 1e-05


def multiply(left_side, right_side):
    return jnp.dot(left_side, right_side, preferred_element_type=jnp.float32)


def against(left_side, right_side):
    return lax.dot_general(
        left_side, right_side, (((1,), (1,)), ((), ())), preferred_element_type=jnp.float32
    )


def outer_sum(left_side, right_side):
    return lax.dot_general(
        left_side, right_side, (((0,), (0,)), ((), ())), preferred_element_type=jnp.float32
    )


def rms_forward(values, gain_row):
    scales = lax.rsqrt(jnp.mean(values * values, axis=1, keepdims=True) + norm_eps)
    return (scales, values * scales * gain_row)


def rms_backward(values, scales, gain_row, grad_normed):
    weighted = grad_normed * gain_row
    grad_gain = jnp.sum(grad_normed * values * scales, axis=0)
    inner_mean = jnp.mean(weighted * values, axis=1, keepdims=True)
    return (scales * weighted - values * scales * scales * scales * inner_mean, grad_gain)


def swap(shard, step):
    axis, bit = step
    count = lax.axis_size(axis)
    return lax.ppermute(shard, axis, [(i, i ^ bit) for i in range(count)])


def exchange_gather(block, steps):
    stack = block[None]
    for step in steps[:-1]:
        stack = jnp.concatenate([stack, swap(stack, step)], axis=0)
    return [stack, swap(stack, steps[-1])]


def exchange_scatter(keep, send, steps):
    for step in reversed(steps):
        total = keep.astype(jnp.float32) + swap(send, step).astype(jnp.float32)
        half = total.shape[0] // 2
        if half:
            keep = total[:half].astype(jnp.bfloat16)
            send = total[half:].astype(jnp.bfloat16)
    return total[0]


def masks_at(position, steps):
    masks = {"dp": 0, "seq": 0}
    for place, (axis, bit) in enumerate(steps):
        masks[axis] = masks[axis] + ((position >> place) & 1) * bit
    return masks["dp"], masks["seq"]


def move_blocks(ids, sources, out_shapes, moves, into_vmem):
    def kernel(ids_ref, *refs):
        ins, outs, sems = refs[: len(sources)], refs[len(sources) : -1], refs[-1]
        own_dp, own_seq = ids_ref[0], ids_ref[1]
        for source, target, first, count, steps, views in moves:

            def start(position, carry):
                mask_dp, mask_seq = masks_at(position + first, steps)
                for view in views:
                    a, b = view(
                        ins[source],
                        outs[target],
                        position,
                        own_dp ^ mask_dp,
                        own_seq ^ mask_seq,
                    )
                    pltpu.make_async_copy(a, b, sems.at[target]).start()
                return carry

            lax.fori_loop(0, count, start, 0)
        for place, out in enumerate(outs):
            pltpu.make_async_copy(out, out, sems.at[place]).wait()

    return pl.pallas_call(
        kernel,
        out_shape=out_shapes,
        grid_spec=pltpu.PrefetchScalarGridSpec(
            num_scalar_prefetch=1,
            in_specs=[pl.BlockSpec(memory_space=pl.ANY if into_vmem else pltpu.VMEM)] * len(sources),
            out_specs=[pl.BlockSpec(memory_space=pltpu.VMEM if into_vmem else pl.ANY)] * len(out_shapes),
            scratch_shapes=[pltpu.SemaphoreType.DMA((len(out_shapes),))],
            grid=(),
        ),
        compiler_params=pltpu.CompilerParams(vmem_limit_bytes=VMEM_BYTES),
    )(ids, *sources)


def tile_of(ref, row, rows, col, cols):
    return ref.at[pl.ds(pl.multiple_of(row * rows, rows), rows), pl.ds(pl.multiple_of(col * cols, cols), cols)]


def assembled(ids, stacks, steps, shape, view):
    sources, moves = [], []
    for piece, parts in enumerate(stacks):
        first = 0
        for part in parts:
            moves.append(
                (
                    len(sources),
                    0,
                    first,
                    part.shape[0],
                    steps[piece],
                    [lambda a, b, at, dp, seq, piece=piece: (a.at[at], view(b, piece, dp, seq))],
                )
            )
            sources.append(part)
            first += part.shape[0]
    return move_blocks(ids, sources, [jax.ShapeDtypeStruct(shape, jnp.bfloat16)], moves, True)[0]


def blocks_of(ids, whole, steps, block, view):
    shapes, moves = [], []
    for piece, order in enumerate(steps):
        half = 2 ** (len(order) - 1)
        for first in (0, half):
            moves.append(
                (
                    0,
                    len(shapes),
                    first,
                    half,
                    order,
                    [lambda a, b, at, dp, seq, piece=piece: (view(a, piece, dp, seq), b.at[at])],
                )
            )
            shapes.append(jax.ShapeDtypeStruct((half, *block), jnp.bfloat16))
    parts = move_blocks(ids, [whole], shapes, moves, False)
    return [(parts[2 * i], parts[2 * i + 1]) for i in range(len(steps))]


def dp_gather(block, steps):
    blocks = [block]
    for step in steps:
        blocks = blocks + [swap(b, step) for b in blocks]
    return blocks


def dp_scatter(parts, steps):
    for step in reversed(steps):
        half = len(parts) // 2
        parts = [
            keep + swap(send.astype(jnp.bfloat16), step).astype(jnp.float32)
            for keep, send in zip(parts[:half], parts[half:])
        ]
    return parts[0]


def bits_below(count):
    return [1 << i for i in range(count.bit_length() - 1)]


def per_device(
    tokens,
    mixer_gain,
    in_weight,
    conv_weight,
    out_weight,
    feed_gain,
    gate_weight,
    up_weight,
    down_weight,
    lengths,
    cotangent,
):
    n_dp, n_seq = lax.axis_size("dp"), lax.axis_size("seq")
    tok_rows, features = tokens.shape
    slot_size = min(SLOT_MAX, tok_rows * n_seq)
    own_dp, own_seq = lax.axis_index("dp"), lax.axis_index("seq")
    ids = jnp.stack([own_dp, own_seq]).astype(jnp.int32)

    seq_bits = bits_below(n_seq)
    along_y = seq_bits[: len(seq_bits) // 2]
    ys = [("seq", b) for b in reversed(along_y)]
    zs = [("seq", b) for b in reversed(seq_bits[len(along_y) :])]
    core = [("dp", 1)]
    xs = [("dp", b) for b in reversed(bits_below(n_dp)[1:])]
    in_orders = [zs + xs + ys + core, zs + ys + xs + core, zs[:1] + ys + xs + zs[1:] + core]
    out_order = zs + ys + xs + core
    gate_order, up_order, down_order = zs + ys, zs + ys, zs[:1] + ys + zs[1:]
    token_order = xs + core

    position = own_seq * tok_rows + jnp.arange(tok_rows, dtype=jnp.int32)
    in_slot = position % slot_size
    slot_index = position // slot_size
    slot_ids = jnp.arange(lengths.shape[1], dtype=jnp.int32)
    slot_length = jnp.sum(
        jnp.where(slot_index[:, None] == slot_ids[None, :], lengths[0][None, :], 0), axis=1
    )
    live_mask = (in_slot < slot_length).astype(jnp.float32)[:, None]
    tap_masks = [(in_slot >= 2 - tap_index).astype(jnp.float32)[:, None] for tap_index in range(3)]

    in_rows, in_cols = in_weight.shape[0], in_weight.shape[1] // 3
    out_rows, out_cols = out_weight.shape
    small = jnp.concatenate([mixer_gain[None], feed_gain[None], conv_weight], axis=0)
    small = jnp.pad(small, ((0, SMALL_ROWS - small.shape[0]), (0, out_cols - small.shape[1])))
    out_block = jnp.concatenate([out_weight, small], axis=0)
    before = lax.ppermute(
        tokens[tok_rows - HALO :], "seq", [(i, i + 1) for i in range(n_seq - 1)]
    )
    in_stacks = []
    for piece, order in enumerate(in_orders):
        shard = in_weight[:, piece * in_cols : (piece + 1) * in_cols]
        in_stacks.append(exchange_gather(shard, order))
    out_stacks = exchange_gather(out_block, out_order)

    def in_view(ref, piece, dp, seq):
        return tile_of(ref, seq, in_rows, dp * 3 + piece, in_cols)

    weight_in = assembled(ids, in_stacks, in_orders, (features, 3 * features), in_view)
    out_moves, first = [], 0
    for source, part in enumerate(out_stacks):
        out_moves.append(
            (
                source,
                0,
                first,
                part.shape[0],
                out_order,
                [
                    lambda a, b, at, dp, seq: (
                        a.at[at, pl.ds(0, out_rows)],
                        tile_of(b, seq, out_rows, dp, out_cols),
                    )
                ],
            )
        )
        out_moves.append(
            (
                source,
                1,
                first,
                part.shape[0],
                out_order,
                [
                    lambda a, b, at, dp, seq: (
                        a.at[at, pl.ds(out_rows, SMALL_ROWS)],
                        b.at[dp, seq],
                    )
                ],
            )
        )
        first += part.shape[0]
    weight_out, smalls = move_blocks(
        ids,
        out_stacks,
        [
            jax.ShapeDtypeStruct((features, features), jnp.bfloat16),
            jax.ShapeDtypeStruct((n_dp, n_seq, SMALL_ROWS, out_cols), jnp.bfloat16),
        ],
        out_moves,
        True,
    )
    smalls = smalls[0, :, :5, : mixer_gain.shape[0]].astype(jnp.float32)
    smalls = smalls.transpose(1, 0, 2).reshape(5, features)
    gain_one, gain_two, conv_taps = smalls[0], smalls[1], smalls[2:]

    ratio = n_seq // n_dp
    home = [
        (e * n_seq + s, (s // ratio) * n_seq + e * ratio + s % ratio)
        for e in range(n_dp)
        for s in range(n_seq)
    ]
    down_shard = lax.ppermute(down_weight, ("dp", "seq"), home)
    hidden_units = gate_weight.shape[1]
    gate_rows = gate_weight.shape[0]
    down_rows, down_cols = down_weight.shape
    gate_stacks = exchange_gather(gate_weight, gate_order)
    up_stacks = exchange_gather(up_weight, up_order)
    down_stacks = exchange_gather(down_shard, down_order)

    def gate_view(ref, piece, dp, seq):
        return ref.at[pl.ds(pl.multiple_of(seq * gate_rows, gate_rows), gate_rows)]

    def down_view(ref, piece, dp, seq):
        return tile_of(ref, seq % ratio, down_rows, seq // ratio, down_cols)

    wide = (features, hidden_units)
    weight_gate = assembled(ids, [gate_stacks], [gate_order], wide, gate_view)
    weight_up = assembled(ids, [up_stacks], [up_order], wide, gate_view)
    weight_down = assembled(ids, [down_stacks], [down_order], (hidden_units, features), down_view)

    residual = tokens.astype(jnp.float32)
    extended_rows = jnp.concatenate([before, tokens], axis=0).astype(jnp.float32)
    scale_ext, normed_ext = rms_forward(extended_rows, gain_one)
    normed_ext = normed_ext.astype(jnp.bfloat16)
    scale_one, normed_one = scale_ext[HALO:], normed_ext[HALO:]
    projected = multiply(normed_ext, weight_in)
    mixed_ext = projected[:, :features] * projected[:, 2 * features :]
    b_part = projected[HALO:, :features]
    c_part = projected[HALO:, features : 2 * features]
    x_part = projected[HALO:, 2 * features :]
    extended = mixed_ext[HALO - 2 :].astype(jnp.bfloat16).astype(jnp.float32)
    conv_out = sum(
        (
            tap_masks[tap_index] * conv_taps[tap_index] * extended[tap_index : tap_index + tok_rows]
            for tap_index in range(3)
        )
    )
    gated = (c_part * conv_out).astype(jnp.bfloat16)
    hidden = residual + multiply(gated, weight_out)
    scale_two, normed_mid = rms_forward(hidden, gain_two)
    normed_two = normed_mid.astype(jnp.bfloat16)

    grad_final = (live_mask * cotangent.astype(jnp.float32)).astype(jnp.bfloat16)
    final_all = jnp.concatenate(dp_gather(grad_final, token_order), axis=0)
    normed_all = jnp.concatenate(dp_gather(normed_two, token_order), axis=0)

    def split_rows(v):
        return [v[i * tok_rows : (i + 1) * tok_rows] for i in range(n_dp)]

    gate_val = multiply(normed_all, weight_gate)
    up_val = multiply(normed_all, weight_up)
    sigmoid_gate = jax.nn.sigmoid(gate_val)
    silu_gate = gate_val * sigmoid_gate
    activated = (silu_gate * up_val).astype(jnp.bfloat16)
    feed_out = dp_scatter(split_rows(multiply(activated, weight_down)), token_order)
    output = (live_mask * (hidden + feed_out)).astype(jnp.bfloat16)
    grad_down = outer_sum(activated, final_all).astype(jnp.bfloat16)
    grad_act = against(final_all, weight_down)
    grad_gate = (grad_act * up_val * sigmoid_gate * (1.0 + gate_val * (1.0 - sigmoid_gate))).astype(
        jnp.bfloat16
    )
    grad_up = (grad_act * silu_gate).astype(jnp.bfloat16)
    grad_norm_parts = against(grad_gate, weight_gate) + against(grad_up, weight_up)
    grad_norm_two = dp_scatter(split_rows(grad_norm_parts), token_order)
    grad_gate_w = outer_sum(normed_all, grad_gate).astype(jnp.bfloat16)
    grad_up_w = outer_sum(normed_all, grad_up).astype(jnp.bfloat16)

    def scattered(whole, order, block, view):
        ((keep, send),) = blocks_of(ids, whole, [order], block, view)
        return exchange_scatter(keep, send, order)

    own_down = scattered(grad_down, down_order, down_weight.shape, down_view)
    own_down = lax.ppermute(
        own_down.astype(jnp.bfloat16), ("dp", "seq"), [(b, a) for a, b in home]
    ).astype(jnp.float32)
    own_gate = scattered(grad_gate_w, gate_order, gate_weight.shape, gate_view)
    own_up = scattered(grad_up_w, up_order, up_weight.shape, gate_view)

    grad_from_norm, grad_gain_two = rms_backward(hidden, scale_two, gain_two, grad_norm_two)
    grad_hidden = grad_final.astype(jnp.float32) + grad_from_norm
    grad_branch = grad_hidden.astype(jnp.bfloat16)
    grad_out_w = outer_sum(gated, grad_branch).astype(jnp.bfloat16)

    def out_view(ref, piece, dp, seq):
        return tile_of(ref, seq, out_rows, dp, out_cols)

    own_out = scattered(grad_out_w, out_order, out_weight.shape, out_view)
    grad_gated = against(grad_branch, weight_out)
    grad_conv = grad_gated * c_part
    grad_c = grad_gated * conv_out
    grad_taps = [tap_masks[tap_index] * grad_conv for tap_index in range(3)]
    grad_conv_w = jnp.stack(
        [
            jnp.sum(grad_taps[tap_index] * extended[tap_index : tap_index + tok_rows], axis=0)
            for tap_index in range(3)
        ]
    )
    grad_extended = sum(
        (
            jnp.pad(
                grad_taps[tap_index] * conv_taps[tap_index], ((tap_index, 2 - tap_index), (0, 0))
            )
            for tap_index in range(3)
        )
    )
    returned = lax.ppermute(grad_extended[:2], "seq", [(i + 1, i) for i in range(n_seq - 1)])
    grad_mixed = grad_extended[2:] + jnp.pad(returned, ((tok_rows - 2, 0), (0, 0)))
    grad_proj = jnp.concatenate([grad_mixed * x_part, grad_c, grad_mixed * b_part], axis=1).astype(
        jnp.bfloat16
    )
    grad_in_w = outer_sum(normed_one, grad_proj).astype(jnp.bfloat16)
    in_parts = blocks_of(ids, grad_in_w, in_orders, (in_rows, in_cols), in_view)
    own_in = jnp.concatenate(
        [exchange_scatter(keep, send, order) for (keep, send), order in zip(in_parts, in_orders)],
        axis=1,
    )
    grad_norm_one = against(grad_proj, weight_in)
    grad_from_first, grad_gain_one = rms_backward(residual, scale_one, gain_one, grad_norm_one)
    grad_tokens = (grad_hidden + grad_from_first).astype(jnp.bfloat16)

    sums = jnp.concatenate([grad_gain_one[None], grad_gain_two[None], grad_conv_w], axis=0)
    sums = jnp.pad(sums, ((0, 3), (0, 0)))
    for step in zs + ys + xs + core:
        sums = sums + swap(sums, step)
    columns = mixer_gain.shape[0]
    own_sums = lax.dynamic_slice(sums, (0, own_seq * columns), (8, columns))
    return (
        output,
        grad_tokens,
        own_sums[0],
        own_in,
        own_sums[2:5],
        own_out,
        own_sums[1],
        own_gate,
        own_up,
        own_down,
    )


def solution(mesh):
    in_specs = (
        P(("dp", "seq"), None),
        P("seq"),
        P("seq", "dp"),
        P(None, "seq"),
        P("seq", "dp"),
        P("seq"),
        P("seq", "dp"),
        P("seq", "dp"),
        P("seq", "dp"),
        P("dp", None),
        P(("dp", "seq"), None),
    )
    out_specs = (
        P(("dp", "seq"), None),
        P(("dp", "seq"), None),
        P("seq"),
        P("seq", "dp"),
        P(None, "seq"),
        P("seq", "dp"),
        P("seq"),
        P("seq", "dp"),
        P("seq", "dp"),
        P("seq", "dp"),
    )
    return jax.shard_map(
        per_device, mesh=mesh, in_specs=in_specs, out_specs=out_specs, check_vma=False
    )
```

```python
from typing import NamedTuple

import jax
import jax.numpy as jnp
from jax import lax
from jax.experimental import pallas as pl
from jax.experimental.pallas import tpu as pltpu
from jax.sharding import PartitionSpec as P

SLOT_MAX = 8192
HALO = 16
SMALL_ROWS = 16
VMEM_BYTES = 56 << 20
TILE = 256
KERNEL_COST = pl.CostEstimate(flops=1 << 36, bytes_accessed=1 << 20, transcendentals=0)

norm_eps = 1e-05


def multiply(left_side, right_side):
    return jnp.dot(left_side, right_side, preferred_element_type=jnp.float32)


def against(left_side, right_side):
    return lax.dot_general(
        left_side, right_side, (((1,), (1,)), ((), ())), preferred_element_type=jnp.float32
    )


def outer_sum(left_side, right_side):
    return lax.dot_general(
        left_side, right_side, (((0,), (0,)), ((), ())), preferred_element_type=jnp.float32
    )


def tie(*values):
    return lax.optimization_barrier(values)


def swap(shard, step):
    axis, bit = step
    count = lax.axis_size(axis)
    return lax.ppermute(shard, axis, [(i, i ^ bit) for i in range(count)])


def gather_steps(stack, steps):
    for step in steps:
        stack = jnp.concatenate([stack, swap(stack, step)], axis=0)
    return stack


def last_step(stack, step):
    return [stack, swap(stack, step)]


def scatter_step(parts, step):
    keep, send = parts
    total = keep.astype(jnp.float32) + swap(send, step).astype(jnp.float32)
    half = total.shape[0] // 2
    if not half:
        return total[0]
    return total[:half].astype(jnp.bfloat16), total[half:].astype(jnp.bfloat16)


def scatter_steps(parts, steps):
    for step in reversed(steps):
        parts = scatter_step(parts, step)
    return parts


def masks_at(position, steps):
    masks = {"dp": 0, "seq": 0}
    for place, (axis, bit) in enumerate(steps):
        masks[axis] = masks[axis] + ((position >> place) & 1) * bit
    return masks["dp"], masks["seq"]


def tile_of(ref, row, rows, col, cols):
    return ref.at[pl.ds(pl.multiple_of(row * rows, rows), rows), pl.ds(pl.multiple_of(col * cols, cols), cols)]


def dp_gather(block, steps):
    blocks = [block]
    for step in steps:
        blocks = blocks + [swap(b, step) for b in blocks]
    return blocks


def dp_scatter(parts, steps):
    for step in reversed(steps):
        half = len(parts) // 2
        moved = [swap(send.astype(jnp.bfloat16), step) for send in parts[half:]]
        parts = [
            new if keep is None else keep.astype(jnp.float32) + new.astype(jnp.float32)
            for keep, new in zip(parts[:half], moved)
        ]
    return parts


class Piece(NamedTuple):
    steps: list
    block: tuple
    view: object


def start_loads(ids_ref, refs, pieces, into, sem):
    for place, piece in enumerate(pieces):
        first = 0
        for part in refs[2 * place : 2 * place + 2]:

            def start(position, carry, part=part, first=first, piece=piece):
                mask_dp, mask_seq = masks_at(position + first, piece.steps)
                pltpu.make_async_copy(
                    part.at[position],
                    piece.view(into, ids_ref[0] ^ mask_dp, ids_ref[1] ^ mask_seq),
                    sem,
                ).start()
                return carry

            lax.fori_loop(0, part.shape[0], start, 0)
            first += part.shape[0]


def start_stores(ids_ref, whole, pieces, outs, sem):
    for place, piece in enumerate(pieces):
        half = 2 ** (len(piece.steps) - 1)
        for first, out in ((0, outs[2 * place]), (half, outs[2 * place + 1])):

            def start(position, carry, first=first, out=out, piece=piece):
                mask_dp, mask_seq = masks_at(position + first, piece.steps)
                source = piece.view(whole, ids_ref[0] ^ mask_dp, ids_ref[1] ^ mask_seq)
                pltpu.make_async_copy(source, out.at[position], sem).start()
                return carry

            lax.fori_loop(0, half, start, 0)


def wait_whole(ref, sem):
    pltpu.make_async_copy(ref, ref, sem).wait()


def fetch_block(blocks, buffers, sems):
    i = pl.program_id(0)

    rows = buffers.shape[1]

    def copy(place):
        slot = place % 2
        source = blocks[place // 2].at[pl.ds(place % 2 * rows, rows)]
        return pltpu.make_async_copy(source, buffers.at[slot], sems.at[slot])

    for place in range(2 * len(blocks)):

        @pl.when(i == place)
        def _(place=place):
            if place == 0:
                copy(0).start()
            if place + 1 < 2 * len(blocks):
                copy(place + 1).start()
            copy(place).wait()

    return buffers[i % 2]


def token_call(kernel, ids, blocks, tiled, stacks, outs, scratch):
    rows, width = blocks[0].shape
    rows, count, steps = rows // 2, len(blocks), 2 * len(blocks)
    return pl.pallas_call(
        kernel,
        out_shape=[jax.ShapeDtypeStruct((rows * steps, n), t) for n, t in outs],
        grid_spec=pltpu.PrefetchScalarGridSpec(
            num_scalar_prefetch=1,
            grid=(steps,),
            in_specs=[pl.BlockSpec(memory_space=pl.ANY)] * count
            + [pl.BlockSpec((rows, v.shape[1]), lambda i, ids: (i, 0)) for v in tiled]
            + [pl.BlockSpec(memory_space=pl.ANY)] * len(stacks),
            out_specs=[pl.BlockSpec((rows, n), lambda i, ids: (i, 0)) for n, _ in outs],
            scratch_shapes=[
                pltpu.VMEM((2, rows, width), jnp.bfloat16),
                pltpu.SemaphoreType.DMA((2,)),
                *scratch,
            ],
        ),
        compiler_params=pltpu.CompilerParams(vmem_limit_bytes=VMEM_BYTES),
        cost_estimate=KERNEL_COST,
    )(ids, *blocks, *tiled, *stacks)


def feed_up(ids, normed, gate, gate_stacks, up, up_stacks, shape):
    count = len(normed)

    def kernel(ids_ref, *refs):
        blocks, stacks, refs = refs[:count], refs[count:-8], refs[-8:]
        act, slope, silu, buffers, block_sems, gate_v, up_v, sems = refs

        @pl.when(pl.program_id(0) == 0)
        def _():
            start_loads(ids_ref, stacks[: 2 * len(gate)], gate, gate_v, sems.at[0])
            start_loads(ids_ref, stacks[2 * len(gate) :], up, up_v, sems.at[1])

        x = fetch_block(blocks, buffers, block_sems)

        @pl.when(pl.program_id(0) == 0)
        def _():
            wait_whole(gate_v, sems.at[0])
            wait_whole(up_v, sems.at[1])

        gate_val = multiply(x, gate_v[...])
        up_val = multiply(x, up_v[...])
        sigmoid = jax.nn.sigmoid(gate_val)
        silu_gate = gate_val * sigmoid
        act[...] = (silu_gate * up_val).astype(jnp.bfloat16)
        slope[...] = (up_val * sigmoid * (1.0 + gate_val * (1.0 - sigmoid))).astype(jnp.bfloat16)
        silu[...] = silu_gate.astype(jnp.bfloat16)

    n = shape[1]
    return token_call(
        kernel,
        ids,
        normed,
        [],
        [*gate_stacks, *up_stacks],
        [(n, jnp.bfloat16)] * 3,
        [pltpu.VMEM(shape, jnp.bfloat16)] * 2 + [pltpu.SemaphoreType.DMA((2,))],
    )


def feed_back(ids, final, activated, slope, silu, gate, gate_stacks, up, up_stacks, down, down_stacks, shape):
    count = len(final)
    ends = [2 * len(gate), 2 * len(gate) + 2 * len(up)]

    def kernel(ids_ref, *refs):
        blocks, (act_ref, slope_ref, silu_ref) = refs[:count], refs[count : count + 3]
        stacks, refs = refs[count + 3 : -10], refs[-10:]
        grad_gate, grad_up, grad_norm, out, buffers, block_sems, gate_v, up_v, down_v, sems = refs

        @pl.when(pl.program_id(0) == 0)
        def _():
            start_loads(ids_ref, stacks[ends[1] :], down, down_v, sems.at[2])
            start_loads(ids_ref, stacks[: ends[0]], gate, gate_v, sems.at[0])
            start_loads(ids_ref, stacks[ends[0] : ends[1]], up, up_v, sems.at[1])

        f = fetch_block(blocks, buffers, block_sems)

        @pl.when(pl.program_id(0) == 0)
        def _():
            wait_whole(down_v, sems.at[2])
            wait_whole(gate_v, sems.at[0])
            wait_whole(up_v, sems.at[1])

        grad_act = against(f, down_v[...])
        gg = (grad_act * slope_ref[...].astype(jnp.float32)).astype(jnp.bfloat16)
        gu = (grad_act * silu_ref[...].astype(jnp.float32)).astype(jnp.bfloat16)
        grad_gate[...] = gg
        grad_up[...] = gu
        out[...] = multiply(act_ref[...], down_v[...]).astype(jnp.bfloat16)
        grad_norm[...] = (against(gg, gate_v[...]) + against(gu, up_v[...])).astype(jnp.bfloat16)

    features, n = shape
    return token_call(
        kernel,
        ids,
        final,
        [activated, slope, silu],
        [*gate_stacks, *up_stacks, *down_stacks],
        [(n, jnp.bfloat16), (n, jnp.bfloat16), (features, jnp.bfloat16), (features, jnp.bfloat16)],
        [
            pltpu.VMEM(shape, jnp.bfloat16),
            pltpu.VMEM(shape, jnp.bfloat16),
            pltpu.VMEM((n, features), jnp.bfloat16),
            pltpu.SemaphoreType.DMA((3,)),
        ],
    )


def stack_shapes(pieces):
    shapes = []
    for piece in pieces:
        half = 2 ** (len(piece.steps) - 1)
        shapes += [jax.ShapeDtypeStruct((half, *piece.block), jnp.bfloat16)] * 2
    return shapes


def paired(parts):
    return [(parts[i], parts[i + 1]) for i in range(0, len(parts), 2)]


def weight_gradient(ids, lefts, rights, pieces):
    rows, columns = lefts[0].shape[1], rights[0].shape[1]
    step = min(v.shape[0] for v in (*lefts, *rights))
    tile = next((t for t in (512, 384, 256, 128) if rows % t == 0), rows)
    count = rows // tile
    shapes = stack_shapes(pieces)

    def kernel(ids_ref, *refs):
        sides, refs = refs[: len(lefts) + len(rights)], refs[len(lefts) + len(rights) :]
        outs, (whole, sems) = refs[:-2], refs[-2:]
        i = pl.program_id(0)
        left_rows, right_rows = [
            [v[at : at + step] for v in side for at in range(0, v.shape[0], step)]
            for side in (sides[: len(lefts)], sides[len(lefts) :])
        ]
        total = sum(outer_sum(a, b) for a, b in zip(left_rows, right_rows))
        whole[pl.ds(pl.multiple_of(i * tile, tile), tile)] = total.astype(jnp.bfloat16)

        @pl.when(i == count - 1)
        def _():
            start_stores(ids_ref, whole, pieces, outs, sems.at[0])
            wait_whole(whole, sems.at[0])

    parts = pl.pallas_call(
        kernel,
        out_shape=shapes,
        grid_spec=pltpu.PrefetchScalarGridSpec(
            num_scalar_prefetch=1,
            grid=(count,),
            in_specs=[
                *(pl.BlockSpec((v.shape[0], tile), lambda i, ids: (0, i)) for v in lefts),
                *(pl.BlockSpec((v.shape[0], columns), lambda i, ids: (0, 0)) for v in rights),
            ],
            out_specs=[pl.BlockSpec(memory_space=pl.ANY)] * len(shapes),
            scratch_shapes=[
                pltpu.VMEM((rows, columns), jnp.bfloat16),
                pltpu.SemaphoreType.DMA((1,)),
            ],
        ),
        compiler_params=pltpu.CompilerParams(vmem_limit_bytes=VMEM_BYTES),
        cost_estimate=KERNEL_COST,
    )(ids, *lefts, *rights)
    return paired(parts)


def mixer_forward(ids, extended, consts, in_pieces, in_stacks, out_pieces, out_stacks, slot_size):
    rows, features = extended.shape
    rows = rows - HALO
    tile = rows // 2
    count = len(in_stacks)
    wide = 3 * features

    def kernel(ids_ref, ext_ref, const_ref, *refs):
        stacks, refs = refs[: count + len(out_stacks)], refs[count + len(out_stacks) :]
        normed_one, b_out, c_out, x_out, mixed_out, conv_out, gated_out, hidden_out, normed_two = refs[:9]
        in_v, out_v, mixed_s, sems = refs[9:]
        i = pl.program_id(0)

        @pl.when(i == 0)
        def _():
            start_loads(ids_ref, stacks[:count], in_pieces, in_v, sems.at[0])
            start_loads(ids_ref, stacks[count:], out_pieces, out_v, sems.at[1])

        at = pl.multiple_of(i * tile, HALO)
        x = ext_ref[pl.ds(at, HALO + tile)].astype(jnp.float32)
        scale = lax.rsqrt(jnp.mean(x * x, axis=1, keepdims=True) + norm_eps)
        normed = (x * scale * const_ref[0:1]).astype(jnp.bfloat16)
        normed_one[...] = normed[HALO:]

        @pl.when(i == 0)
        def _():
            wait_whole(in_v, sems.at[0])
            wait_whole(out_v, sems.at[1])

        b_part = multiply(normed, in_v[:, :features])
        x_part = multiply(normed, in_v[:, 2 * features :])
        b_out[...] = b_part[HALO:]
        x_out[...] = x_part[HALO:]
        mixed = (b_part * x_part).astype(jnp.bfloat16)
        mixed_s[...] = mixed.astype(jnp.float32)
        base = lax.rem(ids_ref[1] * rows, slot_size)

        @pl.when(jnp.logical_and(i == 0, base == 0))
        def _():
            mixed_s[0:HALO] = jnp.zeros((HALO, features), jnp.float32)

        mixed_out[pl.ds(at, HALO)] = mixed_s[0:HALO].astype(jnp.bfloat16)
        mixed_out[pl.ds(pl.multiple_of(at + HALO, HALO), tile)] = mixed[HALO:]
        conv = sum(
            const_ref[2 + k : 3 + k] * mixed_s[HALO - 2 + k : HALO - 2 + k + tile] for k in range(3)
        )
        conv_out[...] = conv
        c_part = multiply(normed[HALO:], in_v[:, features : 2 * features])
        c_out[...] = c_part
        gated = (c_part * conv).astype(jnp.bfloat16)
        gated_out[...] = gated
        hidden = x[HALO:] + multiply(gated, out_v[...])
        hidden_out[...] = hidden
        scale = lax.rsqrt(jnp.mean(hidden * hidden, axis=1, keepdims=True) + norm_eps)
        normed_two[...] = (hidden * scale * const_ref[1:2]).astype(jnp.bfloat16)

    f32, bf16 = jnp.float32, jnp.bfloat16
    kinds = [bf16, f32, f32, f32, bf16, f32, bf16, f32, bf16]
    shapes = [(rows + (HALO if i == 4 else 0), features) for i in range(9)]
    whole = pl.BlockSpec((rows + HALO, features), lambda i, ids: (0, 0))
    part = pl.BlockSpec((tile, features), lambda i, ids: (i, 0))
    return pl.pallas_call(
        kernel,
        out_shape=[jax.ShapeDtypeStruct(s, t) for s, t in zip(shapes, kinds)],
        grid_spec=pltpu.PrefetchScalarGridSpec(
            num_scalar_prefetch=1,
            grid=(2,),
            in_specs=[whole, pl.BlockSpec(consts.shape, lambda i, ids: (0, 0))]
            + [pl.BlockSpec(memory_space=pl.ANY)] * (count + len(out_stacks)),
            out_specs=[whole if i == 4 else part for i in range(9)],
            scratch_shapes=[
                pltpu.VMEM((features, wide), bf16),
                pltpu.VMEM((features, features), bf16),
                pltpu.VMEM((tile + HALO, features), f32),
                pltpu.SemaphoreType.DMA((2,)),
            ],
        ),
        compiler_params=pltpu.CompilerParams(vmem_limit_bytes=VMEM_BYTES),
        cost_estimate=KERNEL_COST,
    )(ids, extended, consts, *in_stacks, *out_stacks)


def mixer_back(
    ids, near, more, far, final, hidden, c_part, conv, gated, mixed, consts, out_pieces, out_stacks, slot_size
):
    rows, features = hidden.shape
    tile = rows // 2
    shapes = stack_shapes(out_pieces)

    def kernel(
        ids_ref, near_ref, more_ref, far_ref, final_ref, hidden_ref, c_ref, conv_ref, gated_ref, mixed_ref, const_ref, *refs
    ):
        stacks, refs = refs[: len(out_stacks)], refs[len(out_stacks) :]
        grad_hidden, grad_c, grad_mixed, head, sums = refs[:5]
        outs, (out_v, whole, mixed_s, conv_s, sems) = refs[5:-5], refs[-5:]
        i = pl.program_id(0)

        @pl.when(i == 0)
        def _():
            start_loads(ids_ref, stacks, out_pieces, out_v, sems.at[0])
            sums[...] = jnp.zeros(sums.shape, jnp.float32)
            conv_s[tile:] = jnp.zeros((8, features), jnp.float32)

        @pl.when(i > 0)
        def _():
            conv_s[tile:] = conv_s[0:8]

        normed_grad = near_ref[...].astype(jnp.float32) + more_ref[...].astype(jnp.float32)
        normed_grad += far_ref[...].astype(jnp.float32)
        h = hidden_ref[...]
        scale = lax.rsqrt(jnp.mean(h * h, axis=1, keepdims=True) + norm_eps)
        weighted = normed_grad * const_ref[1:2]
        inner = jnp.mean(weighted * h, axis=1, keepdims=True)
        sums[1:2] += jnp.sum(normed_grad * h * scale, axis=0, keepdims=True)
        total = final_ref[...].astype(jnp.float32) + scale * weighted - h * (scale * scale * scale * inner)
        grad_hidden[...] = total
        branch = total.astype(jnp.bfloat16)
        outer = outer_sum(gated_ref[...], branch)

        @pl.when(i == 0)
        def _():
            wait_whole(out_v, sems.at[0])

        grad_gated = against(branch, out_v[...])
        grad_c[...] = (grad_gated * conv_ref[...]).astype(jnp.bfloat16)
        grad_conv = grad_gated * c_ref[...]
        conv_s[0:tile] = grad_conv
        at = pl.multiple_of((1 - i) * tile, HALO)
        mixed_s[...] = mixed_ref[pl.ds(at, HALO + tile)].astype(jnp.float32)
        for k in range(3):
            sums[2 + k : 3 + k] += jnp.sum(
                grad_conv * mixed_s[HALO - 2 + k : HALO - 2 + k + tile], axis=0, keepdims=True
            )
        grad_mixed[...] = sum(const_ref[2 + k : 3 + k] * conv_s[2 - k : 2 - k + tile] for k in range(3))

        @pl.when(i == 1)
        def _():
            live = jnp.where(lax.rem(ids_ref[1] * rows, slot_size) > 0, 1.0, 0.0)
            head[...] = jnp.zeros(head.shape, jnp.float32)
            head[0:1] = live * const_ref[2:3] * conv_s[0:1]
            head[1:2] = live * (const_ref[2:3] * conv_s[1:2] + const_ref[3:4] * conv_s[0:1])
            out_v[...] = (whole[...] + outer).astype(jnp.bfloat16)
            start_stores(ids_ref, out_v, out_pieces, outs, sems.at[0])
            wait_whole(out_v, sems.at[0])

        @pl.when(i == 0)
        def _():
            whole[...] = outer

    f32, bf16 = jnp.float32, jnp.bfloat16
    part = pl.BlockSpec((tile, features), lambda i, ids: (1 - i, 0))
    once = pl.BlockSpec((8, features), lambda i, ids: (0, 0))
    parts = pl.pallas_call(
        kernel,
        out_shape=[jax.ShapeDtypeStruct((rows, features), t) for t in (f32, bf16, f32)]
        + [jax.ShapeDtypeStruct((8, features), f32)] * 2
        + shapes,
        grid_spec=pltpu.PrefetchScalarGridSpec(
            num_scalar_prefetch=1,
            grid=(2,),
            in_specs=[part] * 8
            + [pl.BlockSpec((rows + HALO, features), lambda i, ids: (0, 0)), once]
            + [pl.BlockSpec(memory_space=pl.ANY)] * len(out_stacks),
            out_specs=[part] * 3 + [once] * 2 + [pl.BlockSpec(memory_space=pl.ANY)] * len(shapes),
            scratch_shapes=[
                pltpu.VMEM((features, features), bf16),
                pltpu.VMEM((features, features), f32),
                pltpu.VMEM((tile + HALO, features), f32),
                pltpu.VMEM((tile + 8, features), f32),
                pltpu.SemaphoreType.DMA((1,)),
            ],
        ),
        compiler_params=pltpu.CompilerParams(vmem_limit_bytes=VMEM_BYTES),
        cost_estimate=KERNEL_COST,
    )(ids, near, more, far, final, hidden, c_part, conv, gated, mixed, consts, *out_stacks)
    return [*parts[:5], paired(parts[5:])]


def projection_gradient(ids, normed, grad_mixed, returned, grad_c, b_part, x_part, pieces):
    rows, features = normed.shape
    tile = features // 4
    shapes = stack_shapes(pieces)

    def kernel(ids_ref, normed_ref, mixed_ref, back_ref, c_ref, b_ref, x_ref, proj, *refs):
        outs, (whole, mixed_s, sems) = refs[:-3], refs[-3:]
        i = pl.program_id(0)

        @pl.when(i == 0)
        def _():
            mixed_s[...] = mixed_ref[...]
            mixed_s[rows - 2 :] += back_ref[0:2]
            grad = mixed_s[...]
            proj[:, :features] = (grad * x_ref[...]).astype(jnp.bfloat16)
            proj[:, features : 2 * features] = c_ref[...]
            proj[:, 2 * features :] = (grad * b_ref[...]).astype(jnp.bfloat16)

        whole[pl.ds(pl.multiple_of(i * tile, tile), tile)] = outer_sum(
            normed_ref[...], proj[...]
        ).astype(jnp.bfloat16)

        @pl.when(i == 3)
        def _():
            start_stores(ids_ref, whole, pieces, outs, sems.at[0])
            wait_whole(whole, sems.at[0])

    def same(n, width):
        return pl.BlockSpec((n, width), lambda i, ids: (0, 0))

    parts = pl.pallas_call(
        kernel,
        out_shape=[jax.ShapeDtypeStruct((rows, 3 * features), jnp.bfloat16), *shapes],
        grid_spec=pltpu.PrefetchScalarGridSpec(
            num_scalar_prefetch=1,
            grid=(4,),
            in_specs=[
                pl.BlockSpec((rows, tile), lambda i, ids: (0, i)),
                same(rows, features),
                same(8, features),
                same(rows, features),
                same(rows, features),
                same(rows, features),
            ],
            out_specs=[same(rows, 3 * features)] + [pl.BlockSpec(memory_space=pl.ANY)] * len(shapes),
            scratch_shapes=[
                pltpu.VMEM((features, 3 * features), jnp.bfloat16),
                pltpu.VMEM((rows, features), jnp.float32),
                pltpu.SemaphoreType.DMA((1,)),
            ],
        ),
        compiler_params=pltpu.CompilerParams(vmem_limit_bytes=VMEM_BYTES),
        cost_estimate=KERNEL_COST,
    )(ids, normed, grad_mixed, returned, grad_c, b_part, x_part)
    return parts[0], paired(parts[1:])


def mixer_first(ids, proj, tokens, grad_hidden, sums, consts, in_pieces, in_stacks):
    rows, features = tokens.shape
    tile = rows // 2

    def kernel(ids_ref, proj_ref, x_ref, hidden_ref, sums_ref, const_ref, *refs):
        stacks, (grad_tokens, sums_out, in_v, sems) = refs[:-4], refs[-4:]

        @pl.when(pl.program_id(0) == 0)
        def _():
            start_loads(ids_ref, stacks, in_pieces, in_v, sems.at[0])
            sums_out[...] = sums_ref[...]
            wait_whole(in_v, sems.at[0])

        normed_grad = against(proj_ref[...], in_v[...])
        x = x_ref[...].astype(jnp.float32)
        scale = lax.rsqrt(jnp.mean(x * x, axis=1, keepdims=True) + norm_eps)
        weighted = normed_grad * const_ref[0:1]
        inner = jnp.mean(weighted * x, axis=1, keepdims=True)
        sums_out[0:1] += jnp.sum(normed_grad * x * scale, axis=0, keepdims=True)
        grad_tokens[...] = (
            hidden_ref[...] + scale * weighted - x * (scale * scale * scale * inner)
        ).astype(jnp.bfloat16)

    part = pl.BlockSpec((tile, features), lambda i, ids: (i, 0))
    once = pl.BlockSpec((8, features), lambda i, ids: (0, 0))
    return pl.pallas_call(
        kernel,
        out_shape=[
            jax.ShapeDtypeStruct((rows, features), jnp.bfloat16),
            jax.ShapeDtypeStruct((8, features), jnp.float32),
        ],
        grid_spec=pltpu.PrefetchScalarGridSpec(
            num_scalar_prefetch=1,
            grid=(2,),
            in_specs=[pl.BlockSpec((tile, 3 * features), lambda i, ids: (i, 0)), part, part, once, once]
            + [pl.BlockSpec(memory_space=pl.ANY)] * len(in_stacks),
            out_specs=[part, once],
            scratch_shapes=[
                pltpu.VMEM((features, 3 * features), jnp.bfloat16),
                pltpu.SemaphoreType.DMA((1,)),
            ],
        ),
        compiler_params=pltpu.CompilerParams(vmem_limit_bytes=VMEM_BYTES),
        cost_estimate=KERNEL_COST,
    )(ids, proj, tokens, grad_hidden, sums, consts, *in_stacks)


def bits_below(count):
    return [1 << i for i in range(count.bit_length() - 1)]


def per_device(
    tokens,
    mixer_gain,
    in_weight,
    conv_weight,
    out_weight,
    feed_gain,
    gate_weight,
    up_weight,
    down_weight,
    lengths,
    cotangent,
):
    n_dp, n_seq = lax.axis_size("dp"), lax.axis_size("seq")
    tok_rows, features = tokens.shape
    slot_size = min(SLOT_MAX, tok_rows * n_seq)
    own_dp, own_seq = lax.axis_index("dp"), lax.axis_index("seq")
    ids = jnp.stack([own_dp, own_seq]).astype(jnp.int32)

    seq_bits = bits_below(n_seq)
    along_y = seq_bits[: len(seq_bits) // 2]
    ys = [("seq", b) for b in reversed(along_y)]
    zs = [("seq", b) for b in reversed(seq_bits[len(along_y) :])]
    core = [("dp", 1)]
    xs = [("dp", b) for b in reversed(bits_below(n_dp)[1:])]
    in_orders = [zs + xs + ys + core, ys + zs + xs + core]
    out_order = zs[:1] + xs + ys + zs[1:] + core
    far_order, near_order = zs[:1] + ys + zs[1:], zs + ys
    token_order = xs + core

    position = own_seq * tok_rows + jnp.arange(tok_rows, dtype=jnp.int32)
    in_slot = position % slot_size
    slot_index = position // slot_size
    slot_ids = jnp.arange(lengths.shape[1], dtype=jnp.int32)
    slot_length = jnp.sum(
        jnp.where(slot_index[:, None] == slot_ids[None, :], lengths[0][None, :], 0), axis=1
    )
    live_mask = (in_slot < slot_length).astype(jnp.float32)[:, None]

    in_rows, in_cols = in_weight.shape
    out_rows, out_cols = out_weight.shape
    in_cut = (in_cols // 128 + 1) // 2 * 128
    in_cuts = [0, in_cut, in_cols]
    small_cols = mixer_gain.shape[0]
    small = jnp.concatenate([mixer_gain[None], feed_gain[None], conv_weight], axis=0)
    small = jnp.pad(small, ((0, SMALL_ROWS - small.shape[0]), (0, -small_cols % 128)))
    small_order = zs + ys
    small = gather_steps(small[None], small_order)
    places = jnp.stack([jnp.int32(masks_at(p, small_order)[1]) for p in range(n_seq)])
    chosen = (own_seq ^ jnp.arange(n_seq))[:, None] == places[None]
    consts = jnp.einsum(
        "sp,pkc->ksc",
        chosen.astype(jnp.bfloat16),
        small[:, :8, :small_cols],
        preferred_element_type=jnp.float32,
    ).reshape(8, features)
    mixer = [in_weight[None, :, :in_cut], in_weight[None, :, in_cut:], out_weight[None]]
    orders = [*in_orders, out_order]
    before = lax.ppermute(
        tokens[tok_rows - HALO :], "seq", [(i, i + 1) for i in range(n_seq - 1)]
    )
    extended = jnp.concatenate([before, tokens], axis=0)
    hidden_units = gate_weight.shape[1]
    gate_rows = gate_weight.shape[0]
    down_rows, down_cols = down_weight.shape
    ratio = n_seq // n_dp
    home = [
        (e * n_seq + s, (s // ratio) * n_seq + e * ratio + s % ratio)
        for e in range(n_dp)
        for s in range(n_seq)
    ]
    cuts = [0, -(-down_rows // 32) * 16, down_rows]

    def gate_view(ref, dp, seq):
        return ref.at[pl.ds(pl.multiple_of(seq * gate_rows, gate_rows), gate_rows)]

    def down_view(cut):
        low, high = cuts[cut], cuts[cut + 1]

        def view(ref, dp, seq):
            row = pl.multiple_of((seq % ratio) * down_rows + low, 16)
            col = pl.multiple_of((seq // ratio) * down_cols, down_cols)
            return ref.at[pl.ds(row, high - low), pl.ds(col, down_cols)]

        return view

    gate = [Piece(near_order, gate_weight.shape, gate_view)]
    up = [Piece(far_order, up_weight.shape, gate_view)]
    down = [
        Piece(order, (cuts[i + 1] - cuts[i], down_cols), down_view(i))
        for i, order in enumerate((near_order, far_order))
    ]

    grad_final = (live_mask * cotangent.astype(jnp.float32)).astype(jnp.bfloat16)
    middle = len(orders[0]) // 2
    z_first, last = len(zs) // 2, len(zs) + len(ys) - 1
    mixer = [gather_steps(v, order[:middle]) for v, order in zip(mixer, orders)]
    mixer, gate_weight, up_weight = tie(mixer, gate_weight, up_weight)
    mixer = [gather_steps(v, order[middle:-1]) for v, order in zip(mixer, orders)]
    gate_up = [
        gather_steps(v[None], p.steps[:z_first])
        for v, p in zip((gate_weight, up_weight), (*gate, *up))
    ]
    mixer, gate_up, consts, extended, down_weight, grad_final = tie(
        mixer, gate_up, consts, extended, down_weight, grad_final
    )
    stacks = [last_step(v, order[-1]) for v, order in zip(mixer, orders)]
    stacks, gate_up, down_weight, grad_final = tie(stacks, gate_up, down_weight, grad_final)

    def in_view(cut):
        low, high = in_cuts[cut], in_cuts[cut + 1]

        def view(ref, dp, seq):
            row = pl.multiple_of(seq * in_rows, in_rows)
            col = pl.multiple_of(dp * in_cols + low, 128)
            return ref.at[pl.ds(row, in_rows), pl.ds(col, high - low)]

        return view

    def out_view(ref, dp, seq):
        return tile_of(ref, seq, out_rows, dp, out_cols)

    in_pieces = [
        Piece(order, (in_rows, in_cuts[i + 1] - in_cuts[i]), in_view(i))
        for i, order in enumerate(in_orders)
    ]
    out_pieces = [Piece(out_order, out_weight.shape, out_view)]
    in_stacks, out_stacks = stacks[0] + stacks[1], stacks[2]

    gate_up = [gather_steps(v, p.steps[z_first:last]) for v, p in zip(gate_up, (*gate, *up))]
    down_shard = lax.ppermute(down_weight, ("dp", "seq"), home)
    forward = mixer_forward(
        ids, extended, consts, in_pieces, in_stacks, out_pieces, out_stacks, slot_size
    )
    forward, gate_up, down_shard, grad_final = tie(forward, gate_up, down_shard, grad_final)
    normed_one, b_part, c_part, x_part, mixed, conv, gated, hidden, normed_two = forward

    def split_rows(v):
        return [v[i : i + tok_rows] for i in range(0, v.shape[0], tok_rows)]

    def with_core(blocks):
        return blocks + [swap(v, core[0]) for v in blocks]

    wide = (features, hidden_units)
    gate_stacks, up_stacks = [last_step(v, p.steps[-1]) for v, p in zip(gate_up, (*gate, *up))]
    downs = [
        gather_steps(down_shard[None, a:b], p.steps[:z_first])
        for a, b, p in zip(cuts, cuts[1:], down)
    ]
    normed_there = dp_gather(normed_two, xs)[1:]
    normed_two, normed_there, gate_stacks, up_stacks, downs, grad_final = tie(
        normed_two, normed_there, gate_stacks, up_stacks, downs, grad_final
    )
    normed_blocks = with_core([normed_two]) + with_core(normed_there)
    downs = [gather_steps(v, p.steps[z_first:last]) for v, p in zip(downs, down)]
    normed_blocks, downs, gate_stacks, up_stacks, grad_final = tie(
        normed_blocks, downs, gate_stacks, up_stacks, grad_final
    )
    down_stacks = [v for stack, p in zip(downs, down) for v in last_step(stack, p.steps[-1])]
    final_there = dp_gather(grad_final, xs)[1:]
    activated, slope, silu = feed_up(ids, normed_blocks, gate, gate_stacks, up, up_stacks, wide)
    activated, down_stacks, grad_final, final_there = tie(
        activated, down_stacks, grad_final, final_there
    )
    final_blocks = with_core([grad_final]) + with_core(final_there)
    down_parts = weight_gradient(ids, [activated], final_blocks, down)
    down_parts, down_stacks = tie(down_parts, down_stacks)

    def lower(parts):
        return tuple(v[: v.shape[0] // 2] for v in parts)

    def upper(parts):
        return tuple(v[v.shape[0] // 2 :] for v in parts)

    def one_step(parts, pieces, place):
        return [scatter_step(v, p.steps[place]) for v, p in zip(parts, pieces)]

    def exchanged(parts, step):
        return (parts[0], swap(parts[1], step))

    def added(low, high):
        return tuple(
            (v[0].astype(jnp.float32) + v[1].astype(jnp.float32)).astype(jnp.bfloat16)
            for v in (low, high)
        )

    def core_halves(v):
        blocks = split_rows(v)
        near, far = blocks[:2], blocks[2:]
        half = len(far) // 2
        return near[0], near[1], far[:half], far[half:]

    down_parts = one_step(down_parts, down, -1)
    grad_gate, grad_up, back, feed = feed_back(
        ids, final_blocks, activated, slope, silu, gate, gate_stacks, up, up_stacks, down, down_stacks, wide
    )
    back, feed, grad_gate, grad_up, down_parts = tie(back, feed, grad_gate, grad_up, down_parts)
    near, near_send, far, far_send = core_halves(back)
    far = dp_scatter(far + far_send, core)
    far, near, near_send, grad_gate, grad_up, feed = tie(far, near, near_send, grad_gate, grad_up, feed)
    far = [v.astype(jnp.bfloat16) for v in far]
    half_rows = tok_rows // 2
    far_low = dp_scatter([None] + [v[:half_rows] for v in far], xs)
    near_more = swap(near_send, core[0])
    feed_near, feed_send, feed_far, feed_far_send = core_halves(feed)
    down_parts = one_step(down_parts, down, -2)
    gate_parts = weight_gradient(ids, normed_blocks, [grad_gate], gate)
    gate_parts, far, far_low, grad_up, near, near_more, down_parts, feed_far, feed_far_send = tie(
        gate_parts, far, far_low, grad_up, near, near_more, down_parts, feed_far, feed_far_send
    )
    far_high = dp_scatter([None] + [v[half_rows:] for v in far], xs)
    gate_low = exchanged(lower(gate_parts[0]), gate[0].steps[-1])
    feed_far = [v.astype(jnp.bfloat16) for v in dp_scatter(feed_far + feed_far_send, core)]
    up_parts = weight_gradient(ids, normed_blocks, [grad_up], up)
    up_parts, far_low, far_high, gate_low, gate_parts, feed_far, down_parts = tie(
        up_parts, far_low, far_high, gate_low, gate_parts, feed_far, down_parts
    )

    gate_high = exchanged(upper(gate_parts[0]), gate[0].steps[-1])
    up_low = exchanged(lower(up_parts[0]), up[0].steps[-1])
    feed_low = dp_scatter([None] + [v[:half_rows] for v in feed_far], xs)
    far = jnp.concatenate(far_low + far_high, axis=0)
    grad_hidden, grad_c, grad_mixed, first_rows, sums, out_parts = mixer_back(
        ids,
        near,
        near_more,
        far,
        grad_final,
        hidden,
        c_part,
        conv,
        gated,
        mixed,
        consts,
        out_pieces,
        out_stacks,
        slot_size,
    )
    out_parts, grad_mixed, first_rows, gate_low, gate_high, up_low, up_parts, feed_far, feed_low = tie(
        out_parts, grad_mixed, first_rows, gate_low, gate_high, up_low, up_parts, feed_far, feed_low
    )
    returned = lax.ppermute(first_rows, "seq", [(i + 1, i) for i in range(n_seq - 1)])
    up_high = exchanged(upper(up_parts[0]), up[0].steps[-1])
    feed_high = dp_scatter([None] + [v[half_rows:] for v in feed_far], xs)
    own_down = [scatter_steps(v, p.steps[:-2]) for v, p in zip(down_parts, down)]
    own_down = jnp.concatenate(own_down, axis=0).astype(jnp.bfloat16)
    grad_proj, in_parts = projection_gradient(
        ids, normed_one, grad_mixed, returned, grad_c, b_part, x_part, in_pieces
    )
    in_parts, up_low, up_high, own_down, gate_low, gate_high, grad_proj, out_parts, feed_high = tie(
        in_parts, up_low, up_high, own_down, gate_low, gate_high, grad_proj, out_parts, feed_high
    )
    in_parts = one_step(in_parts, in_pieces, -1)
    out_parts = one_step(out_parts, out_pieces, -1)
    in_parts, out_parts, grad_proj, gate_low, gate_high, up_low, up_high = tie(
        in_parts, out_parts, grad_proj, gate_low, gate_high, up_low, up_high
    )
    in_parts = one_step(in_parts, in_pieces, -2)
    out_parts = one_step(out_parts, out_pieces, -2)
    gate_parts = scatter_step(added(gate_low, gate_high), gate[0].steps[-2])
    up_parts = added(up_low, up_high)
    grad_tokens, sums = mixer_first(ids, grad_proj, tokens, grad_hidden, sums, consts, in_pieces, in_stacks)
    in_parts, sums, out_parts, gate_parts, up_parts, own_down = tie(
        in_parts, sums, out_parts, gate_parts, up_parts, own_down
    )
    in_parts = one_step(in_parts, in_pieces, -3)
    out_parts = one_step(out_parts, out_pieces, -3)
    own_gate = scatter_steps(gate_parts, gate[0].steps[:-2])
    up_parts = scatter_step(up_parts, up[0].steps[-2])
    sum_steps = zs + ys + xs + core
    for step in sum_steps[:2]:
        sums = sums + swap(sums, step)
    in_parts, out_parts, own_gate, up_parts, sums, own_down = tie(
        in_parts, out_parts, own_gate, up_parts, sums, own_down
    )
    own_in = [scatter_step(v, p.steps[-4]) for v, p in zip(in_parts, in_pieces)]
    own_up = scatter_steps(up_parts, up[0].steps[:-2])
    out_parts = one_step(out_parts, out_pieces, -4)
    for step in sum_steps[2:4]:
        sums = sums + swap(sums, step)
    own_in, out_parts, own_up, sums, own_down = tie(own_in, out_parts, own_up, sums, own_down)
    own_in = [scatter_steps(v, p.steps[:-4]) for v, p in zip(own_in, in_pieces)]
    own_in = jnp.concatenate(own_in, axis=1)
    own_out = scatter_steps(out_parts[0], out_order[:-4])
    for step in sum_steps[4:]:
        sums = sums + swap(sums, step)
    own_down = lax.ppermute(own_down, ("dp", "seq"), [(b, a) for a, b in home]).astype(jnp.float32)
    own_sums = lax.dynamic_slice(sums, (0, own_seq * small_cols), (8, small_cols))
    feed_more = swap(feed_send, core[0])
    feed_out = jnp.concatenate(feed_low + feed_high, axis=0).astype(jnp.float32)
    feed_out = feed_out + feed_near.astype(jnp.float32) + feed_more.astype(jnp.float32)
    output = (live_mask * (hidden + feed_out)).astype(jnp.bfloat16)
    return (
        output,
        grad_tokens,
        own_sums[0],
        own_in,
        own_sums[2:5],
        own_out,
        own_sums[1],
        own_gate,
        own_up,
        own_down,
    )


def solution(mesh):
    in_specs = (
        P(("dp", "seq"), None),
        P("seq"),
        P("seq", "dp"),
        P(None, "seq"),
        P("seq", "dp"),
        P("seq"),
        P("seq", "dp"),
        P("seq", "dp"),
        P("seq", "dp"),
        P("dp", None),
        P(("dp", "seq"), None),
    )
    out_specs = (
        P(("dp", "seq"), None),
        P(("dp", "seq"), None),
        P("seq"),
        P("seq", "dp"),
        P(None, "seq"),
        P("seq", "dp"),
        P("seq"),
        P("seq", "dp"),
        P("seq", "dp"),
        P("seq", "dp"),
    )
    return jax.shard_map(
        per_device, mesh=mesh, in_specs=in_specs, out_specs=out_specs, check_vma=False
    )
```

```python
from typing import NamedTuple

import jax
import jax.numpy as jnp
from jax import lax
from jax.experimental import pallas as pl
from jax.experimental.pallas import tpu as pltpu
from jax.sharding import PartitionSpec as P

SLOT_MAX = 8192
HALO = 16
SMALL_ROWS = 16
VMEM_BYTES = 56 << 20
TILE = 256
KERNEL_COST = pl.CostEstimate(flops=1 << 36, bytes_accessed=1 << 20, transcendentals=0)

norm_eps = 1e-05


def multiply(left_side, right_side):
    return jnp.dot(left_side, right_side, preferred_element_type=jnp.float32)


def against(left_side, right_side):
    return lax.dot_general(
        left_side, right_side, (((1,), (1,)), ((), ())), preferred_element_type=jnp.float32
    )


def outer_sum(left_side, right_side):
    return lax.dot_general(
        left_side, right_side, (((0,), (0,)), ((), ())), preferred_element_type=jnp.float32
    )


def tie(*values):
    return lax.optimization_barrier(values)


def swap(shard, step):
    axis, bit = step
    count = lax.axis_size(axis)
    return lax.ppermute(shard, axis, [(i, i ^ bit) for i in range(count)])


def gather_steps(stack, steps):
    for step in steps:
        stack = jnp.concatenate([stack, swap(stack, step)], axis=0)
    return stack


def last_step(stack, step):
    return [stack, swap(stack, step)]


def exchanged(parts, step):
    keep, send = parts
    return keep, swap(send, step)


def folded(parts):
    keep, come = parts
    total = keep.astype(jnp.float32) + come.astype(jnp.float32)
    half = total.shape[0] // 2
    if not half:
        return total[0]
    return total[:half].astype(jnp.bfloat16), total[half:].astype(jnp.bfloat16)


def masks_at(position, steps):
    masks = {"dp": 0, "seq": 0}
    for place, (axis, bit) in enumerate(steps):
        masks[axis] = masks[axis] + ((position >> place) & 1) * bit
    return masks["dp"], masks["seq"]


def tile_of(ref, row, rows, col, cols):
    return ref.at[pl.ds(pl.multiple_of(row * rows, rows), rows), pl.ds(pl.multiple_of(col * cols, cols), cols)]


def dp_gather(block, steps):
    blocks = [block]
    for step in steps:
        blocks = blocks + [swap(b, step) for b in blocks]
    return blocks


def dp_scatter(parts, steps):
    for step in reversed(steps):
        half = len(parts) // 2
        moved = [swap(send.astype(jnp.bfloat16), step) for send in parts[half:]]
        parts = [
            new if keep is None else keep.astype(jnp.float32) + new.astype(jnp.float32)
            for keep, new in zip(parts[:half], moved)
        ]
    return parts


class Piece(NamedTuple):
    steps: list
    block: tuple
    view: object


def start_loads(ids_ref, refs, pieces, into, sem):
    for place, piece in enumerate(pieces):
        first = 0
        for part in refs[2 * place : 2 * place + 2]:

            def start(position, carry, part=part, first=first, piece=piece):
                mask_dp, mask_seq = masks_at(position + first, piece.steps)
                pltpu.make_async_copy(
                    part.at[position],
                    piece.view(into, ids_ref[0] ^ mask_dp, ids_ref[1] ^ mask_seq),
                    sem,
                ).start()
                return carry

            lax.fori_loop(0, part.shape[0], start, 0)
            first += part.shape[0]


def start_stores(ids_ref, whole, pieces, outs, sem):
    for place, piece in enumerate(pieces):
        half = 2 ** (len(piece.steps) - 1)
        for first, out in ((0, outs[2 * place]), (half, outs[2 * place + 1])):

            def start(position, carry, first=first, out=out, piece=piece):
                mask_dp, mask_seq = masks_at(position + first, piece.steps)
                source = piece.view(whole, ids_ref[0] ^ mask_dp, ids_ref[1] ^ mask_seq)
                pltpu.make_async_copy(source, out.at[position], sem).start()
                return carry

            lax.fori_loop(0, half, start, 0)


def wait_whole(ref, sem):
    pltpu.make_async_copy(ref, ref, sem).wait()


def fetch_block(blocks, buffers, sems):
    i = pl.program_id(0)

    rows = buffers.shape[1]

    def copy(place):
        slot = place % 2
        source = blocks[place // 2].at[pl.ds(place % 2 * rows, rows)]
        return pltpu.make_async_copy(source, buffers.at[slot], sems.at[slot])

    for place in range(2 * len(blocks)):

        @pl.when(i == place)
        def _(place=place):
            if place == 0:
                copy(0).start()
            if place + 1 < 2 * len(blocks):
                copy(place + 1).start()
            copy(place).wait()

    return buffers[i % 2]


def token_call(kernel, ids, blocks, tiled, stacks, outs, apart, scratch):
    rows, width = blocks[0].shape
    rows, count, steps = rows // 2, len(blocks), 2 * len(blocks)
    return pl.pallas_call(
        kernel,
        out_shape=[jax.ShapeDtypeStruct((rows * steps, n), t) for n, t in outs]
        + [jax.ShapeDtypeStruct((rows * 2, n), t) for n, t in apart for _ in range(count)],
        grid_spec=pltpu.PrefetchScalarGridSpec(
            num_scalar_prefetch=1,
            grid=(steps,),
            in_specs=[pl.BlockSpec(memory_space=pl.ANY)] * count
            + [pl.BlockSpec((rows, v.shape[1]), lambda i, ids: (i, 0)) for v in tiled]
            + [pl.BlockSpec(memory_space=pl.ANY)] * len(stacks),
            out_specs=[pl.BlockSpec((rows, n), lambda i, ids: (i, 0)) for n, _ in outs]
            + [
                pl.BlockSpec((rows, n), lambda i, ids, b=b: (jnp.clip(i - 2 * b, 0, 1), 0))
                for n, _ in apart
                for b in range(count)
            ],
            scratch_shapes=[
                pltpu.VMEM((2, rows, width), jnp.bfloat16),
                pltpu.SemaphoreType.DMA((2,)),
                *scratch,
            ],
        ),
        compiler_params=pltpu.CompilerParams(vmem_limit_bytes=VMEM_BYTES),
        cost_estimate=KERNEL_COST,
    )(ids, *blocks, *tiled, *stacks)


def feed_up(ids, normed, gate, gate_stacks, up, up_stacks, shape):
    count = len(normed)

    def kernel(ids_ref, *refs):
        blocks, stacks, refs = refs[:count], refs[count:-8], refs[-8:]
        act, slope, silu, buffers, block_sems, gate_v, up_v, sems = refs

        @pl.when(pl.program_id(0) == 0)
        def _():
            start_loads(ids_ref, stacks[: 2 * len(gate)], gate, gate_v, sems.at[0])
            start_loads(ids_ref, stacks[2 * len(gate) :], up, up_v, sems.at[1])

        x = fetch_block(blocks, buffers, block_sems)

        @pl.when(pl.program_id(0) == 0)
        def _():
            wait_whole(gate_v, sems.at[0])
            wait_whole(up_v, sems.at[1])

        gate_val = multiply(x, gate_v[...])
        up_val = multiply(x, up_v[...])
        sigmoid = jax.nn.sigmoid(gate_val)
        silu_gate = gate_val * sigmoid
        act[...] = (silu_gate * up_val).astype(jnp.bfloat16)
        slope[...] = (up_val * sigmoid * (1.0 + gate_val * (1.0 - sigmoid))).astype(jnp.bfloat16)
        silu[...] = silu_gate.astype(jnp.bfloat16)

    n = shape[1]
    return token_call(
        kernel,
        ids,
        normed,
        [],
        [*gate_stacks, *up_stacks],
        [(n, jnp.bfloat16)] * 3,
        [],
        [pltpu.VMEM(shape, jnp.bfloat16)] * 2 + [pltpu.SemaphoreType.DMA((2,))],
    )


def feed_back(ids, final, activated, slope, silu, gate, gate_stacks, up, up_stacks, down, down_stacks, shape):
    count = len(final)
    ends = [2 * len(gate), 2 * len(gate) + 2 * len(up)]

    def kernel(ids_ref, *refs):
        blocks, (act_ref, slope_ref, silu_ref) = refs[:count], refs[count : count + 3]
        parts = 2 * count
        stacks, refs = refs[count + 3 : -8 - parts], refs[-8 - parts :]
        grad_gate, grad_up, buffers, block_sems, gate_v, up_v, down_v, sems = refs[:2] + refs[2 + parts :]
        norm_parts, out_parts = refs[2 : 2 + count], refs[2 + count : 2 + parts]

        @pl.when(pl.program_id(0) == 0)
        def _():
            start_loads(ids_ref, stacks[ends[1] :], down, down_v, sems.at[2])
            start_loads(ids_ref, stacks[: ends[0]], gate, gate_v, sems.at[0])
            start_loads(ids_ref, stacks[ends[0] : ends[1]], up, up_v, sems.at[1])

        f = fetch_block(blocks, buffers, block_sems)

        @pl.when(pl.program_id(0) == 0)
        def _():
            wait_whole(down_v, sems.at[2])
            wait_whole(gate_v, sems.at[0])
            wait_whole(up_v, sems.at[1])

        grad_act = against(f, down_v[...])
        gg = (grad_act * slope_ref[...].astype(jnp.float32)).astype(jnp.bfloat16)
        gu = (grad_act * silu_ref[...].astype(jnp.float32)).astype(jnp.bfloat16)
        grad_gate[...] = gg
        grad_up[...] = gu
        out = multiply(act_ref[...], down_v[...]).astype(jnp.bfloat16)
        grad_norm = (against(gg, gate_v[...]) + against(gu, up_v[...])).astype(jnp.bfloat16)
        for place in range(count):

            @pl.when(pl.program_id(0) // 2 == place)
            def _(place=place):
                norm_parts[place][...] = grad_norm
                out_parts[place][...] = out

    features, n = shape
    return token_call(
        kernel,
        ids,
        final,
        [activated, slope, silu],
        [*gate_stacks, *up_stacks, *down_stacks],
        [(n, jnp.bfloat16)] * 2,
        [(features, jnp.bfloat16)] * 2,
        [
            pltpu.VMEM(shape, jnp.bfloat16),
            pltpu.VMEM(shape, jnp.bfloat16),
            pltpu.VMEM((n, features), jnp.bfloat16),
            pltpu.SemaphoreType.DMA((3,)),
        ],
    )


def stack_shapes(pieces):
    shapes = []
    for piece in pieces:
        half = 2 ** (len(piece.steps) - 1)
        shapes += [jax.ShapeDtypeStruct((half, *piece.block), jnp.bfloat16)] * 2
    return shapes


def paired(parts):
    return [(parts[i], parts[i + 1]) for i in range(0, len(parts), 2)]


def weight_gradient(ids, lefts, rights, pieces):
    rows, columns = lefts[0].shape[1], rights[0].shape[1]
    step = min(v.shape[0] for v in (*lefts, *rights))
    tile = next((t for t in (512, 384, 256, 128) if rows % t == 0), rows)
    count = rows // tile
    shapes = stack_shapes(pieces)

    def kernel(ids_ref, *refs):
        sides, refs = refs[: len(lefts) + len(rights)], refs[len(lefts) + len(rights) :]
        outs, (whole, sems) = refs[:-2], refs[-2:]
        i = pl.program_id(0)
        left_rows, right_rows = [
            [v[at : at + step] for v in side for at in range(0, v.shape[0], step)]
            for side in (sides[: len(lefts)], sides[len(lefts) :])
        ]
        total = sum(outer_sum(a, b) for a, b in zip(left_rows, right_rows))
        whole[pl.ds(pl.multiple_of(i * tile, tile), tile)] = total.astype(jnp.bfloat16)

        @pl.when(i == count - 1)
        def _():
            start_stores(ids_ref, whole, pieces, outs, sems.at[0])
            wait_whole(whole, sems.at[0])

    parts = pl.pallas_call(
        kernel,
        out_shape=shapes,
        grid_spec=pltpu.PrefetchScalarGridSpec(
            num_scalar_prefetch=1,
            grid=(count,),
            in_specs=[
                *(pl.BlockSpec((v.shape[0], tile), lambda i, ids: (0, i)) for v in lefts),
                *(pl.BlockSpec((v.shape[0], columns), lambda i, ids: (0, 0)) for v in rights),
            ],
            out_specs=[pl.BlockSpec(memory_space=pl.ANY)] * len(shapes),
            scratch_shapes=[
                pltpu.VMEM((rows, columns), jnp.bfloat16),
                pltpu.SemaphoreType.DMA((1,)),
            ],
        ),
        compiler_params=pltpu.CompilerParams(vmem_limit_bytes=VMEM_BYTES),
        cost_estimate=KERNEL_COST,
    )(ids, *lefts, *rights)
    return paired(parts)


def mixer_forward(ids, extended, consts, in_pieces, in_stacks, out_pieces, out_stacks, slot_size):
    rows, features = extended.shape
    rows = rows - HALO
    tile = rows // 2
    count = len(in_stacks)
    wide = 3 * features

    def kernel(ids_ref, ext_ref, const_ref, *refs):
        stacks, refs = refs[: count + len(out_stacks)], refs[count + len(out_stacks) :]
        normed_one, b_out, c_out, x_out, mixed_out, conv_out, gated_out, hidden_out, normed_two = refs[:9]
        in_v, out_v, mixed_s, sems = refs[9:]
        i = pl.program_id(0)

        @pl.when(i == 0)
        def _():
            start_loads(ids_ref, stacks[:count], in_pieces, in_v, sems.at[0])
            start_loads(ids_ref, stacks[count:], out_pieces, out_v, sems.at[1])

        at = pl.multiple_of(i * tile, HALO)
        x = ext_ref[pl.ds(at, HALO + tile)].astype(jnp.float32)
        scale = lax.rsqrt(jnp.mean(x * x, axis=1, keepdims=True) + norm_eps)
        normed = (x * scale * const_ref[0:1]).astype(jnp.bfloat16)
        normed_one[...] = normed[HALO:]

        @pl.when(i == 0)
        def _():
            wait_whole(in_v, sems.at[0])
            wait_whole(out_v, sems.at[1])

        b_part = multiply(normed, in_v[:, :features])
        x_part = multiply(normed, in_v[:, 2 * features :])
        b_out[...] = b_part[HALO:]
        x_out[...] = x_part[HALO:]
        mixed = (b_part * x_part).astype(jnp.bfloat16)
        mixed_s[...] = mixed.astype(jnp.float32)
        base = lax.rem(ids_ref[1] * rows, slot_size)

        @pl.when(jnp.logical_and(i == 0, base == 0))
        def _():
            mixed_s[0:HALO] = jnp.zeros((HALO, features), jnp.float32)

        mixed_out[pl.ds(at, HALO)] = mixed_s[0:HALO].astype(jnp.bfloat16)
        mixed_out[pl.ds(pl.multiple_of(at + HALO, HALO), tile)] = mixed[HALO:]
        conv = sum(
            const_ref[2 + k : 3 + k] * mixed_s[HALO - 2 + k : HALO - 2 + k + tile] for k in range(3)
        )
        conv_out[...] = conv
        c_part = multiply(normed[HALO:], in_v[:, features : 2 * features])
        c_out[...] = c_part
        gated = (c_part * conv).astype(jnp.bfloat16)
        gated_out[...] = gated
        hidden = x[HALO:] + multiply(gated, out_v[...])
        hidden_out[...] = hidden
        scale = lax.rsqrt(jnp.mean(hidden * hidden, axis=1, keepdims=True) + norm_eps)
        normed_two[...] = (hidden * scale * const_ref[1:2]).astype(jnp.bfloat16)

    f32, bf16 = jnp.float32, jnp.bfloat16
    kinds = [bf16, f32, f32, f32, bf16, f32, bf16, f32, bf16]
    shapes = [(rows + (HALO if i == 4 else 0), features) for i in range(9)]
    whole = pl.BlockSpec((rows + HALO, features), lambda i, ids: (0, 0))
    part = pl.BlockSpec((tile, features), lambda i, ids: (i, 0))
    return pl.pallas_call(
        kernel,
        out_shape=[jax.ShapeDtypeStruct(s, t) for s, t in zip(shapes, kinds)],
        grid_spec=pltpu.PrefetchScalarGridSpec(
            num_scalar_prefetch=1,
            grid=(2,),
            in_specs=[whole, pl.BlockSpec(consts.shape, lambda i, ids: (0, 0))]
            + [pl.BlockSpec(memory_space=pl.ANY)] * (count + len(out_stacks)),
            out_specs=[whole if i == 4 else part for i in range(9)],
            scratch_shapes=[
                pltpu.VMEM((features, wide), bf16),
                pltpu.VMEM((features, features), bf16),
                pltpu.VMEM((tile + HALO, features), f32),
                pltpu.SemaphoreType.DMA((2,)),
            ],
        ),
        compiler_params=pltpu.CompilerParams(vmem_limit_bytes=VMEM_BYTES),
        cost_estimate=KERNEL_COST,
    )(ids, extended, consts, *in_stacks, *out_stacks)


def mixer_back(ids, tiled, far, mixed, consts, out_pieces, out_stacks, out_grads, slot_size):
    rows, features = tiled[0].shape
    tile = rows // 2
    shapes = stack_shapes(out_grads)

    def kernel(ids_ref, *refs):
        near_ref, more_ref, final_ref, hidden_ref, c_ref, conv_ref, gated_ref = refs[:7]
        low_ref, high_ref, mixed_ref, const_ref = refs[7:11]
        refs = refs[11:]
        stacks, refs = refs[: len(out_stacks)], refs[len(out_stacks) :]
        grad_hidden, grad_c, grad_mixed, head, sums = refs[:5]
        outs, (out_v, whole, mixed_s, conv_s, sems) = refs[5:-5], refs[-5:]
        i = pl.program_id(0)

        @pl.when(i == 0)
        def _():
            start_loads(ids_ref, stacks, out_pieces, out_v, sems.at[0])
            sums[...] = jnp.zeros(sums.shape, jnp.float32)
            conv_s[tile:] = jnp.zeros((8, features), jnp.float32)

        @pl.when(i > 0)
        def _():
            conv_s[tile:] = conv_s[0:8]

        normed_grad = near_ref[...].astype(jnp.float32) + more_ref[...].astype(jnp.float32)
        normed_grad += jnp.where(i == 0, high_ref[...].astype(jnp.float32), low_ref[...].astype(jnp.float32))
        h = hidden_ref[...]
        scale = lax.rsqrt(jnp.mean(h * h, axis=1, keepdims=True) + norm_eps)
        weighted = normed_grad * const_ref[1:2]
        inner = jnp.mean(weighted * h, axis=1, keepdims=True)
        sums[1:2] += jnp.sum(normed_grad * h * scale, axis=0, keepdims=True)
        total = final_ref[...].astype(jnp.float32) + scale * weighted - h * (scale * scale * scale * inner)
        grad_hidden[...] = total
        branch = total.astype(jnp.bfloat16)
        outer = outer_sum(gated_ref[...], branch)

        @pl.when(i == 0)
        def _():
            wait_whole(out_v, sems.at[0])

        grad_gated = against(branch, out_v[...])
        grad_c[...] = (grad_gated * conv_ref[...]).astype(jnp.bfloat16)
        grad_conv = grad_gated * c_ref[...]
        conv_s[0:tile] = grad_conv
        at = pl.multiple_of((1 - i) * tile, HALO)
        mixed_s[...] = mixed_ref[pl.ds(at, HALO + tile)].astype(jnp.float32)
        for k in range(3):
            sums[2 + k : 3 + k] += jnp.sum(
                grad_conv * mixed_s[HALO - 2 + k : HALO - 2 + k + tile], axis=0, keepdims=True
            )
        grad_mixed[...] = sum(const_ref[2 + k : 3 + k] * conv_s[2 - k : 2 - k + tile] for k in range(3))

        @pl.when(i == 1)
        def _():
            live = jnp.where(lax.rem(ids_ref[1] * rows, slot_size) > 0, 1.0, 0.0)
            head[...] = jnp.zeros(head.shape, jnp.float32)
            head[0:1] = live * const_ref[2:3] * conv_s[0:1]
            head[1:2] = live * (const_ref[2:3] * conv_s[1:2] + const_ref[3:4] * conv_s[0:1])
            out_v[...] = (whole[...] + outer).astype(jnp.bfloat16)
            start_stores(ids_ref, out_v, out_grads, outs, sems.at[0])
            wait_whole(out_v, sems.at[0])

        @pl.when(i == 0)
        def _():
            whole[...] = outer

    f32, bf16 = jnp.float32, jnp.bfloat16
    part = pl.BlockSpec((tile, features), lambda i, ids: (1 - i, 0))
    once = pl.BlockSpec((8, features), lambda i, ids: (0, 0))
    parts = pl.pallas_call(
        kernel,
        out_shape=[jax.ShapeDtypeStruct((rows, features), t) for t in (f32, bf16, f32)]
        + [jax.ShapeDtypeStruct((8, features), f32)] * 2
        + shapes,
        grid_spec=pltpu.PrefetchScalarGridSpec(
            num_scalar_prefetch=1,
            grid=(2,),
            in_specs=[part] * 7
            + [pl.BlockSpec((tile, features), lambda i, ids: (0, 0))] * 2
            + [pl.BlockSpec((rows + HALO, features), lambda i, ids: (0, 0)), once]
            + [pl.BlockSpec(memory_space=pl.ANY)] * len(out_stacks),
            out_specs=[part] * 3 + [once] * 2 + [pl.BlockSpec(memory_space=pl.ANY)] * len(shapes),
            scratch_shapes=[
                pltpu.VMEM((features, features), bf16),
                pltpu.VMEM((features, features), f32),
                pltpu.VMEM((tile + HALO, features), f32),
                pltpu.VMEM((tile + 8, features), f32),
                pltpu.SemaphoreType.DMA((1,)),
            ],
        ),
        compiler_params=pltpu.CompilerParams(vmem_limit_bytes=VMEM_BYTES),
        cost_estimate=KERNEL_COST,
    )(ids, *tiled, *far, mixed, consts, *out_stacks)
    return [*parts[:5], paired(parts[5:])]


def projection_gradient(ids, normed, grad_mixed, returned, grad_c, b_part, x_part, pieces):
    rows, features = normed.shape
    tile = features // 4
    shapes = stack_shapes(pieces)

    def kernel(ids_ref, normed_ref, mixed_ref, back_ref, c_ref, b_ref, x_ref, proj, *refs):
        outs, (whole, mixed_s, sems) = refs[:-3], refs[-3:]
        i = pl.program_id(0)

        @pl.when(i == 0)
        def _():
            mixed_s[...] = mixed_ref[...]
            mixed_s[rows - 2 :] += back_ref[0:2]
            grad = mixed_s[...]
            proj[:, :features] = (grad * x_ref[...]).astype(jnp.bfloat16)
            proj[:, features : 2 * features] = c_ref[...]
            proj[:, 2 * features :] = (grad * b_ref[...]).astype(jnp.bfloat16)

        whole[pl.ds(pl.multiple_of(i * tile, tile), tile)] = outer_sum(
            normed_ref[...], proj[...]
        ).astype(jnp.bfloat16)

        @pl.when(i == 3)
        def _():
            start_stores(ids_ref, whole, pieces, outs, sems.at[0])
            wait_whole(whole, sems.at[0])

    def same(n, width):
        return pl.BlockSpec((n, width), lambda i, ids: (0, 0))

    parts = pl.pallas_call(
        kernel,
        out_shape=[jax.ShapeDtypeStruct((rows, 3 * features), jnp.bfloat16), *shapes],
        grid_spec=pltpu.PrefetchScalarGridSpec(
            num_scalar_prefetch=1,
            grid=(4,),
            in_specs=[
                pl.BlockSpec((rows, tile), lambda i, ids: (0, i)),
                same(rows, features),
                same(8, features),
                same(rows, features),
                same(rows, features),
                same(rows, features),
            ],
            out_specs=[same(rows, 3 * features)] + [pl.BlockSpec(memory_space=pl.ANY)] * len(shapes),
            scratch_shapes=[
                pltpu.VMEM((features, 3 * features), jnp.bfloat16),
                pltpu.VMEM((rows, features), jnp.float32),
                pltpu.SemaphoreType.DMA((1,)),
            ],
        ),
        compiler_params=pltpu.CompilerParams(vmem_limit_bytes=VMEM_BYTES),
        cost_estimate=KERNEL_COST,
    )(ids, normed, grad_mixed, returned, grad_c, b_part, x_part)
    return parts[0], paired(parts[1:])


def mixer_first(ids, proj, tokens, grad_hidden, sums, consts, in_pieces, in_stacks):
    rows, features = tokens.shape
    tile = rows // 2

    def kernel(ids_ref, proj_ref, x_ref, hidden_ref, sums_ref, const_ref, *refs):
        stacks, (grad_tokens, sums_out, in_v, sems) = refs[:-4], refs[-4:]

        @pl.when(pl.program_id(0) == 0)
        def _():
            start_loads(ids_ref, stacks, in_pieces, in_v, sems.at[0])
            sums_out[...] = sums_ref[...]
            wait_whole(in_v, sems.at[0])

        normed_grad = against(proj_ref[...], in_v[...])
        x = x_ref[...].astype(jnp.float32)
        scale = lax.rsqrt(jnp.mean(x * x, axis=1, keepdims=True) + norm_eps)
        weighted = normed_grad * const_ref[0:1]
        inner = jnp.mean(weighted * x, axis=1, keepdims=True)
        sums_out[0:1] += jnp.sum(normed_grad * x * scale, axis=0, keepdims=True)
        grad_tokens[...] = (
            hidden_ref[...] + scale * weighted - x * (scale * scale * scale * inner)
        ).astype(jnp.bfloat16)

    part = pl.BlockSpec((tile, features), lambda i, ids: (i, 0))
    once = pl.BlockSpec((8, features), lambda i, ids: (0, 0))
    return pl.pallas_call(
        kernel,
        out_shape=[
            jax.ShapeDtypeStruct((rows, features), jnp.bfloat16),
            jax.ShapeDtypeStruct((8, features), jnp.float32),
        ],
        grid_spec=pltpu.PrefetchScalarGridSpec(
            num_scalar_prefetch=1,
            grid=(2,),
            in_specs=[pl.BlockSpec((tile, 3 * features), lambda i, ids: (i, 0)), part, part, once, once]
            + [pl.BlockSpec(memory_space=pl.ANY)] * len(in_stacks),
            out_specs=[part, once],
            scratch_shapes=[
                pltpu.VMEM((features, 3 * features), jnp.bfloat16),
                pltpu.SemaphoreType.DMA((1,)),
            ],
        ),
        compiler_params=pltpu.CompilerParams(vmem_limit_bytes=VMEM_BYTES),
        cost_estimate=KERNEL_COST,
    )(ids, proj, tokens, grad_hidden, sums, consts, *in_stacks)


def bits_below(count):
    return [1 << i for i in range(count.bit_length() - 1)]


def per_device(
    tokens,
    mixer_gain,
    in_weight,
    conv_weight,
    out_weight,
    feed_gain,
    gate_weight,
    up_weight,
    down_weight,
    lengths,
    cotangent,
):
    n_dp, n_seq = lax.axis_size("dp"), lax.axis_size("seq")
    tok_rows, features = tokens.shape
    slot_size = min(SLOT_MAX, tok_rows * n_seq)
    own_dp, own_seq = lax.axis_index("dp"), lax.axis_index("seq")
    ids = jnp.stack([own_dp, own_seq]).astype(jnp.int32)

    seq_bits = bits_below(n_seq)
    along_y = seq_bits[: len(seq_bits) // 2]
    ys = [("seq", b) for b in reversed(along_y)]
    zs = [("seq", b) for b in reversed(seq_bits[len(along_y) :])]
    core = [("dp", 1)]
    xs = [("dp", b) for b in reversed(bits_below(n_dp)[1:])]
    in_orders = [zs + xs + ys + core, ys + zs + xs + core]
    out_order = zs[:1] + xs + ys + zs[1:] + core
    far_order, near_order = zs[:1] + ys + zs[1:], zs + ys
    token_order = xs + core

    position = own_seq * tok_rows + jnp.arange(tok_rows, dtype=jnp.int32)
    in_slot = position % slot_size
    slot_index = position // slot_size
    slot_ids = jnp.arange(lengths.shape[1], dtype=jnp.int32)
    slot_length = jnp.sum(
        jnp.where(slot_index[:, None] == slot_ids[None, :], lengths[0][None, :], 0), axis=1
    )
    live_mask = (in_slot < slot_length).astype(jnp.float32)[:, None]

    in_rows, in_cols = in_weight.shape
    out_rows, out_cols = out_weight.shape
    in_cut = (in_cols // 128 + 1) // 2 * 128
    in_cuts = [0, in_cut, in_cols]
    third = in_cols // 3
    small_cols = mixer_gain.shape[0]
    small = jnp.concatenate([mixer_gain[None], feed_gain[None], conv_weight], axis=0)
    small = jnp.pad(small, ((0, SMALL_ROWS - small.shape[0]), (0, -small_cols % 128)))
    small_order = zs + ys
    mixer = [in_weight[None, :, :in_cut], in_weight[None, :, in_cut:], out_weight[None]]
    orders = [*in_orders, out_order]
    hidden_units = gate_weight.shape[1]
    gate_rows = gate_weight.shape[0]
    down_rows, down_cols = down_weight.shape
    ratio = n_seq // n_dp
    turned = [(e % 2) * (n_dp // 2) + e // 2 for e in range(n_dp)]
    home = [
        (e * n_seq + s, (s // ratio) * n_seq + turned[e] * ratio + s % ratio)
        for e in range(n_dp)
        for s in range(n_seq)
    ]
    cuts = [0, -(-down_rows // 32) * 16, down_rows]

    def gate_view(ref, dp, seq):
        return ref.at[pl.ds(pl.multiple_of(seq * gate_rows, gate_rows), gate_rows)]

    def down_view(cut):
        low, high = cuts[cut], cuts[cut + 1]

        def view(ref, dp, seq):
            row = pl.multiple_of((seq % ratio) * down_rows + low, 16)
            place = seq // ratio
            place = place % (n_dp // 2) * 2 + place // (n_dp // 2)
            col = pl.multiple_of(place * down_cols, down_cols)
            return ref.at[pl.ds(row, high - low), pl.ds(col, down_cols)]

        return view

    gate = [Piece(near_order, gate_weight.shape, gate_view)]
    up = [Piece(far_order, up_weight.shape, gate_view)]
    down = [
        Piece(order, (cuts[i + 1] - cuts[i], down_cols), down_view(i))
        for i, order in enumerate((near_order, far_order))
    ]

    def with_core(blocks):
        return blocks + [swap(v, core[0]) for v in blocks]

    grad_final = (live_mask * cotangent.astype(jnp.float32)).astype(jnp.bfloat16)
    middle = len(orders[0]) // 2
    z_first, last = len(zs) // 2, len(zs) + len(ys) - 1
    mixer = [gather_steps(v, order[:1]) for v, order in zip(mixer, orders)]
    mixer, small, tokens = tie(mixer, small, tokens)
    mixer = [gather_steps(v, order[1:middle]) for v, order in zip(mixer, orders)]
    before = lax.ppermute(
        tokens[tok_rows - HALO :], "seq", [(i, i + 1) for i in range(n_seq - 1)]
    )
    small = gather_steps(small[None], small_order)
    mixer, gate_weight, up_weight = tie(mixer, gate_weight, up_weight)
    mixer = [gather_steps(v, order[middle:-1]) for v, order in zip(mixer, orders)]
    gate_up = [
        gather_steps(v[None], p.steps[:z_first])
        for v, p in zip((gate_weight, up_weight), (*gate, *up))
    ]
    extended = jnp.concatenate([before, tokens], axis=0)
    places = jnp.stack([jnp.int32(masks_at(p, small_order)[1]) for p in range(n_seq)])
    chosen = (own_seq ^ jnp.arange(n_seq))[:, None] == places[None]
    consts = jnp.einsum(
        "sp,pkc->ksc",
        chosen.astype(jnp.bfloat16),
        small[:, :8, :small_cols],
        preferred_element_type=jnp.float32,
    ).reshape(8, features)
    mixer, gate_up, consts, extended, down_weight, grad_final = tie(
        mixer, gate_up, consts, extended, down_weight, grad_final
    )
    stacks = [last_step(v, order[-1]) for v, order in zip(mixer, orders)]
    stacks, gate_up, down_weight, grad_final = tie(stacks, gate_up, down_weight, grad_final)

    def in_view(low, high):

        def view(ref, dp, seq):
            row = pl.multiple_of(seq * in_rows, in_rows)
            col = pl.multiple_of(dp * in_cols + low, 128)
            return ref.at[pl.ds(row, in_rows), pl.ds(col, high - low)]

        return view

    def out_view(ref, dp, seq):
        return tile_of(ref, seq, out_rows, dp, out_cols)

    in_pieces = [
        Piece(order, (in_rows, in_cuts[i + 1] - in_cuts[i]), in_view(in_cuts[i], in_cuts[i + 1]))
        for i, order in enumerate(in_orders)
    ]
    in_grads = [
        Piece(order, (in_rows, third), in_view(i * third, (i + 1) * third))
        for i, order in enumerate(orders)
    ]
    out_grads = [Piece(zs + xs + ys + core, out_weight.shape, out_view)]
    out_pieces = [Piece(out_order, out_weight.shape, out_view)]
    in_stacks, out_stacks = stacks[0] + stacks[1], stacks[2]

    gate_up = [gather_steps(v, p.steps[z_first:last]) for v, p in zip(gate_up, (*gate, *up))]
    down_shard = lax.ppermute(down_weight, ("dp", "seq"), home)
    forward = mixer_forward(
        ids, extended, consts, in_pieces, in_stacks, out_pieces, out_stacks, slot_size
    )
    forward, gate_up, down_shard, grad_final = tie(forward, gate_up, down_shard, grad_final)
    normed_one, b_part, c_part, x_part, mixed, conv, gated, hidden, normed_two = forward

    wide = (features, hidden_units)
    gate_stacks, up_stacks = [last_step(v, p.steps[-1]) for v, p in zip(gate_up, (*gate, *up))]
    downs = [
        gather_steps(down_shard[None, a:b], p.steps[:z_first])
        for a, b, p in zip(cuts, cuts[1:], down)
    ]
    normed_there = dp_gather(normed_two, xs)[1:]
    normed_two, normed_there, gate_stacks, up_stacks, downs, grad_final = tie(
        normed_two, normed_there, gate_stacks, up_stacks, downs, grad_final
    )
    normed_blocks = with_core([normed_two]) + with_core(normed_there)
    normed_blocks, downs, gate_stacks, up_stacks, grad_final = tie(
        normed_blocks, downs, gate_stacks, up_stacks, grad_final
    )
    final_there = dp_gather(grad_final, xs)[1:]
    final_near = swap(grad_final, core[0])
    downs = [gather_steps(v, p.steps[z_first:last]) for v, p in zip(downs, down)]
    activated, slope, silu = feed_up(ids, normed_blocks, gate, gate_stacks, up, up_stacks, wide)
    activated, downs, grad_final, final_near, final_there = tie(
        activated, downs, grad_final, final_near, final_there
    )
    final_blocks = [grad_final, final_near] + with_core(final_there)
    down_stacks = [v for stack, p in zip(downs, down) for v in last_step(stack, p.steps[-1])]
    down_parts = weight_gradient(ids, [activated], final_blocks, down)
    down_parts, down_stacks = tie(down_parts, down_stacks)

    def lower(parts):
        return tuple(v[: v.shape[0] // 2] for v in parts)

    def upper(parts):
        return tuple(v[v.shape[0] // 2 :] for v in parts)

    def sent(parts, pieces, place):
        return [exchanged(v, p.steps[place]) for v, p in zip(parts, pieces)]

    def fold_all(parts):
        return [folded(v) for v in parts]

    def added(low, high):
        return tuple(
            (v[0].astype(jnp.float32) + v[1].astype(jnp.float32)).astype(jnp.bfloat16)
            for v in (low, high)
        )

    def core_halves(v):
        near, far = v[:2], v[2:]
        half = len(far) // 2
        return near[0], near[1], far[:half], far[half:]

    def far_added(keep, come):
        return [
            (a.astype(jnp.float32) + b.astype(jnp.float32)).astype(jnp.bfloat16)
            for a, b in zip(keep, come)
        ]

    down_parts = sent(down_parts, down, -1)
    grad_gate, grad_up, *back = feed_back(
        ids, final_blocks, activated, slope, silu, gate, gate_stacks, up, up_stacks, down, down_stacks, wide
    )
    back, feed = back[:n_dp], back[n_dp:]
    back, feed, grad_gate, grad_up, down_parts = tie(back, feed, grad_gate, grad_up, down_parts)
    near, near_send, far, far_send = core_halves(back)
    far_come = [swap(v, core[0]) for v in far_send]
    far, far_come, near, near_send, grad_gate, grad_up, feed, down_parts = tie(
        far, far_come, near, near_send, grad_gate, grad_up, feed, down_parts
    )
    far = far_added(far, far_come)
    half_rows = tok_rows // 2
    far_low, far_high = [v[:half_rows] for v in far], [v[half_rows:] for v in far]
    down_parts = fold_all(down_parts)
    far_low, far_high, down_parts, near, near_send, grad_gate, grad_up, feed = tie(
        far_low, far_high, down_parts, near, near_send, grad_gate, grad_up, feed
    )
    far_low = dp_scatter([None] + far_low, xs)
    near_more = swap(near_send, core[0])
    down_parts = sent(down_parts, down, -2)
    gate_parts = weight_gradient(ids, normed_blocks, [grad_gate], gate)
    gate_parts, far_low, far_high, grad_up, near, near_more, down_parts, feed = tie(
        gate_parts, far_low, far_high, grad_up, near, near_more, down_parts, feed
    )
    down_parts = fold_all(down_parts)
    gate_low, gate_high = lower(gate_parts[0]), upper(gate_parts[0])
    feed_near, feed_send, feed_far, feed_come = core_halves(feed)
    down_parts, gate_low, gate_high, feed_far, feed_come, grad_up, far_low, far_high = tie(
        down_parts, gate_low, gate_high, feed_far, feed_come, grad_up, far_low, far_high
    )
    far_high = dp_scatter([None] + far_high, xs)
    gate_low = exchanged(gate_low, gate[0].steps[-1])
    feed_come = [swap(v, core[0]) for v in feed_come]
    down_parts = sent(down_parts, down, -3)
    up_parts = weight_gradient(ids, normed_blocks, [grad_up], up)
    up_parts, far_low, far_high, gate_low, gate_high, feed_far, feed_come, down_parts = tie(
        up_parts, far_low, far_high, gate_low, gate_high, feed_far, feed_come, down_parts
    )

    feed_far = far_added(feed_far, feed_come)
    feed_low, feed_high = [v[:half_rows] for v in feed_far], [v[half_rows:] for v in feed_far]
    up_low, up_high = lower(up_parts[0]), upper(up_parts[0])
    own_down = fold_all(down_parts)
    for place in range(len(down[0].steps) - 4, -1, -1):
        own_down = fold_all(sent(own_down, down, place))
    own_down = jnp.concatenate(own_down, axis=0).astype(jnp.bfloat16)
    feed_low, feed_high, up_low, up_high, gate_low, gate_high, far_low, far_high, own_down = tie(
        feed_low, feed_high, up_low, up_high, gate_low, gate_high, far_low, far_high, own_down
    )
    gate_high = exchanged(gate_high, gate[0].steps[-1])
    up_low = exchanged(up_low, up[0].steps[-1])
    feed_low = dp_scatter([None] + feed_low, xs)
    own_down = lax.ppermute(own_down, ("dp", "seq"), [(b, a) for a, b in home])
    grad_hidden, grad_c, grad_mixed, first_rows, sums, out_parts = mixer_back(
        ids,
        [near, near_more, grad_final, hidden, c_part, conv, gated],
        far_low + far_high,
        mixed,
        consts,
        out_pieces,
        out_stacks,
        out_grads,
        slot_size,
    )
    out_parts, grad_mixed, first_rows, gate_low, gate_high, up_low, up_high, feed_low, feed_high, own_down = tie(
        out_parts, grad_mixed, first_rows, gate_low, gate_high, up_low, up_high, feed_low, feed_high, own_down
    )
    returned = lax.ppermute(first_rows, "seq", [(i + 1, i) for i in range(n_seq - 1)])
    out_parts = fold_all(sent(out_parts, out_grads, -1))
    gate_parts = added(gate_low, gate_high)
    returned, out_parts, up_high, gate_parts, feed_high = tie(
        returned, out_parts, up_high, gate_parts, feed_high
    )
    up_high = exchanged(up_high, up[0].steps[-1])
    out_parts = sent(out_parts, out_grads, -2)
    feed_high = dp_scatter([None] + feed_high, xs)
    grad_proj, in_parts = projection_gradient(
        ids, normed_one, grad_mixed, returned, grad_c, b_part, x_part, in_grads
    )
    in_parts, up_low, up_high, gate_parts, grad_proj, out_parts, feed_high = tie(
        in_parts, up_low, up_high, gate_parts, grad_proj, out_parts, feed_high
    )
    up_parts, out_parts = added(up_low, up_high), fold_all(out_parts)
    in_parts, up_parts, gate_parts, out_parts, grad_proj = tie(
        in_parts, up_parts, gate_parts, out_parts, grad_proj
    )
    in_parts = sent(in_parts, in_grads, -1)
    out_parts = sent(out_parts, out_grads, -3)
    gate_parts = exchanged(gate_parts, gate[0].steps[-2])
    up_parts = exchanged(up_parts, up[0].steps[-2])
    grad_tokens, sums = mixer_first(ids, grad_proj, tokens, grad_hidden, sums, consts, in_pieces, in_stacks)
    in_parts, out_parts, sums, gate_parts, up_parts, feed_send = tie(
        in_parts, out_parts, sums, gate_parts, up_parts, feed_send
    )
    sum_steps = core + ys + xs + zs[::-1]
    for step in sum_steps[:1]:
        sums = sums + swap(sums, step)
    in_parts, out_parts, gate_parts, up_parts = fold_all(in_parts), fold_all(out_parts), folded(gate_parts), folded(up_parts)
    in_parts, out_parts, gate_parts, up_parts, sums = tie(in_parts, out_parts, gate_parts, up_parts, sums)
    in_parts = sent(in_parts, in_grads, -2)
    out_parts = sent(out_parts, out_grads, -4)
    gate_parts = exchanged(gate_parts, gate[0].steps[-3])
    sums = (sums, swap(sums, sum_steps[1]))
    in_parts, out_parts, gate_parts, up_parts, sums, feed_send = tie(
        in_parts, out_parts, gate_parts, up_parts, sums, feed_send
    )
    in_parts, out_parts, sums = fold_all(in_parts), fold_all(out_parts), sums[0] + sums[1]
    in_parts, out_parts, up_parts, sums = tie(in_parts, out_parts, up_parts, sums)
    in_parts = sent(in_parts, in_grads, -3)
    out_parts = sent(out_parts, out_grads, -5)
    up_parts = exchanged(up_parts, up[0].steps[-3])
    sums = (sums, swap(sums, sum_steps[2]))
    in_parts, out_parts, up_parts, sums, feed_send = tie(in_parts, out_parts, up_parts, sums, feed_send)
    in_parts, sums = fold_all(in_parts), sums[0] + sums[1]
    in_parts, sums = tie(in_parts, sums)
    in_parts = sent(in_parts, in_grads, -4)
    sums = (sums, swap(sums, sum_steps[3]))
    feed_more = swap(feed_send, core[0])
    in_parts, sums, feed_more = tie(in_parts, sums, feed_more)
    sums = sums[0] + sums[1]
    for step in sum_steps[4:]:
        sums = sums + swap(sums, step)
    own_down = own_down.astype(jnp.float32)

    def rest(parts, piece, done):
        parts = folded(parts)
        for place in range(len(piece.steps) - done - 1, -1, -1):
            parts = folded(exchanged(parts, piece.steps[place]))
        return parts

    own_in = [rest(v, p, 4) for v, p in zip(in_parts, in_grads)]
    own_in = jnp.concatenate(own_in, axis=1)
    own_out = rest(out_parts[0], out_grads[0], 5)
    own_gate = rest(gate_parts, gate[0], 3)
    own_up = rest(up_parts, up[0], 3)
    own_sums = lax.dynamic_slice(sums, (0, own_seq * small_cols), (8, small_cols))
    feed_out = jnp.concatenate(feed_low + feed_high, axis=0).astype(jnp.float32)
    feed_out = feed_out + feed_near.astype(jnp.float32) + feed_more.astype(jnp.float32)
    output = (live_mask * (hidden + feed_out)).astype(jnp.bfloat16)
    return (
        output,
        grad_tokens,
        own_sums[0],
        own_in,
        own_sums[2:5],
        own_out,
        own_sums[1],
        own_gate,
        own_up,
        own_down,
    )


def solution(mesh):
    in_specs = (
        P(("dp", "seq"), None),
        P("seq"),
        P("seq", "dp"),
        P(None, "seq"),
        P("seq", "dp"),
        P("seq"),
        P("seq", "dp"),
        P("seq", "dp"),
        P("seq", "dp"),
        P("dp", None),
        P(("dp", "seq"), None),
    )
    out_specs = (
        P(("dp", "seq"), None),
        P(("dp", "seq"), None),
        P("seq"),
        P("seq", "dp"),
        P(None, "seq"),
        P("seq", "dp"),
        P("seq"),
        P("seq", "dp"),
        P("seq", "dp"),
        P("seq", "dp"),
    )
    return jax.shard_map(
        per_device, mesh=mesh, in_specs=in_specs, out_specs=out_specs, check_vma=False
    )
```

```python
from typing import NamedTuple

import jax
import jax.numpy as jnp
from jax import lax
from jax.experimental import pallas as pl
from jax.experimental.pallas import tpu as pltpu
from jax.sharding import PartitionSpec as P

SLOT_MAX = 8192
HALO = 16
SMALL_ROWS = 16
VMEM_BYTES = 56 << 20
TILE = 256
KERNEL_COST = pl.CostEstimate(flops=1 << 36, bytes_accessed=1 << 20, transcendentals=0)

norm_eps = 1e-05


def multiply(left_side, right_side):
    return jnp.dot(left_side, right_side, preferred_element_type=jnp.float32)


def against(left_side, right_side):
    return lax.dot_general(
        left_side, right_side, (((1,), (1,)), ((), ())), preferred_element_type=jnp.float32
    )


def outer_sum(left_side, right_side):
    return lax.dot_general(
        left_side, right_side, (((0,), (0,)), ((), ())), preferred_element_type=jnp.float32
    )


def tie(*values):
    return lax.optimization_barrier(values)


def swap(shard, step):
    axis, bit = step
    count = lax.axis_size(axis)
    return lax.ppermute(shard, axis, [(i, i ^ bit) for i in range(count)])


def gather_steps(stack, steps):
    for step in steps:
        stack = jnp.concatenate([stack, swap(stack, step)], axis=0)
    return stack


def last_step(stack, step):
    return [stack, swap(stack, step)]


def exchanged(parts, step):
    keep, send = parts
    return keep, swap(send, step)


def folded(parts):
    keep, come = parts
    total = keep.astype(jnp.float32) + come.astype(jnp.float32)
    half = total.shape[0] // 2
    if not half:
        return total[0]
    return total[:half].astype(jnp.bfloat16), total[half:].astype(jnp.bfloat16)


def masks_at(position, steps):
    masks = {"dp": 0, "seq": 0}
    for place, (axis, bit) in enumerate(steps):
        masks[axis] = masks[axis] + ((position >> place) & 1) * bit
    return masks["dp"], masks["seq"]


def tile_of(ref, row, rows, col, cols):
    return ref.at[pl.ds(pl.multiple_of(row * rows, rows), rows), pl.ds(pl.multiple_of(col * cols, cols), cols)]


def dp_gather(block, steps):
    blocks = [block]
    for step in steps:
        blocks = blocks + [swap(b, step) for b in blocks]
    return blocks


def dp_scatter(parts, steps):
    for step in reversed(steps):
        half = len(parts) // 2
        moved = [swap(send.astype(jnp.bfloat16), step) for send in parts[half:]]
        parts = [
            new if keep is None else keep.astype(jnp.float32) + new.astype(jnp.float32)
            for keep, new in zip(parts[:half], moved)
        ]
    return parts


class Piece(NamedTuple):
    steps: list
    block: tuple
    view: object


def start_loads(ids_ref, refs, pieces, into, sem):
    for place, piece in enumerate(pieces):
        first = 0
        for part in refs[2 * place : 2 * place + 2]:

            def start(position, carry, part=part, first=first, piece=piece):
                mask_dp, mask_seq = masks_at(position + first, piece.steps)
                pltpu.make_async_copy(
                    part.at[position],
                    piece.view(into, ids_ref[0] ^ mask_dp, ids_ref[1] ^ mask_seq),
                    sem,
                ).start()
                return carry

            lax.fori_loop(0, part.shape[0], start, 0)
            first += part.shape[0]


def start_stores(ids_ref, whole, pieces, outs, sem):
    each = len(outs) // len(pieces)
    for place, piece in enumerate(pieces):
        size = 2 ** len(piece.steps) // each
        for part in range(each):

            def start(position, carry, first=part * size, out=outs[each * place + part], piece=piece):
                mask_dp, mask_seq = masks_at(position + first, piece.steps)
                source = piece.view(whole, ids_ref[0] ^ mask_dp, ids_ref[1] ^ mask_seq)
                pltpu.make_async_copy(source, out.at[position], sem).start()
                return carry

            lax.fori_loop(0, size, start, 0)


def wait_whole(ref, sem):
    pltpu.make_async_copy(ref, ref, sem).wait()


def fetch_block(blocks, buffers, sems):
    i = pl.program_id(0)

    rows = buffers.shape[1]

    def copy(place):
        slot = place % 2
        source = blocks[place // 2].at[pl.ds(place % 2 * rows, rows)]
        return pltpu.make_async_copy(source, buffers.at[slot], sems.at[slot])

    for place in range(2 * len(blocks)):

        @pl.when(i == place)
        def _(place=place):
            if place == 0:
                copy(0).start()
            if place + 1 < 2 * len(blocks):
                copy(place + 1).start()
            copy(place).wait()

    return buffers[i % 2]


def token_call(kernel, ids, blocks, tiled, stacks, outs, apart, scratch):
    rows, width = blocks[0].shape
    rows, count, steps = rows // 2, len(blocks), 2 * len(blocks)
    return pl.pallas_call(
        kernel,
        out_shape=[jax.ShapeDtypeStruct((rows * steps, n), t) for n, t in outs]
        + [jax.ShapeDtypeStruct((rows * 2, n), t) for n, t in apart for _ in range(count)],
        grid_spec=pltpu.PrefetchScalarGridSpec(
            num_scalar_prefetch=1,
            grid=(steps,),
            in_specs=[pl.BlockSpec(memory_space=pl.ANY)] * count
            + [pl.BlockSpec((rows, v.shape[1]), lambda i, ids: (i, 0)) for v in tiled]
            + [pl.BlockSpec(memory_space=pl.ANY)] * len(stacks),
            out_specs=[pl.BlockSpec((rows, n), lambda i, ids: (i, 0)) for n, _ in outs]
            + [
                pl.BlockSpec((rows, n), lambda i, ids, b=b: (jnp.clip(i - 2 * b, 0, 1), 0))
                for n, _ in apart
                for b in range(count)
            ],
            scratch_shapes=[
                pltpu.VMEM((2, rows, width), jnp.bfloat16),
                pltpu.SemaphoreType.DMA((2,)),
                *scratch,
            ],
        ),
        compiler_params=pltpu.CompilerParams(vmem_limit_bytes=VMEM_BYTES),
        cost_estimate=KERNEL_COST,
    )(ids, *blocks, *tiled, *stacks)


def feed_up(ids, normed, gate, gate_stacks, up, up_stacks, shape):
    count = len(normed)

    def kernel(ids_ref, *refs):
        blocks, stacks, refs = refs[:count], refs[count:-9], refs[-9:]
        act, slope, silu, whole, buffers, block_sems, gate_v, up_v, sems = refs

        @pl.when(pl.program_id(0) == 0)
        def _():
            start_loads(ids_ref, stacks[: 2 * len(gate)], gate, gate_v, sems.at[0])
            start_loads(ids_ref, stacks[2 * len(gate) :], up, up_v, sems.at[1])

        x = fetch_block(blocks, buffers, block_sems)

        @pl.when(pl.program_id(0) == 0)
        def _():
            wait_whole(gate_v, sems.at[0])
            wait_whole(up_v, sems.at[1])

        whole[...] = x
        gate_val = multiply(x, gate_v[...])
        up_val = multiply(x, up_v[...])
        sigmoid = jax.nn.sigmoid(gate_val)
        silu_gate = gate_val * sigmoid
        act[...] = (silu_gate * up_val).astype(jnp.bfloat16)
        slope[...] = (up_val * sigmoid * (1.0 + gate_val * (1.0 - sigmoid))).astype(jnp.bfloat16)
        silu[...] = silu_gate.astype(jnp.bfloat16)

    n = shape[1]
    return token_call(
        kernel,
        ids,
        normed,
        [],
        [*gate_stacks, *up_stacks],
        [(n, jnp.bfloat16)] * 3 + [(shape[0], jnp.bfloat16)],
        [],
        [pltpu.VMEM(shape, jnp.bfloat16)] * 2 + [pltpu.SemaphoreType.DMA((2,))],
    )


def feed_back(ids, final, activated, slope, silu, gate, gate_stacks, up, up_stacks, down, down_stacks, shape):
    count = len(final)
    ends = [2 * len(gate), 2 * len(gate) + 2 * len(up)]

    def kernel(ids_ref, *refs):
        blocks, (act_ref, slope_ref, silu_ref) = refs[:count], refs[count : count + 3]
        parts = 2 * count
        stacks, refs = refs[count + 3 : -8 - parts], refs[-8 - parts :]
        grad_gate, grad_up, buffers, block_sems, gate_v, up_v, down_v, sems = refs[:2] + refs[2 + parts :]
        norm_parts, out_parts = refs[2 : 2 + count], refs[2 + count : 2 + parts]

        @pl.when(pl.program_id(0) == 0)
        def _():
            start_loads(ids_ref, stacks[ends[1] :], down, down_v, sems.at[2])
            start_loads(ids_ref, stacks[: ends[0]], gate, gate_v, sems.at[0])
            start_loads(ids_ref, stacks[ends[0] : ends[1]], up, up_v, sems.at[1])

        f = fetch_block(blocks, buffers, block_sems)

        @pl.when(pl.program_id(0) == 0)
        def _():
            wait_whole(down_v, sems.at[2])
            wait_whole(gate_v, sems.at[0])
            wait_whole(up_v, sems.at[1])

        grad_act = against(f, down_v[...])
        gg = (grad_act * slope_ref[...].astype(jnp.float32)).astype(jnp.bfloat16)
        gu = (grad_act * silu_ref[...].astype(jnp.float32)).astype(jnp.bfloat16)
        grad_gate[...] = gg
        grad_up[...] = gu
        out = multiply(act_ref[...], down_v[...]).astype(jnp.bfloat16)
        grad_norm = (against(gg, gate_v[...]) + against(gu, up_v[...])).astype(jnp.bfloat16)
        for place in range(count):

            @pl.when(pl.program_id(0) // 2 == place)
            def _(place=place):
                norm_parts[place][...] = grad_norm
                out_parts[place][...] = out

    features, n = shape
    return token_call(
        kernel,
        ids,
        final,
        [activated, slope, silu],
        [*gate_stacks, *up_stacks, *down_stacks],
        [(n, jnp.bfloat16)] * 2,
        [(features, jnp.bfloat16)] * 2,
        [
            pltpu.VMEM(shape, jnp.bfloat16),
            pltpu.VMEM(shape, jnp.bfloat16),
            pltpu.VMEM((n, features), jnp.bfloat16),
            pltpu.SemaphoreType.DMA((3,)),
        ],
    )


def stack_shapes(pieces, each=2):
    shapes = []
    for piece in pieces:
        size = 2 ** len(piece.steps) // each
        shapes += [jax.ShapeDtypeStruct((size, *piece.block), jnp.bfloat16)] * each
    return shapes


def paired(parts, each=2):
    return [tuple(parts[i : i + each]) for i in range(0, len(parts), each)]


def weight_gradient(ids, lefts, rights, pieces, each=2):
    rows, columns = lefts[0].shape[1], rights[0].shape[1]
    step = min(v.shape[0] for v in (*lefts, *rights))
    tile = next((t for t in (512, 384, 256, 128) if rows % t == 0), rows)
    count = rows // tile
    shapes = stack_shapes(pieces, each)

    def kernel(ids_ref, *refs):
        sides, refs = refs[: len(lefts) + len(rights)], refs[len(lefts) + len(rights) :]
        outs, (whole, sems) = refs[:-2], refs[-2:]
        i = pl.program_id(0)
        left_rows, right_rows = [
            [v[at : at + step] for v in side for at in range(0, v.shape[0], step)]
            for side in (sides[: len(lefts)], sides[len(lefts) :])
        ]
        total = sum(outer_sum(a, b) for a, b in zip(left_rows, right_rows))
        whole[pl.ds(pl.multiple_of(i * tile, tile), tile)] = total.astype(jnp.bfloat16)

        @pl.when(i == count - 1)
        def _():
            start_stores(ids_ref, whole, pieces, outs, sems.at[0])
            wait_whole(whole, sems.at[0])

    parts = pl.pallas_call(
        kernel,
        out_shape=shapes,
        grid_spec=pltpu.PrefetchScalarGridSpec(
            num_scalar_prefetch=1,
            grid=(count,),
            in_specs=[
                *(pl.BlockSpec((v.shape[0], tile), lambda i, ids: (0, i)) for v in lefts),
                *(pl.BlockSpec((v.shape[0], columns), lambda i, ids: (0, 0)) for v in rights),
            ],
            out_specs=[pl.BlockSpec(memory_space=pl.ANY)] * len(shapes),
            scratch_shapes=[
                pltpu.VMEM((rows, columns), jnp.bfloat16),
                pltpu.SemaphoreType.DMA((1,)),
            ],
        ),
        compiler_params=pltpu.CompilerParams(vmem_limit_bytes=VMEM_BYTES),
        cost_estimate=KERNEL_COST,
    )(ids, *lefts, *rights)
    return paired(parts, each)


def mixer_forward(ids, extended, consts, in_pieces, in_stacks, out_pieces, out_stacks, slot_size):
    rows, features = extended.shape
    rows = rows - HALO
    tile = rows // 2
    count = len(in_stacks)
    wide = 3 * features

    def kernel(ids_ref, ext_ref, const_ref, *refs):
        stacks, refs = refs[: count + len(out_stacks)], refs[count + len(out_stacks) :]
        normed_one, b_out, c_out, x_out, mixed_out, gated_out, hidden_out, normed_two = refs[:8]
        in_v, out_v, mixed_s, sems = refs[8:]
        i = pl.program_id(0)

        @pl.when(i == 0)
        def _():
            start_loads(ids_ref, stacks[:count], in_pieces, in_v, sems.at[0])
            start_loads(ids_ref, stacks[count:], out_pieces, out_v, sems.at[1])

        at = pl.multiple_of(i * tile, HALO)
        x = ext_ref[pl.ds(at, HALO + tile)].astype(jnp.float32)
        scale = lax.rsqrt(jnp.mean(x * x, axis=1, keepdims=True) + norm_eps)
        normed = (x * scale * const_ref[0:1]).astype(jnp.bfloat16)
        normed_one[...] = normed[HALO:]

        @pl.when(i == 0)
        def _():
            wait_whole(in_v, sems.at[0])
            wait_whole(out_v, sems.at[1])

        b_part = multiply(normed, in_v[:, :features])
        x_part = multiply(normed, in_v[:, 2 * features :])
        b_out[...] = b_part[HALO:].astype(jnp.bfloat16)
        x_out[...] = x_part[HALO:].astype(jnp.bfloat16)
        mixed = (b_part * x_part).astype(jnp.bfloat16)
        mixed_s[...] = mixed.astype(jnp.float32)
        base = lax.rem(ids_ref[1] * rows, slot_size)

        @pl.when(jnp.logical_and(i == 0, base == 0))
        def _():
            mixed_s[0:HALO] = jnp.zeros((HALO, features), jnp.float32)

        mixed_out[pl.ds(at, HALO)] = mixed_s[0:HALO].astype(jnp.bfloat16)
        mixed_out[pl.ds(pl.multiple_of(at + HALO, HALO), tile)] = mixed[HALO:]
        conv = sum(
            const_ref[2 + k : 3 + k] * mixed_s[HALO - 2 + k : HALO - 2 + k + tile] for k in range(3)
        )
        c_part = multiply(normed[HALO:], in_v[:, features : 2 * features])
        c_out[...] = c_part.astype(jnp.bfloat16)
        gated = (c_part * conv).astype(jnp.bfloat16)
        gated_out[...] = gated
        hidden = x[HALO:] + multiply(gated, out_v[...])
        hidden_out[...] = hidden
        scale = lax.rsqrt(jnp.mean(hidden * hidden, axis=1, keepdims=True) + norm_eps)
        normed_two[...] = (hidden * scale * const_ref[1:2]).astype(jnp.bfloat16)

    f32, bf16 = jnp.float32, jnp.bfloat16
    kinds = [bf16, bf16, bf16, bf16, bf16, bf16, f32, bf16]
    shapes = [(rows + (HALO if i == 4 else 0), features) for i in range(8)]
    whole = pl.BlockSpec((rows + HALO, features), lambda i, ids: (0, 0))
    part = pl.BlockSpec((tile, features), lambda i, ids: (i, 0))
    return pl.pallas_call(
        kernel,
        out_shape=[jax.ShapeDtypeStruct(s, t) for s, t in zip(shapes, kinds)],
        grid_spec=pltpu.PrefetchScalarGridSpec(
            num_scalar_prefetch=1,
            grid=(2,),
            in_specs=[whole, pl.BlockSpec(consts.shape, lambda i, ids: (0, 0))]
            + [pl.BlockSpec(memory_space=pl.ANY)] * (count + len(out_stacks)),
            out_specs=[whole if i == 4 else part for i in range(8)],
            scratch_shapes=[
                pltpu.VMEM((features, wide), bf16),
                pltpu.VMEM((features, features), bf16),
                pltpu.VMEM((tile + HALO, features), f32),
                pltpu.SemaphoreType.DMA((2,)),
            ],
        ),
        compiler_params=pltpu.CompilerParams(vmem_limit_bytes=VMEM_BYTES),
        cost_estimate=KERNEL_COST,
    )(ids, extended, consts, *in_stacks, *out_stacks)


def mixer_back(ids, tiled, far, mixed, consts, out_pieces, out_stacks, out_grads, slot_size):
    rows, features = tiled[0].shape
    tile = rows // 2
    shapes = stack_shapes(out_grads)

    def kernel(ids_ref, *refs):
        near_ref, more_ref, final_ref, hidden_ref, c_ref, gated_ref = refs[:6]
        low_ref, high_ref, mixed_ref, const_ref = refs[6:10]
        refs = refs[10:]
        stacks, refs = refs[: len(out_stacks)], refs[len(out_stacks) :]
        grad_hidden, grad_c, grad_mixed, head, sums = refs[:5]
        outs, (out_v, whole, mixed_s, conv_s, sems) = refs[5:-5], refs[-5:]
        i = pl.program_id(0)

        @pl.when(i == 0)
        def _():
            start_loads(ids_ref, stacks, out_pieces, out_v, sems.at[0])
            sums[...] = jnp.zeros(sums.shape, jnp.float32)
            conv_s[tile:] = jnp.zeros((8, features), jnp.float32)

        @pl.when(i > 0)
        def _():
            conv_s[tile:] = conv_s[0:8]

        normed_grad = near_ref[...].astype(jnp.float32) + more_ref[...].astype(jnp.float32)
        normed_grad += jnp.where(i == 0, high_ref[...].astype(jnp.float32), low_ref[...].astype(jnp.float32))
        h = hidden_ref[...]
        scale = lax.rsqrt(jnp.mean(h * h, axis=1, keepdims=True) + norm_eps)
        weighted = normed_grad * const_ref[1:2]
        inner = jnp.mean(weighted * h, axis=1, keepdims=True)
        sums[1:2] += jnp.sum(normed_grad * h * scale, axis=0, keepdims=True)
        total = final_ref[...].astype(jnp.float32) + scale * weighted - h * (scale * scale * scale * inner)
        grad_hidden[...] = total
        branch = total.astype(jnp.bfloat16)
        outer = outer_sum(gated_ref[...], branch)

        @pl.when(i == 0)
        def _():
            wait_whole(out_v, sems.at[0])

        grad_gated = against(branch, out_v[...])
        at = pl.multiple_of((1 - i) * tile, HALO)
        mixed_s[...] = mixed_ref[pl.ds(at, HALO + tile)].astype(jnp.float32)
        conv = sum(
            const_ref[2 + k : 3 + k] * mixed_s[HALO - 2 + k : HALO - 2 + k + tile] for k in range(3)
        )
        grad_c[...] = (grad_gated * conv).astype(jnp.bfloat16)
        grad_conv = grad_gated * c_ref[...].astype(jnp.float32)
        conv_s[0:tile] = grad_conv
        for k in range(3):
            sums[2 + k : 3 + k] += jnp.sum(
                grad_conv * mixed_s[HALO - 2 + k : HALO - 2 + k + tile], axis=0, keepdims=True
            )
        grad_mixed[...] = sum(const_ref[2 + k : 3 + k] * conv_s[2 - k : 2 - k + tile] for k in range(3))

        @pl.when(i == 1)
        def _():
            live = jnp.where(lax.rem(ids_ref[1] * rows, slot_size) > 0, 1.0, 0.0)
            head[...] = jnp.zeros(head.shape, jnp.float32)
            head[0:1] = live * const_ref[2:3] * conv_s[0:1]
            head[1:2] = live * (const_ref[2:3] * conv_s[1:2] + const_ref[3:4] * conv_s[0:1])
            out_v[...] = (whole[...] + outer).astype(jnp.bfloat16)
            start_stores(ids_ref, out_v, out_grads, outs, sems.at[0])
            wait_whole(out_v, sems.at[0])

        @pl.when(i == 0)
        def _():
            whole[...] = outer

    f32, bf16 = jnp.float32, jnp.bfloat16
    part = pl.BlockSpec((tile, features), lambda i, ids: (1 - i, 0))
    once = pl.BlockSpec((8, features), lambda i, ids: (0, 0))
    parts = pl.pallas_call(
        kernel,
        out_shape=[jax.ShapeDtypeStruct((rows, features), t) for t in (f32, bf16, f32)]
        + [jax.ShapeDtypeStruct((8, features), f32)] * 2
        + shapes,
        grid_spec=pltpu.PrefetchScalarGridSpec(
            num_scalar_prefetch=1,
            grid=(2,),
            in_specs=[part] * 6
            + [pl.BlockSpec((tile, features), lambda i, ids: (0, 0))] * 2
            + [pl.BlockSpec((rows + HALO, features), lambda i, ids: (0, 0)), once]
            + [pl.BlockSpec(memory_space=pl.ANY)] * len(out_stacks),
            out_specs=[part] * 3 + [once] * 2 + [pl.BlockSpec(memory_space=pl.ANY)] * len(shapes),
            scratch_shapes=[
                pltpu.VMEM((features, features), bf16),
                pltpu.VMEM((features, features), f32),
                pltpu.VMEM((tile + HALO, features), f32),
                pltpu.VMEM((tile + 8, features), f32),
                pltpu.SemaphoreType.DMA((1,)),
            ],
        ),
        compiler_params=pltpu.CompilerParams(vmem_limit_bytes=VMEM_BYTES),
        cost_estimate=KERNEL_COST,
    )(ids, *tiled, *far, mixed, consts, *out_stacks)
    return [*parts[:5], paired(parts[5:])]


def projection_gradient(ids, normed, grad_mixed, returned, grad_c, b_part, x_part, pieces):
    rows, features = normed.shape
    tile = features // 4
    shapes = stack_shapes(pieces)

    def kernel(ids_ref, normed_ref, mixed_ref, back_ref, c_ref, b_ref, x_ref, proj, *refs):
        outs, (whole, mixed_s, sems) = refs[:-3], refs[-3:]
        i = pl.program_id(0)

        @pl.when(i == 0)
        def _():
            mixed_s[...] = mixed_ref[...]
            mixed_s[rows - 2 :] += back_ref[0:2]
            grad = mixed_s[...]
            proj[:, :features] = (grad * x_ref[...].astype(jnp.float32)).astype(jnp.bfloat16)
            proj[:, features : 2 * features] = c_ref[...]
            proj[:, 2 * features :] = (grad * b_ref[...].astype(jnp.float32)).astype(jnp.bfloat16)

        whole[pl.ds(pl.multiple_of(i * tile, tile), tile)] = outer_sum(
            normed_ref[...], proj[...]
        ).astype(jnp.bfloat16)

        @pl.when(i == 3)
        def _():
            start_stores(ids_ref, whole, pieces, outs, sems.at[0])
            wait_whole(whole, sems.at[0])

    def same(n, width):
        return pl.BlockSpec((n, width), lambda i, ids: (0, 0))

    parts = pl.pallas_call(
        kernel,
        out_shape=[jax.ShapeDtypeStruct((rows, 3 * features), jnp.bfloat16), *shapes],
        grid_spec=pltpu.PrefetchScalarGridSpec(
            num_scalar_prefetch=1,
            grid=(4,),
            in_specs=[
                pl.BlockSpec((rows, tile), lambda i, ids: (0, i)),
                same(rows, features),
                same(8, features),
                same(rows, features),
                same(rows, features),
                same(rows, features),
            ],
            out_specs=[same(rows, 3 * features)] + [pl.BlockSpec(memory_space=pl.ANY)] * len(shapes),
            scratch_shapes=[
                pltpu.VMEM((features, 3 * features), jnp.bfloat16),
                pltpu.VMEM((rows, features), jnp.float32),
                pltpu.SemaphoreType.DMA((1,)),
            ],
        ),
        compiler_params=pltpu.CompilerParams(vmem_limit_bytes=VMEM_BYTES),
        cost_estimate=KERNEL_COST,
    )(ids, normed, grad_mixed, returned, grad_c, b_part, x_part)
    return parts[0], paired(parts[1:])


def mixer_first(ids, proj, tokens, grad_hidden, sums, consts, in_pieces, in_stacks):
    rows, features = tokens.shape
    tile = rows // 2

    def kernel(ids_ref, proj_ref, x_ref, hidden_ref, sums_ref, const_ref, *refs):
        stacks, (grad_tokens, sums_out, in_v, sems) = refs[:-4], refs[-4:]

        @pl.when(pl.program_id(0) == 0)
        def _():
            start_loads(ids_ref, stacks, in_pieces, in_v, sems.at[0])
            sums_out[...] = sums_ref[...]
            wait_whole(in_v, sems.at[0])

        normed_grad = against(proj_ref[...], in_v[...])
        x = x_ref[...].astype(jnp.float32)
        scale = lax.rsqrt(jnp.mean(x * x, axis=1, keepdims=True) + norm_eps)
        weighted = normed_grad * const_ref[0:1]
        inner = jnp.mean(weighted * x, axis=1, keepdims=True)
        sums_out[0:1] += jnp.sum(normed_grad * x * scale, axis=0, keepdims=True)
        grad_tokens[...] = (
            hidden_ref[...] + scale * weighted - x * (scale * scale * scale * inner)
        ).astype(jnp.bfloat16)

    part = pl.BlockSpec((tile, features), lambda i, ids: (i, 0))
    once = pl.BlockSpec((8, features), lambda i, ids: (0, 0))
    return pl.pallas_call(
        kernel,
        out_shape=[
            jax.ShapeDtypeStruct((rows, features), jnp.bfloat16),
            jax.ShapeDtypeStruct((8, features), jnp.float32),
        ],
        grid_spec=pltpu.PrefetchScalarGridSpec(
            num_scalar_prefetch=1,
            grid=(2,),
            in_specs=[pl.BlockSpec((tile, 3 * features), lambda i, ids: (i, 0)), part, part, once, once]
            + [pl.BlockSpec(memory_space=pl.ANY)] * len(in_stacks),
            out_specs=[part, once],
            scratch_shapes=[
                pltpu.VMEM((features, 3 * features), jnp.bfloat16),
                pltpu.SemaphoreType.DMA((1,)),
            ],
        ),
        compiler_params=pltpu.CompilerParams(vmem_limit_bytes=VMEM_BYTES),
        cost_estimate=KERNEL_COST,
    )(ids, proj, tokens, grad_hidden, sums, consts, *in_stacks)


def bits_below(count):
    return [1 << i for i in range(count.bit_length() - 1)]


def per_device(
    tokens,
    mixer_gain,
    in_weight,
    conv_weight,
    out_weight,
    feed_gain,
    gate_weight,
    up_weight,
    down_weight,
    lengths,
    cotangent,
):
    n_dp, n_seq = lax.axis_size("dp"), lax.axis_size("seq")
    tok_rows, features = tokens.shape
    slot_size = min(SLOT_MAX, tok_rows * n_seq)
    own_dp, own_seq = lax.axis_index("dp"), lax.axis_index("seq")
    ids = jnp.stack([own_dp, own_seq]).astype(jnp.int32)

    seq_bits = bits_below(n_seq)
    along_y = seq_bits[: len(seq_bits) // 2]
    ys = [("seq", b) for b in reversed(along_y)]
    zs = [("seq", b) for b in reversed(seq_bits[len(along_y) :])]
    core = [("dp", 1)]
    xs = [("dp", b) for b in reversed(bits_below(n_dp)[1:])]
    in_orders = [zs + xs + ys + core, ys + zs + xs + core]
    out_order = zs[:1] + xs + ys + zs[1:] + core
    far_order, near_order = zs[:1] + ys + zs[1:], zs + ys
    token_order = xs + core

    position = own_seq * tok_rows + jnp.arange(tok_rows, dtype=jnp.int32)
    in_slot = position % slot_size
    slot_index = position // slot_size
    slot_ids = jnp.arange(lengths.shape[1], dtype=jnp.int32)
    slot_length = jnp.sum(
        jnp.where(slot_index[:, None] == slot_ids[None, :], lengths[0][None, :], 0), axis=1
    )
    live_mask = (in_slot < slot_length).astype(jnp.float32)[:, None]

    in_rows, in_cols = in_weight.shape
    out_rows, out_cols = out_weight.shape
    in_cut = (in_cols // 128 + 1) // 2 * 128
    in_cuts = [0, in_cut, in_cols]
    third = in_cols // 3
    small_cols = mixer_gain.shape[0]
    small = jnp.concatenate([mixer_gain[None], feed_gain[None], conv_weight], axis=0)
    small = jnp.pad(small, ((0, SMALL_ROWS - small.shape[0]), (0, -small_cols % 128)))
    small_order = zs + ys
    mixer = [in_weight[None, :, :in_cut], in_weight[None, :, in_cut:], out_weight[None]]
    orders = [*in_orders, out_order]
    hidden_units = gate_weight.shape[1]
    gate_rows = gate_weight.shape[0]
    down_rows, down_cols = down_weight.shape
    ratio = n_seq // n_dp
    turned = [(e % 2) * (n_dp // 2) + e // 2 for e in range(n_dp)]
    home = [
        (e * n_seq + s, (s // ratio) * n_seq + turned[e] * ratio + s % ratio)
        for e in range(n_dp)
        for s in range(n_seq)
    ]
    cuts = [0, -(-down_rows // 32) * 16, down_rows]

    def gate_view(ref, dp, seq):
        return ref.at[pl.ds(pl.multiple_of(seq * gate_rows, gate_rows), gate_rows)]

    def down_view(cut):
        low, high = cuts[cut], cuts[cut + 1]

        def view(ref, dp, seq):
            row = pl.multiple_of((seq % ratio) * down_rows + low, 16)
            place = seq // ratio
            place = place % (n_dp // 2) * 2 + place // (n_dp // 2)
            col = pl.multiple_of(place * down_cols, down_cols)
            return ref.at[pl.ds(row, high - low), pl.ds(col, down_cols)]

        return view

    gate = [Piece(near_order, gate_weight.shape, gate_view)]
    up = [Piece(far_order, up_weight.shape, gate_view)]
    down = [
        Piece(order, (cuts[i + 1] - cuts[i], down_cols), down_view(i))
        for i, order in enumerate((near_order, far_order))
    ]

    def with_core(blocks):
        return blocks + [swap(v, core[0]) for v in blocks]

    grad_final = (live_mask * cotangent.astype(jnp.float32)).astype(jnp.bfloat16)
    middle = len(orders[0]) // 2
    z_first, last = 1, len(zs) + len(ys) - 1
    mixer = [gather_steps(v, order[:1]) for v, order in zip(mixer, orders)]
    mixer, small, tokens = tie(mixer, small, tokens)
    mixer = [gather_steps(v, order[1:middle]) for v, order in zip(mixer, orders)]
    before = lax.ppermute(
        tokens[tok_rows - HALO :], "seq", [(i, i + 1) for i in range(n_seq - 1)]
    )
    small = gather_steps(small[None], small_order)
    mixer, gate_weight, up_weight = tie(mixer, gate_weight, up_weight)
    mixer = [gather_steps(v, order[middle:-1]) for v, order in zip(mixer, orders)]
    gate_up = [
        gather_steps(v[None], p.steps[:z_first])
        for v, p in zip((gate_weight, up_weight), (*gate, *up))
    ]
    extended = jnp.concatenate([before, tokens], axis=0)
    places = jnp.stack([jnp.int32(masks_at(p, small_order)[1]) for p in range(n_seq)])
    chosen = (own_seq ^ jnp.arange(n_seq))[:, None] == places[None]
    consts = jnp.einsum(
        "sp,pkc->ksc",
        chosen.astype(jnp.bfloat16),
        small[:, :8, :small_cols],
        preferred_element_type=jnp.float32,
    ).reshape(8, features)
    mixer, gate_up, consts, extended, down_weight, grad_final = tie(
        mixer, gate_up, consts, extended, down_weight, grad_final
    )
    stacks = [last_step(v, order[-1]) for v, order in zip(mixer, orders)]
    stacks, gate_up, down_weight, grad_final = tie(stacks, gate_up, down_weight, grad_final)

    def in_view(low, high):

        def view(ref, dp, seq):
            row = pl.multiple_of(seq * in_rows, in_rows)
            col = pl.multiple_of(dp * in_cols + low, 128)
            return ref.at[pl.ds(row, in_rows), pl.ds(col, high - low)]

        return view

    def out_view(ref, dp, seq):
        return tile_of(ref, seq, out_rows, dp, out_cols)

    in_pieces = [
        Piece(order, (in_rows, in_cuts[i + 1] - in_cuts[i]), in_view(in_cuts[i], in_cuts[i + 1]))
        for i, order in enumerate(in_orders)
    ]
    half_block = gate_rows // 2

    def half_view(low):
        def view(ref, dp, seq):
            row = pl.multiple_of(seq * gate_rows + low, half_block)
            return ref.at[pl.ds(row, half_block)]

        return view

    feed_grads = [
        Piece(order, (half_block, hidden_units), half_view(low))
        for order, low in ((near_order, 0), (far_order, half_block))
    ]
    in_grads = [
        Piece(order, (in_rows, third), in_view(i * third, (i + 1) * third))
        for i, order in enumerate(orders)
    ]
    out_grads = [Piece(zs + xs + ys + core, out_weight.shape, out_view)]
    out_pieces = [Piece(out_order, out_weight.shape, out_view)]
    in_stacks, out_stacks = stacks[0] + stacks[1], stacks[2]

    gate_up = [gather_steps(v, p.steps[z_first:last]) for v, p in zip(gate_up, (*gate, *up))]
    down_shard = lax.ppermute(down_weight, ("dp", "seq"), home)
    final_there = dp_gather(grad_final, xs)[1:]
    final_near = swap(grad_final, core[0])
    forward = mixer_forward(
        ids, extended, consts, in_pieces, in_stacks, out_pieces, out_stacks, slot_size
    )
    forward, gate_up, down_shard, grad_final, final_near, final_there = tie(
        forward, gate_up, down_shard, grad_final, final_near, final_there
    )
    normed_one, b_part, c_part, x_part, mixed, gated, hidden, normed_two = forward

    wide = (features, hidden_units)
    gate_stacks, up_stacks = [last_step(v, p.steps[-1]) for v, p in zip(gate_up, (*gate, *up))]
    down_stack = gather_steps(down_shard[None], near_order[:z_first])
    normed_there = dp_gather(normed_two, xs)[1:]
    final_blocks = [grad_final, final_near] + with_core(final_there)
    normed_two, normed_there, gate_stacks, up_stacks, down_stack, final_blocks = tie(
        normed_two, normed_there, gate_stacks, up_stacks, down_stack, final_blocks
    )
    downs = [down_stack[:, a:b] for a, b in zip(cuts, cuts[1:])]
    normed_blocks = with_core([normed_two]) + with_core(normed_there)
    normed_blocks, downs, gate_stacks, up_stacks = tie(normed_blocks, downs, gate_stacks, up_stacks)
    downs = [gather_steps(v, p.steps[z_first:last]) for v, p in zip(downs, down)]
    activated, slope, silu, normed_all = feed_up(ids, normed_blocks, gate, gate_stacks, up, up_stacks, wide)
    activated, downs = tie(activated, downs)
    down_stacks = [v for stack, p in zip(downs, down) for v in last_step(stack, p.steps[-1])]
    down_parts = weight_gradient(ids, [activated], final_blocks, down)
    down_parts, down_stacks = tie(down_parts, down_stacks)

    def sent(parts, pieces, place):
        return [exchanged(v, p.steps[place]) for v, p in zip(parts, pieces)]

    def fold_all(parts):
        return [folded(v) for v in parts]

    def sent_on(parts, pieces):
        count = len(pieces[0].steps)
        for place in range(count - 2, 0, -1):
            parts = sent(fold_all(parts) if place < count - 2 else parts, pieces, place)
        return parts

    def joined(parts):
        return [tuple(jnp.concatenate(v, axis=1) for v in zip(*parts))]

    def core_halves(v):
        near, far = v[:2], v[2:]
        half = len(far) // 2
        return near[0], near[1], far[:half], far[half:]

    def far_added(keep, come):
        return [
            (a.astype(jnp.float32) + b.astype(jnp.float32)).astype(jnp.bfloat16)
            for a, b in zip(keep, come)
        ]

    down_parts = sent(down_parts, down, -1)
    grad_gate, grad_up, *back = feed_back(
        ids, final_blocks, activated, slope, silu, gate, gate_stacks, up, up_stacks, down, down_stacks, wide
    )
    back, feed = back[:n_dp], back[n_dp:]
    back, feed, grad_gate, grad_up, down_parts = tie(back, feed, grad_gate, grad_up, down_parts)
    near, near_send, far, far_send = core_halves(back)
    far_come = [swap(v, core[0]) for v in far_send]
    far, far_come, near, near_send, grad_gate, grad_up, feed, down_parts = tie(
        far, far_come, near, near_send, grad_gate, grad_up, feed, down_parts
    )
    far = far_added(far, far_come)
    half_rows = tok_rows // 2
    far_low, far_high = [v[:half_rows] for v in far], [v[half_rows:] for v in far]
    down_parts = fold_all(down_parts)
    far_low, far_high, down_parts, near, near_send, grad_gate, grad_up, feed = tie(
        far_low, far_high, down_parts, near, near_send, grad_gate, grad_up, feed
    )
    far_low = dp_scatter([None] + far_low, xs)
    near_more = swap(near_send, core[0])
    down_parts = sent_on(down_parts, down)
    gate_parts = weight_gradient(ids, [normed_all], [grad_gate], feed_grads)
    gate_parts, far_low, far_high, grad_up, near, near_more, down_parts, feed = tie(
        gate_parts, far_low, far_high, grad_up, near, near_more, down_parts, feed
    )
    down_parts = joined(fold_all(down_parts))
    feed_near, feed_send, feed_far, feed_come = core_halves(feed)
    down_parts, gate_parts, feed_far, feed_come, grad_up, far_low, far_high = tie(
        down_parts, gate_parts, feed_far, feed_come, grad_up, far_low, far_high
    )
    far_high = dp_scatter([None] + far_high, xs)
    gate_parts = sent(gate_parts, feed_grads, -1)
    feed_come = [swap(v, core[0]) for v in feed_come]
    down_parts = sent(down_parts, down, 0)
    up_parts = weight_gradient(ids, [normed_all], [grad_up], feed_grads)
    up_parts, far_low, far_high, gate_parts, feed_far, feed_come, down_parts = tie(
        up_parts, far_low, far_high, gate_parts, feed_far, feed_come, down_parts
    )

    feed_far = far_added(feed_far, feed_come)
    feed_low, feed_high = [v[:half_rows] for v in feed_far], [v[half_rows:] for v in feed_far]
    own_down = folded(down_parts[0]).astype(jnp.bfloat16)
    feed_low, feed_high, up_parts, gate_parts, far_low, far_high, own_down = tie(
        feed_low, feed_high, up_parts, gate_parts, far_low, far_high, own_down
    )
    up_parts = sent(up_parts, feed_grads, -1)
    feed_low = dp_scatter([None] + feed_low, xs)
    own_down = lax.ppermute(own_down, ("dp", "seq"), [(b, a) for a, b in home])
    grad_hidden, grad_c, grad_mixed, first_rows, sums, out_parts = mixer_back(
        ids,
        [near, near_more, grad_final, hidden, c_part, gated],
        far_low + far_high,
        mixed,
        consts,
        out_pieces,
        out_stacks,
        out_grads,
        slot_size,
    )
    out_parts, grad_mixed, first_rows, gate_parts, up_parts, feed_low, feed_high, own_down = tie(
        out_parts, grad_mixed, first_rows, gate_parts, up_parts, feed_low, feed_high, own_down
    )
    returned = lax.ppermute(first_rows, "seq", [(i + 1, i) for i in range(n_seq - 1)])
    out_parts = fold_all(sent(out_parts, out_grads, -1))
    gate_parts, up_parts = fold_all(gate_parts), fold_all(up_parts)
    returned, out_parts, up_parts, gate_parts, feed_high = tie(
        returned, out_parts, up_parts, gate_parts, feed_high
    )
    gate_parts = sent_on(gate_parts, feed_grads)
    up_parts = sent_on(up_parts, feed_grads)
    feed_high = dp_scatter([None] + feed_high, xs)
    grad_proj, in_parts = projection_gradient(
        ids, normed_one, grad_mixed, returned, grad_c, b_part, x_part, in_grads
    )
    in_parts, up_parts, gate_parts, grad_proj, out_parts, feed_high = tie(
        in_parts, up_parts, gate_parts, grad_proj, out_parts, feed_high
    )
    gate_parts = joined(fold_all(gate_parts))
    in_parts, gate_parts, out_parts, grad_proj = tie(in_parts, gate_parts, out_parts, grad_proj)
    in_parts = sent(in_parts, in_grads, -1)
    out_parts = sent(out_parts, out_grads, -2)
    gate_parts = sent(gate_parts, feed_grads, 0)
    grad_tokens, sums = mixer_first(ids, grad_proj, tokens, grad_hidden, sums, consts, in_pieces, in_stacks)
    in_parts, out_parts, sums, gate_parts, up_parts, feed_send = tie(
        in_parts, out_parts, sums, gate_parts, up_parts, feed_send
    )
    sum_steps = core + ys + xs + zs[::-1]
    for step in sum_steps[:1]:
        sums = sums + swap(sums, step)
    in_parts, out_parts, up_parts = fold_all(in_parts), fold_all(out_parts), joined(fold_all(up_parts))
    in_parts, out_parts, up_parts, sums = tie(in_parts, out_parts, up_parts, sums)
    in_parts = sent(in_parts, in_grads, -2)
    out_parts = sent(out_parts, out_grads, -3)
    up_parts = sent(up_parts, feed_grads, 0)
    sums = (sums, swap(sums, sum_steps[1]))
    in_parts, out_parts, up_parts, sums, feed_send = tie(in_parts, out_parts, up_parts, sums, feed_send)
    in_parts, out_parts, sums = fold_all(in_parts), fold_all(out_parts), sums[0] + sums[1]
    in_parts, out_parts, sums = tie(in_parts, out_parts, sums)
    in_parts = sent(in_parts, in_grads, -3)
    out_parts = sent(out_parts, out_grads, -4)
    sums = (sums, swap(sums, sum_steps[2]))
    in_parts, out_parts, sums, feed_send = tie(in_parts, out_parts, sums, feed_send)
    in_parts, out_parts, sums = fold_all(in_parts), fold_all(out_parts), sums[0] + sums[1]
    in_parts, out_parts, sums = tie(in_parts, out_parts, sums)
    in_parts = sent(in_parts, in_grads, -4)
    out_parts = sent(out_parts, out_grads, -5)
    sums = (sums, swap(sums, sum_steps[3]))
    feed_more = swap(feed_send, core[0])
    in_parts, out_parts, sums, feed_more, own_down = tie(in_parts, out_parts, sums, feed_more, own_down)
    sums = sums[0] + sums[1]
    for step in sum_steps[4:]:
        sums = sums + swap(sums, step)
    own_down = own_down.astype(jnp.float32)

    def rest(parts, piece, done):
        parts = folded(parts)
        for place in range(len(piece.steps) - done - 1, -1, -1):
            parts = folded(exchanged(parts, piece.steps[place]))
        return parts

    own_in = [rest(v, p, 4) for v, p in zip(in_parts, in_grads)]
    own_in = jnp.concatenate(own_in, axis=1)
    own_out = rest(out_parts[0], out_grads[0], 5)
    own_gate = folded(gate_parts[0])
    own_up = folded(up_parts[0])
    own_sums = lax.dynamic_slice(sums, (0, own_seq * small_cols), (8, small_cols))
    feed_out = jnp.concatenate(feed_low + feed_high, axis=0).astype(jnp.float32)
    feed_out = feed_out + feed_near.astype(jnp.float32) + feed_more.astype(jnp.float32)
    output = (live_mask * (hidden + feed_out)).astype(jnp.bfloat16)
    return (
        output,
        grad_tokens,
        own_sums[0],
        own_in,
        own_sums[2:5],
        own_out,
        own_sums[1],
        own_gate,
        own_up,
        own_down,
    )


def solution(mesh):
    in_specs = (
        P(("dp", "seq"), None),
        P("seq"),
        P("seq", "dp"),
        P(None, "seq"),
        P("seq", "dp"),
        P("seq"),
        P("seq", "dp"),
        P("seq", "dp"),
        P("seq", "dp"),
        P("dp", None),
        P(("dp", "seq"), None),
    )
    out_specs = (
        P(("dp", "seq"), None),
        P(("dp", "seq"), None),
        P("seq"),
        P("seq", "dp"),
        P(None, "seq"),
        P("seq", "dp"),
        P("seq"),
        P("seq", "dp"),
        P("seq", "dp"),
        P("seq", "dp"),
    )
    return jax.shard_map(
        per_device, mesh=mesh, in_specs=in_specs, out_specs=out_specs, check_vma=False
    )
```

```python
from typing import NamedTuple

import jax
import jax.numpy as jnp
from jax import lax
from jax.experimental import pallas as pl
from jax.experimental.pallas import tpu as pltpu
from jax.sharding import PartitionSpec as P

SLOT_MAX = 8192
HALO = 16
SMALL_ROWS = 16
VMEM_BYTES = 56 << 20
TILE = 256
KERNEL_COST = pl.CostEstimate(flops=1 << 36, bytes_accessed=1 << 20, transcendentals=0)

norm_eps = 1e-05


def multiply(left_side, right_side):
    return jnp.dot(left_side, right_side, preferred_element_type=jnp.float32)


def against(left_side, right_side):
    return lax.dot_general(
        left_side, right_side, (((1,), (1,)), ((), ())), preferred_element_type=jnp.float32
    )


def outer_sum(left_side, right_side):
    return lax.dot_general(
        left_side, right_side, (((0,), (0,)), ((), ())), preferred_element_type=jnp.float32
    )


def tie(*values):
    return lax.optimization_barrier(values)


def swap(shard, step):
    axis, bit = step
    count = lax.axis_size(axis)
    return lax.ppermute(shard, axis, [(i, i ^ bit) for i in range(count)])


def gather_steps(stack, steps):
    for step in steps:
        stack = jnp.concatenate([stack, swap(stack, step)], axis=0)
    return stack


def last_step(stack, step):
    return [stack, swap(stack, step)]


def exchanged(parts, step):
    keep, send = parts
    return keep, swap(send, step)


def folded(parts):
    keep, come = parts
    total = keep.astype(jnp.float32) + come.astype(jnp.float32)
    half = total.shape[0] // 2
    if not half:
        return total[0]
    return total[:half].astype(jnp.bfloat16), total[half:].astype(jnp.bfloat16)


def masks_at(position, steps):
    masks = {"dp": 0, "seq": 0}
    for place, (axis, bit) in enumerate(steps):
        masks[axis] = masks[axis] + ((position >> place) & 1) * bit
    return masks["dp"], masks["seq"]


def tile_of(ref, row, rows, col, cols):
    return ref.at[pl.ds(pl.multiple_of(row * rows, rows), rows), pl.ds(pl.multiple_of(col * cols, cols), cols)]


def dp_gather(block, steps):
    blocks = [block]
    for step in steps:
        blocks = blocks + [swap(b, step) for b in blocks]
    return blocks


def dp_scatter(parts, steps):
    for step in reversed(steps):
        half = len(parts) // 2
        moved = [swap(send.astype(jnp.bfloat16), step) for send in parts[half:]]
        parts = [
            new if keep is None else keep.astype(jnp.float32) + new.astype(jnp.float32)
            for keep, new in zip(parts[:half], moved)
        ]
    return parts


class Piece(NamedTuple):
    steps: list
    block: tuple
    view: object


def start_loads(ids_ref, refs, pieces, into, sem):
    for place, piece in enumerate(pieces):
        first = 0
        for part in refs[2 * place : 2 * place + 2]:

            def start(position, carry, part=part, first=first, piece=piece):
                mask_dp, mask_seq = masks_at(position + first, piece.steps)
                pltpu.make_async_copy(
                    part.at[position],
                    piece.view(into, ids_ref[0] ^ mask_dp, ids_ref[1] ^ mask_seq),
                    sem,
                ).start()
                return carry

            lax.fori_loop(0, part.shape[0], start, 0)
            first += part.shape[0]


def start_stores(ids_ref, whole, pieces, outs, sem):
    each = len(outs) // len(pieces)
    for place, piece in enumerate(pieces):
        size = 2 ** len(piece.steps) // each
        for part in range(each):

            def start(position, carry, first=part * size, out=outs[each * place + part], piece=piece):
                mask_dp, mask_seq = masks_at(position + first, piece.steps)
                source = piece.view(whole, ids_ref[0] ^ mask_dp, ids_ref[1] ^ mask_seq)
                pltpu.make_async_copy(source, out.at[position], sem).start()
                return carry

            lax.fori_loop(0, size, start, 0)


def wait_whole(ref, sem):
    pltpu.make_async_copy(ref, ref, sem).wait()


def fetch_block(blocks, buffers, sems):
    i = pl.program_id(0)

    rows = buffers.shape[1]

    def copy(place):
        slot = place % 2
        source = blocks[place // 2].at[pl.ds(place % 2 * rows, rows)]
        return pltpu.make_async_copy(source, buffers.at[slot], sems.at[slot])

    for place in range(2 * len(blocks)):

        @pl.when(i == place)
        def _(place=place):
            if place == 0:
                copy(0).start()
            if place + 1 < 2 * len(blocks):
                copy(place + 1).start()
            copy(place).wait()

    return buffers[i % 2]


def token_call(kernel, ids, blocks, tiled, stacks, outs, apart, scratch):
    rows, width = blocks[0].shape
    rows, count, steps = rows // 2, len(blocks), 2 * len(blocks)
    return pl.pallas_call(
        kernel,
        out_shape=[jax.ShapeDtypeStruct((rows * steps, n), t) for n, t in outs]
        + [jax.ShapeDtypeStruct((rows * 2, n), t) for n, t in apart for _ in range(count)],
        grid_spec=pltpu.PrefetchScalarGridSpec(
            num_scalar_prefetch=1,
            grid=(steps,),
            in_specs=[pl.BlockSpec(memory_space=pl.ANY)] * count
            + [pl.BlockSpec((rows, v.shape[1]), lambda i, ids: (i, 0)) for v in tiled]
            + [pl.BlockSpec(memory_space=pl.ANY)] * len(stacks),
            out_specs=[pl.BlockSpec((rows, n), lambda i, ids: (i, 0)) for n, _ in outs]
            + [
                pl.BlockSpec((rows, n), lambda i, ids, b=b: (jnp.clip(i - 2 * b, 0, 1), 0))
                for n, _ in apart
                for b in range(count)
            ],
            scratch_shapes=[
                pltpu.VMEM((2, rows, width), jnp.bfloat16),
                pltpu.SemaphoreType.DMA((2,)),
                *scratch,
            ],
        ),
        compiler_params=pltpu.CompilerParams(vmem_limit_bytes=VMEM_BYTES),
        cost_estimate=KERNEL_COST,
    )(ids, *blocks, *tiled, *stacks)


def feed_up(ids, normed, gate, gate_stacks, up, up_stacks, shape):
    count = len(normed)

    def kernel(ids_ref, *refs):
        blocks, stacks, refs = refs[:count], refs[count:-9], refs[-9:]
        act, slope, silu, whole, buffers, block_sems, gate_v, up_v, sems = refs

        @pl.when(pl.program_id(0) == 0)
        def _():
            start_loads(ids_ref, stacks[: 2 * len(gate)], gate, gate_v, sems.at[0])
            start_loads(ids_ref, stacks[2 * len(gate) :], up, up_v, sems.at[1])

        x = fetch_block(blocks, buffers, block_sems)

        @pl.when(pl.program_id(0) == 0)
        def _():
            wait_whole(gate_v, sems.at[0])
            wait_whole(up_v, sems.at[1])

        whole[...] = x
        gate_val = multiply(x, gate_v[...])
        up_val = multiply(x, up_v[...])
        sigmoid = jax.nn.sigmoid(gate_val)
        silu_gate = gate_val * sigmoid
        act[...] = (silu_gate * up_val).astype(jnp.bfloat16)
        slope[...] = (up_val * sigmoid * (1.0 + gate_val * (1.0 - sigmoid))).astype(jnp.bfloat16)
        silu[...] = silu_gate.astype(jnp.bfloat16)

    n = shape[1]
    return token_call(
        kernel,
        ids,
        normed,
        [],
        [*gate_stacks, *up_stacks],
        [(n, jnp.bfloat16)] * 3 + [(shape[0], jnp.bfloat16)],
        [],
        [pltpu.VMEM(shape, jnp.bfloat16)] * 2 + [pltpu.SemaphoreType.DMA((2,))],
    )


def feed_back(ids, final, activated, slope, silu, gate, gate_stacks, up, up_stacks, down, down_stacks, shape):
    count = len(final)
    ends = [2 * len(gate), 2 * len(gate) + 2 * len(up)]

    def kernel(ids_ref, *refs):
        blocks, (act_ref, slope_ref, silu_ref) = refs[:count], refs[count : count + 3]
        parts = 2 * count
        stacks, refs = refs[count + 3 : -8 - parts], refs[-8 - parts :]
        grad_gate, grad_up, buffers, block_sems, gate_v, up_v, down_v, sems = refs[:2] + refs[2 + parts :]
        norm_parts, out_parts = refs[2 : 2 + count], refs[2 + count : 2 + parts]

        @pl.when(pl.program_id(0) == 0)
        def _():
            start_loads(ids_ref, stacks[ends[1] :], down, down_v, sems.at[2])
            start_loads(ids_ref, stacks[: ends[0]], gate, gate_v, sems.at[0])
            start_loads(ids_ref, stacks[ends[0] : ends[1]], up, up_v, sems.at[1])

        f = fetch_block(blocks, buffers, block_sems)

        @pl.when(pl.program_id(0) == 0)
        def _():
            wait_whole(down_v, sems.at[2])
            wait_whole(gate_v, sems.at[0])
            wait_whole(up_v, sems.at[1])

        grad_act = against(f, down_v[...])
        gg = (grad_act * slope_ref[...].astype(jnp.float32)).astype(jnp.bfloat16)
        gu = (grad_act * silu_ref[...].astype(jnp.float32)).astype(jnp.bfloat16)
        grad_gate[...] = gg
        grad_up[...] = gu
        out = multiply(act_ref[...], down_v[...]).astype(jnp.bfloat16)
        grad_norm = (against(gg, gate_v[...]) + against(gu, up_v[...])).astype(jnp.bfloat16)
        for place in range(count):

            @pl.when(pl.program_id(0) // 2 == place)
            def _(place=place):
                norm_parts[place][...] = grad_norm
                out_parts[place][...] = out

    features, n = shape
    return token_call(
        kernel,
        ids,
        final,
        [activated, slope, silu],
        [*gate_stacks, *up_stacks, *down_stacks],
        [(n, jnp.bfloat16)] * 2,
        [(features, jnp.bfloat16)] * 2,
        [
            pltpu.VMEM(shape, jnp.bfloat16),
            pltpu.VMEM(shape, jnp.bfloat16),
            pltpu.VMEM((n, features), jnp.bfloat16),
            pltpu.SemaphoreType.DMA((3,)),
        ],
    )


def stack_shapes(pieces, each=2):
    shapes = []
    for piece in pieces:
        size = 2 ** len(piece.steps) // each
        shapes += [jax.ShapeDtypeStruct((size, *piece.block), jnp.bfloat16)] * each
    return shapes


def paired(parts, each=2):
    return [tuple(parts[i : i + each]) for i in range(0, len(parts), each)]


def weight_gradient(ids, lefts, rights, pieces, each=2):
    rows, columns = lefts[0].shape[1], rights[0].shape[1]
    step = min(v.shape[0] for v in (*lefts, *rights))
    tile = next((t for t in (512, 384, 256, 128) if rows % t == 0), rows)
    count = rows // tile
    shapes = stack_shapes(pieces, each)

    def kernel(ids_ref, *refs):
        sides, refs = refs[: len(lefts) + len(rights)], refs[len(lefts) + len(rights) :]
        outs, (whole, sems) = refs[:-2], refs[-2:]
        i = pl.program_id(0)
        left_rows, right_rows = [
            [v[at : at + step] for v in side for at in range(0, v.shape[0], step)]
            for side in (sides[: len(lefts)], sides[len(lefts) :])
        ]
        total = sum(outer_sum(a, b) for a, b in zip(left_rows, right_rows))
        whole[pl.ds(pl.multiple_of(i * tile, tile), tile)] = total.astype(jnp.bfloat16)

        @pl.when(i == count - 1)
        def _():
            start_stores(ids_ref, whole, pieces, outs, sems.at[0])
            wait_whole(whole, sems.at[0])

    parts = pl.pallas_call(
        kernel,
        out_shape=shapes,
        grid_spec=pltpu.PrefetchScalarGridSpec(
            num_scalar_prefetch=1,
            grid=(count,),
            in_specs=[
                *(pl.BlockSpec((v.shape[0], tile), lambda i, ids: (0, i)) for v in lefts),
                *(pl.BlockSpec((v.shape[0], columns), lambda i, ids: (0, 0)) for v in rights),
            ],
            out_specs=[pl.BlockSpec(memory_space=pl.ANY)] * len(shapes),
            scratch_shapes=[
                pltpu.VMEM((rows, columns), jnp.bfloat16),
                pltpu.SemaphoreType.DMA((1,)),
            ],
        ),
        compiler_params=pltpu.CompilerParams(vmem_limit_bytes=VMEM_BYTES),
        cost_estimate=KERNEL_COST,
    )(ids, *lefts, *rights)
    return paired(parts, each)


def mixer_forward(ids, extended, consts, in_pieces, in_stacks, out_pieces, out_stacks, slot_size):
    rows, features = extended.shape
    rows = rows - HALO
    tile = rows // 2
    count = len(in_stacks)
    wide = 3 * features

    def kernel(ids_ref, ext_ref, const_ref, *refs):
        stacks, refs = refs[: count + len(out_stacks)], refs[count + len(out_stacks) :]
        normed_one, b_out, c_out, x_out, mixed_out, gated_out, hidden_out, normed_two = refs[:8]
        in_v, out_v, mixed_s, sems = refs[8:]
        i = pl.program_id(0)

        @pl.when(i == 0)
        def _():
            start_loads(ids_ref, stacks[:count], in_pieces, in_v, sems.at[0])
            start_loads(ids_ref, stacks[count:], out_pieces, out_v, sems.at[1])

        at = pl.multiple_of(i * tile, HALO)
        x = ext_ref[pl.ds(at, HALO + tile)].astype(jnp.float32)
        scale = lax.rsqrt(jnp.mean(x * x, axis=1, keepdims=True) + norm_eps)
        normed = (x * scale * const_ref[0:1]).astype(jnp.bfloat16)
        normed_one[...] = normed[HALO:]

        @pl.when(i == 0)
        def _():
            wait_whole(in_v, sems.at[0])
            wait_whole(out_v, sems.at[1])

        b_part = multiply(normed, in_v[:, :features])
        x_part = multiply(normed, in_v[:, 2 * features :])
        b_out[...] = b_part[HALO:].astype(jnp.bfloat16)
        x_out[...] = x_part[HALO:].astype(jnp.bfloat16)
        mixed = (b_part * x_part).astype(jnp.bfloat16)
        mixed_s[...] = mixed.astype(jnp.float32)
        base = lax.rem(ids_ref[1] * rows, slot_size)

        @pl.when(jnp.logical_and(i == 0, base == 0))
        def _():
            mixed_s[0:HALO] = jnp.zeros((HALO, features), jnp.float32)

        mixed_out[pl.ds(at, HALO)] = mixed_s[0:HALO].astype(jnp.bfloat16)
        mixed_out[pl.ds(pl.multiple_of(at + HALO, HALO), tile)] = mixed[HALO:]
        conv = sum(
            const_ref[2 + k : 3 + k] * mixed_s[HALO - 2 + k : HALO - 2 + k + tile] for k in range(3)
        )
        c_part = multiply(normed[HALO:], in_v[:, features : 2 * features])
        c_out[...] = c_part.astype(jnp.bfloat16)
        gated = (c_part * conv).astype(jnp.bfloat16)
        gated_out[...] = gated
        hidden = x[HALO:] + multiply(gated, out_v[...])
        hidden_out[...] = hidden
        scale = lax.rsqrt(jnp.mean(hidden * hidden, axis=1, keepdims=True) + norm_eps)
        normed_two[...] = (hidden * scale * const_ref[1:2]).astype(jnp.bfloat16)

    f32, bf16 = jnp.float32, jnp.bfloat16
    kinds = [bf16, bf16, bf16, bf16, bf16, bf16, f32, bf16]
    shapes = [(rows + (HALO if i == 4 else 0), features) for i in range(8)]
    whole = pl.BlockSpec((rows + HALO, features), lambda i, ids: (0, 0))
    part = pl.BlockSpec((tile, features), lambda i, ids: (i, 0))
    return pl.pallas_call(
        kernel,
        out_shape=[jax.ShapeDtypeStruct(s, t) for s, t in zip(shapes, kinds)],
        grid_spec=pltpu.PrefetchScalarGridSpec(
            num_scalar_prefetch=1,
            grid=(2,),
            in_specs=[whole, pl.BlockSpec(consts.shape, lambda i, ids: (0, 0))]
            + [pl.BlockSpec(memory_space=pl.ANY)] * (count + len(out_stacks)),
            out_specs=[whole if i == 4 else part for i in range(8)],
            scratch_shapes=[
                pltpu.VMEM((features, wide), bf16),
                pltpu.VMEM((features, features), bf16),
                pltpu.VMEM((tile + HALO, features), f32),
                pltpu.SemaphoreType.DMA((2,)),
            ],
        ),
        compiler_params=pltpu.CompilerParams(vmem_limit_bytes=VMEM_BYTES),
        cost_estimate=KERNEL_COST,
    )(ids, extended, consts, *in_stacks, *out_stacks)


def mixer_back(ids, tiled, far, mixed, consts, out_pieces, out_stacks, out_grads, slot_size):
    rows, features = tiled[0].shape
    tile = rows // 2
    shapes = stack_shapes(out_grads)

    def kernel(ids_ref, *refs):
        near_ref, more_ref, final_ref, hidden_ref, c_ref, gated_ref = refs[:6]
        low_ref, high_ref, mixed_ref, const_ref = refs[6:10]
        refs = refs[10:]
        stacks, refs = refs[: len(out_stacks)], refs[len(out_stacks) :]
        grad_hidden, grad_c, grad_mixed, head, sums = refs[:5]
        outs, (out_v, whole, mixed_s, conv_s, sems) = refs[5:-5], refs[-5:]
        i = pl.program_id(0)

        @pl.when(i == 0)
        def _():
            start_loads(ids_ref, stacks, out_pieces, out_v, sems.at[0])
            sums[...] = jnp.zeros(sums.shape, jnp.float32)
            conv_s[tile:] = jnp.zeros((8, features), jnp.float32)

        @pl.when(i > 0)
        def _():
            conv_s[tile:] = conv_s[0:8]

        normed_grad = near_ref[...].astype(jnp.float32) + more_ref[...].astype(jnp.float32)
        normed_grad += jnp.where(i == 0, high_ref[...].astype(jnp.float32), low_ref[...].astype(jnp.float32))
        h = hidden_ref[...]
        scale = lax.rsqrt(jnp.mean(h * h, axis=1, keepdims=True) + norm_eps)
        weighted = normed_grad * const_ref[1:2]
        inner = jnp.mean(weighted * h, axis=1, keepdims=True)
        sums[1:2] += jnp.sum(normed_grad * h * scale, axis=0, keepdims=True)
        total = final_ref[...].astype(jnp.float32) + scale * weighted - h * (scale * scale * scale * inner)
        grad_hidden[...] = total
        branch = total.astype(jnp.bfloat16)
        outer = outer_sum(gated_ref[...], branch)

        @pl.when(i == 0)
        def _():
            wait_whole(out_v, sems.at[0])

        grad_gated = against(branch, out_v[...])
        at = pl.multiple_of((1 - i) * tile, HALO)
        mixed_s[...] = mixed_ref[pl.ds(at, HALO + tile)].astype(jnp.float32)
        conv = sum(
            const_ref[2 + k : 3 + k] * mixed_s[HALO - 2 + k : HALO - 2 + k + tile] for k in range(3)
        )
        grad_c[...] = (grad_gated * conv).astype(jnp.bfloat16)
        grad_conv = grad_gated * c_ref[...].astype(jnp.float32)
        conv_s[0:tile] = grad_conv
        for k in range(3):
            sums[2 + k : 3 + k] += jnp.sum(
                grad_conv * mixed_s[HALO - 2 + k : HALO - 2 + k + tile], axis=0, keepdims=True
            )
        grad_mixed[...] = sum(const_ref[2 + k : 3 + k] * conv_s[2 - k : 2 - k + tile] for k in range(3))

        @pl.when(i == 1)
        def _():
            live = jnp.where(lax.rem(ids_ref[1] * rows, slot_size) > 0, 1.0, 0.0)
            head[...] = jnp.zeros(head.shape, jnp.float32)
            head[0:1] = live * const_ref[2:3] * conv_s[0:1]
            head[1:2] = live * (const_ref[2:3] * conv_s[1:2] + const_ref[3:4] * conv_s[0:1])
            out_v[...] = (whole[...] + outer).astype(jnp.bfloat16)
            start_stores(ids_ref, out_v, out_grads, outs, sems.at[0])
            wait_whole(out_v, sems.at[0])

        @pl.when(i == 0)
        def _():
            whole[...] = outer

    f32, bf16 = jnp.float32, jnp.bfloat16
    part = pl.BlockSpec((tile, features), lambda i, ids: (1 - i, 0))
    once = pl.BlockSpec((8, features), lambda i, ids: (0, 0))
    parts = pl.pallas_call(
        kernel,
        out_shape=[jax.ShapeDtypeStruct((rows, features), t) for t in (f32, bf16, f32)]
        + [jax.ShapeDtypeStruct((8, features), f32)] * 2
        + shapes,
        grid_spec=pltpu.PrefetchScalarGridSpec(
            num_scalar_prefetch=1,
            grid=(2,),
            in_specs=[part] * 6
            + [pl.BlockSpec((tile, features), lambda i, ids: (0, 0))] * 2
            + [pl.BlockSpec((rows + HALO, features), lambda i, ids: (0, 0)), once]
            + [pl.BlockSpec(memory_space=pl.ANY)] * len(out_stacks),
            out_specs=[part] * 3 + [once] * 2 + [pl.BlockSpec(memory_space=pl.ANY)] * len(shapes),
            scratch_shapes=[
                pltpu.VMEM((features, features), bf16),
                pltpu.VMEM((features, features), f32),
                pltpu.VMEM((tile + HALO, features), f32),
                pltpu.VMEM((tile + 8, features), f32),
                pltpu.SemaphoreType.DMA((1,)),
            ],
        ),
        compiler_params=pltpu.CompilerParams(vmem_limit_bytes=VMEM_BYTES),
        cost_estimate=KERNEL_COST,
    )(ids, *tiled, *far, mixed, consts, *out_stacks)
    return [*parts[:5], paired(parts[5:])]


def projection_gradient(ids, normed, grad_mixed, returned, grad_c, b_part, x_part, pieces):
    rows, features = normed.shape
    tile = features // 4
    shapes = stack_shapes(pieces)

    def kernel(ids_ref, normed_ref, mixed_ref, back_ref, c_ref, b_ref, x_ref, proj, *refs):
        outs, (whole, mixed_s, sems) = refs[:-3], refs[-3:]
        i = pl.program_id(0)

        @pl.when(i == 0)
        def _():
            mixed_s[...] = mixed_ref[...]
            mixed_s[rows - 2 :] += back_ref[0:2]
            grad = mixed_s[...]
            proj[:, :features] = (grad * x_ref[...].astype(jnp.float32)).astype(jnp.bfloat16)
            proj[:, features : 2 * features] = c_ref[...]
            proj[:, 2 * features :] = (grad * b_ref[...].astype(jnp.float32)).astype(jnp.bfloat16)

        whole[pl.ds(pl.multiple_of(i * tile, tile), tile)] = outer_sum(
            normed_ref[...], proj[...]
        ).astype(jnp.bfloat16)

        @pl.when(i == 3)
        def _():
            start_stores(ids_ref, whole, pieces, outs, sems.at[0])
            wait_whole(whole, sems.at[0])

    def same(n, width):
        return pl.BlockSpec((n, width), lambda i, ids: (0, 0))

    parts = pl.pallas_call(
        kernel,
        out_shape=[jax.ShapeDtypeStruct((rows, 3 * features), jnp.bfloat16), *shapes],
        grid_spec=pltpu.PrefetchScalarGridSpec(
            num_scalar_prefetch=1,
            grid=(4,),
            in_specs=[
                pl.BlockSpec((rows, tile), lambda i, ids: (0, i)),
                same(rows, features),
                same(8, features),
                same(rows, features),
                same(rows, features),
                same(rows, features),
            ],
            out_specs=[same(rows, 3 * features)] + [pl.BlockSpec(memory_space=pl.ANY)] * len(shapes),
            scratch_shapes=[
                pltpu.VMEM((features, 3 * features), jnp.bfloat16),
                pltpu.VMEM((rows, features), jnp.float32),
                pltpu.SemaphoreType.DMA((1,)),
            ],
        ),
        compiler_params=pltpu.CompilerParams(vmem_limit_bytes=VMEM_BYTES),
        cost_estimate=KERNEL_COST,
    )(ids, normed, grad_mixed, returned, grad_c, b_part, x_part)
    return parts[0], paired(parts[1:])


def mixer_first(ids, proj, tokens, grad_hidden, sums, consts, in_pieces, in_stacks):
    rows, features = tokens.shape
    tile = rows // 2

    def kernel(ids_ref, proj_ref, x_ref, hidden_ref, sums_ref, const_ref, *refs):
        stacks, (grad_tokens, sums_out, in_v, sems) = refs[:-4], refs[-4:]

        @pl.when(pl.program_id(0) == 0)
        def _():
            start_loads(ids_ref, stacks, in_pieces, in_v, sems.at[0])
            sums_out[...] = sums_ref[...]
            wait_whole(in_v, sems.at[0])

        normed_grad = against(proj_ref[...], in_v[...])
        x = x_ref[...].astype(jnp.float32)
        scale = lax.rsqrt(jnp.mean(x * x, axis=1, keepdims=True) + norm_eps)
        weighted = normed_grad * const_ref[0:1]
        inner = jnp.mean(weighted * x, axis=1, keepdims=True)
        sums_out[0:1] += jnp.sum(normed_grad * x * scale, axis=0, keepdims=True)
        grad_tokens[...] = (
            hidden_ref[...] + scale * weighted - x * (scale * scale * scale * inner)
        ).astype(jnp.bfloat16)

    part = pl.BlockSpec((tile, features), lambda i, ids: (i, 0))
    once = pl.BlockSpec((8, features), lambda i, ids: (0, 0))
    return pl.pallas_call(
        kernel,
        out_shape=[
            jax.ShapeDtypeStruct((rows, features), jnp.bfloat16),
            jax.ShapeDtypeStruct((8, features), jnp.float32),
        ],
        grid_spec=pltpu.PrefetchScalarGridSpec(
            num_scalar_prefetch=1,
            grid=(2,),
            in_specs=[pl.BlockSpec((tile, 3 * features), lambda i, ids: (i, 0)), part, part, once, once]
            + [pl.BlockSpec(memory_space=pl.ANY)] * len(in_stacks),
            out_specs=[part, once],
            scratch_shapes=[
                pltpu.VMEM((features, 3 * features), jnp.bfloat16),
                pltpu.SemaphoreType.DMA((1,)),
            ],
        ),
        compiler_params=pltpu.CompilerParams(vmem_limit_bytes=VMEM_BYTES),
        cost_estimate=KERNEL_COST,
    )(ids, proj, tokens, grad_hidden, sums, consts, *in_stacks)


def bits_below(count):
    return [1 << i for i in range(count.bit_length() - 1)]


def per_device(
    tokens,
    mixer_gain,
    in_weight,
    conv_weight,
    out_weight,
    feed_gain,
    gate_weight,
    up_weight,
    down_weight,
    lengths,
    cotangent,
):
    n_dp, n_seq = lax.axis_size("dp"), lax.axis_size("seq")
    tok_rows, features = tokens.shape
    slot_size = min(SLOT_MAX, tok_rows * n_seq)
    own_dp, own_seq = lax.axis_index("dp"), lax.axis_index("seq")
    ids = jnp.stack([own_dp, own_seq]).astype(jnp.int32)

    seq_bits = bits_below(n_seq)
    along_y = seq_bits[: len(seq_bits) // 2]
    ys = [("seq", b) for b in reversed(along_y)]
    zs = [("seq", b) for b in reversed(seq_bits[len(along_y) :])]
    core = [("dp", 1)]
    xs = [("dp", b) for b in reversed(bits_below(n_dp)[1:])]
    in_orders = [zs + xs + ys + core, zs[::-1] + ys + xs + core]
    out_order = zs[:1] + xs + ys + zs[1:] + core
    far_order, near_order = zs[:1] + ys + zs[1:], zs + ys
    token_order = xs + core

    position = own_seq * tok_rows + jnp.arange(tok_rows, dtype=jnp.int32)
    in_slot = position % slot_size
    slot_index = position // slot_size
    slot_ids = jnp.arange(lengths.shape[1], dtype=jnp.int32)
    slot_length = jnp.sum(
        jnp.where(slot_index[:, None] == slot_ids[None, :], lengths[0][None, :], 0), axis=1
    )
    live_mask = (in_slot < slot_length).astype(jnp.float32)[:, None]

    in_rows, in_cols = in_weight.shape
    out_rows, out_cols = out_weight.shape
    in_cut = (in_cols // 128 + 1) // 2 * 128
    in_cuts = [0, in_cut, in_cols]
    third = in_cols // 3
    small_cols = mixer_gain.shape[0]
    small = jnp.concatenate([mixer_gain[None], feed_gain[None], conv_weight], axis=0)
    small = jnp.pad(small, ((0, SMALL_ROWS - small.shape[0]), (0, -small_cols % 128)))
    small_order = zs + ys
    mixer = [in_weight[None, :, :in_cut], in_weight[None, :, in_cut:], out_weight[None]]
    orders = [*in_orders, out_order]
    hidden_units = gate_weight.shape[1]
    gate_rows = gate_weight.shape[0]
    down_rows, down_cols = down_weight.shape
    ratio = n_seq // n_dp
    turned = [(e % 2) * (n_dp // 2) + e // 2 for e in range(n_dp)]
    home = [
        (e * n_seq + s, (s // ratio) * n_seq + turned[e] * ratio + s % ratio)
        for e in range(n_dp)
        for s in range(n_seq)
    ]
    cuts = [0, -(-down_rows // 32) * 16, down_rows]

    def gate_view(ref, dp, seq):
        return ref.at[pl.ds(pl.multiple_of(seq * gate_rows, gate_rows), gate_rows)]

    def down_view(cut):
        low, high = cuts[cut], cuts[cut + 1]

        def view(ref, dp, seq):
            row = pl.multiple_of((seq % ratio) * down_rows + low, 16)
            place = seq // ratio
            place = place % (n_dp // 2) * 2 + place // (n_dp // 2)
            col = pl.multiple_of(place * down_cols, down_cols)
            return ref.at[pl.ds(row, high - low), pl.ds(col, down_cols)]

        return view

    gate = [Piece(near_order, gate_weight.shape, gate_view)]
    up = [Piece(far_order, up_weight.shape, gate_view)]
    down = [
        Piece(order, (cuts[i + 1] - cuts[i], down_cols), down_view(i))
        for i, order in enumerate((near_order, far_order))
    ]

    def with_core(blocks):
        return blocks + [swap(v, core[0]) for v in blocks]

    grad_final = (live_mask * cotangent.astype(jnp.float32)).astype(jnp.bfloat16)
    middle = len(orders[0]) // 2
    z_first, last = 1, len(zs) + len(ys) - 1
    mixer = [gather_steps(v, order[:1]) for v, order in zip(mixer, orders)]
    mixer, small, tokens = tie(mixer, small, tokens)
    mixer = [gather_steps(v, order[1:middle]) for v, order in zip(mixer, orders)]
    before = lax.ppermute(
        tokens[tok_rows - HALO :], "seq", [(i, i + 1) for i in range(n_seq - 1)]
    )
    small = gather_steps(small[None], small_order)
    mixer, gate_weight, up_weight = tie(mixer, gate_weight, up_weight)
    mixer = [gather_steps(v, order[middle:-1]) for v, order in zip(mixer, orders)]
    gate_up = [
        gather_steps(v[None], p.steps[:z_first])
        for v, p in zip((gate_weight, up_weight), (*gate, *up))
    ]
    extended = jnp.concatenate([before, tokens], axis=0)
    places = jnp.stack([jnp.int32(masks_at(p, small_order)[1]) for p in range(n_seq)])
    chosen = (own_seq ^ jnp.arange(n_seq))[:, None] == places[None]
    consts = jnp.einsum(
        "sp,pkc->ksc",
        chosen.astype(jnp.bfloat16),
        small[:, :8, :small_cols],
        preferred_element_type=jnp.float32,
    ).reshape(8, features)
    mixer, gate_up, consts, extended, down_weight, grad_final = tie(
        mixer, gate_up, consts, extended, down_weight, grad_final
    )
    stacks = [last_step(v, order[-1]) for v, order in zip(mixer, orders)]
    stacks, gate_up, down_weight, grad_final = tie(stacks, gate_up, down_weight, grad_final)

    def in_view(low, high):

        def view(ref, dp, seq):
            row = pl.multiple_of(seq * in_rows, in_rows)
            col = pl.multiple_of(dp * in_cols + low, 128)
            return ref.at[pl.ds(row, in_rows), pl.ds(col, high - low)]

        return view

    def out_view(ref, dp, seq):
        return tile_of(ref, seq, out_rows, dp, out_cols)

    in_pieces = [
        Piece(order, (in_rows, in_cuts[i + 1] - in_cuts[i]), in_view(in_cuts[i], in_cuts[i + 1]))
        for i, order in enumerate(in_orders)
    ]
    half_block = gate_rows // 2

    def half_view(low):
        def view(ref, dp, seq):
            row = pl.multiple_of(seq * gate_rows + low, half_block)
            return ref.at[pl.ds(row, half_block)]

        return view

    feed_grads = [
        Piece(order, (half_block, hidden_units), half_view(low))
        for order, low in ((near_order, 0), (far_order, half_block))
    ]
    in_grads = [
        Piece(order, (in_rows, third), in_view(i * third, (i + 1) * third))
        for i, order in enumerate((in_orders[0], ys + zs + xs + core, out_order))
    ]
    out_grads = [Piece(zs + xs + ys + core, out_weight.shape, out_view)]
    out_pieces = [Piece(out_order, out_weight.shape, out_view)]
    in_stacks, out_stacks = stacks[0] + stacks[1], stacks[2]

    gate_up = [gather_steps(v, p.steps[z_first:last]) for v, p in zip(gate_up, (*gate, *up))]
    down_shard = lax.ppermute(down_weight, ("dp", "seq"), home)
    final_there = dp_gather(grad_final, xs)[1:]
    final_near = swap(grad_final, core[0])
    forward = mixer_forward(
        ids, extended, consts, in_pieces, in_stacks, out_pieces, out_stacks, slot_size
    )
    forward, gate_up, down_shard, grad_final, final_near, final_there = tie(
        forward, gate_up, down_shard, grad_final, final_near, final_there
    )
    normed_one, b_part, c_part, x_part, mixed, gated, hidden, normed_two = forward

    wide = (features, hidden_units)
    gate_stacks, up_stacks = [last_step(v, p.steps[-1]) for v, p in zip(gate_up, (*gate, *up))]
    down_stack = gather_steps(down_shard[None], near_order[:z_first])
    normed_there = dp_gather(normed_two, xs)[1:]
    final_blocks = [grad_final, final_near] + with_core(final_there)
    normed_two, normed_there, gate_stacks, up_stacks, down_stack, final_blocks = tie(
        normed_two, normed_there, gate_stacks, up_stacks, down_stack, final_blocks
    )
    downs = [down_stack[:, a:b] for a, b in zip(cuts, cuts[1:])]
    normed_blocks = with_core([normed_two]) + with_core(normed_there)
    normed_blocks, downs, gate_stacks, up_stacks = tie(normed_blocks, downs, gate_stacks, up_stacks)
    downs = [gather_steps(v, p.steps[z_first:last]) for v, p in zip(downs, down)]
    activated, slope, silu, normed_all = feed_up(ids, normed_blocks, gate, gate_stacks, up, up_stacks, wide)
    activated, downs = tie(activated, downs)
    down_stacks = [v for stack, p in zip(downs, down) for v in last_step(stack, p.steps[-1])]
    down_parts = weight_gradient(ids, [activated], final_blocks, down)
    down_parts, down_stacks = tie(down_parts, down_stacks)

    def sent(parts, pieces, place):
        return [exchanged(v, p.steps[place]) for v, p in zip(parts, pieces)]

    def fold_all(parts):
        return [folded(v) for v in parts]

    def sent_on(parts, pieces):
        count = len(pieces[0].steps)
        for place in range(count - 2, 0, -1):
            parts = sent(fold_all(parts) if place < count - 2 else parts, pieces, place)
        return parts

    def joined(parts):
        return [tuple(jnp.concatenate(v, axis=1) for v in zip(*parts))]

    def core_halves(v):
        near, far = v[:2], v[2:]
        half = len(far) // 2
        return near[0], near[1], far[:half], far[half:]

    def far_added(keep, come):
        return [
            (a.astype(jnp.float32) + b.astype(jnp.float32)).astype(jnp.bfloat16)
            for a, b in zip(keep, come)
        ]

    down_parts = sent(down_parts, down, -1)
    grad_gate, grad_up, *back = feed_back(
        ids, final_blocks, activated, slope, silu, gate, gate_stacks, up, up_stacks, down, down_stacks, wide
    )
    back, feed = back[:n_dp], back[n_dp:]
    back, feed, grad_gate, grad_up, down_parts = tie(back, feed, grad_gate, grad_up, down_parts)
    near, near_send, far, far_send = core_halves(back)
    far_come = [swap(v, core[0]) for v in far_send]
    down_parts = sent_on(fold_all(down_parts), down)
    far, far_come, near, near_send, grad_gate, grad_up, feed, down_parts = tie(
        far, far_come, near, near_send, grad_gate, grad_up, feed, down_parts
    )
    far = far_added(far, far_come)
    half_rows = tok_rows // 2
    far_low, far_high = [v[:half_rows] for v in far], [v[half_rows:] for v in far]
    down_parts = joined(fold_all(down_parts))
    far_low, far_high, down_parts, near, near_send, grad_gate, grad_up, feed = tie(
        far_low, far_high, down_parts, near, near_send, grad_gate, grad_up, feed
    )
    far_low = dp_scatter([None] + far_low, xs)
    near_more = swap(near_send, core[0])
    down_parts = sent(down_parts, down, 0)
    gate_parts = weight_gradient(ids, [normed_all], [grad_gate], feed_grads)
    gate_parts, far_low, far_high, grad_up, near, near_more, down_parts, feed = tie(
        gate_parts, far_low, far_high, grad_up, near, near_more, down_parts, feed
    )
    own_down = folded(down_parts[0]).astype(jnp.bfloat16)
    feed_near, feed_send, feed_far, feed_come = core_halves(feed)
    own_down, gate_parts, feed_far, feed_come, grad_up, far_low, far_high = tie(
        own_down, gate_parts, feed_far, feed_come, grad_up, far_low, far_high
    )
    far_high = dp_scatter([None] + far_high, xs)
    gate_parts = sent(gate_parts, feed_grads, -1)
    feed_come = [swap(v, core[0]) for v in feed_come]
    up_parts = weight_gradient(ids, [normed_all], [grad_up], feed_grads)
    up_parts, far_low, far_high, gate_parts, feed_far, feed_come, own_down = tie(
        up_parts, far_low, far_high, gate_parts, feed_far, feed_come, own_down
    )

    feed_far = far_added(feed_far, feed_come)
    feed_low, feed_high = [v[:half_rows] for v in feed_far], [v[half_rows:] for v in feed_far]
    feed_low, feed_high, up_parts, gate_parts, far_low, far_high, own_down = tie(
        feed_low, feed_high, up_parts, gate_parts, far_low, far_high, own_down
    )
    up_parts = sent(up_parts, feed_grads, -1)
    feed_low = dp_scatter([None] + feed_low, xs)
    own_down = lax.ppermute(own_down, ("dp", "seq"), [(b, a) for a, b in home])
    grad_hidden, grad_c, grad_mixed, first_rows, sums, out_parts = mixer_back(
        ids,
        [near, near_more, grad_final, hidden, c_part, gated],
        far_low + far_high,
        mixed,
        consts,
        out_pieces,
        out_stacks,
        out_grads,
        slot_size,
    )
    out_parts, grad_mixed, first_rows, gate_parts, up_parts, feed_low, feed_high, own_down = tie(
        out_parts, grad_mixed, first_rows, gate_parts, up_parts, feed_low, feed_high, own_down
    )
    returned = lax.ppermute(first_rows, "seq", [(i + 1, i) for i in range(n_seq - 1)])
    out_parts = fold_all(sent(out_parts, out_grads, -1))
    gate_parts, up_parts = fold_all(gate_parts), fold_all(up_parts)
    returned, out_parts, up_parts, gate_parts, feed_high = tie(
        returned, out_parts, up_parts, gate_parts, feed_high
    )
    gate_parts = sent_on(gate_parts, feed_grads)
    up_parts = sent_on(up_parts, feed_grads)
    feed_high = dp_scatter([None] + feed_high, xs)
    grad_proj, in_parts = projection_gradient(
        ids, normed_one, grad_mixed, returned, grad_c, b_part, x_part, in_grads
    )
    in_parts, up_parts, gate_parts, grad_proj, out_parts, feed_high = tie(
        in_parts, up_parts, gate_parts, grad_proj, out_parts, feed_high
    )
    gate_parts = joined(fold_all(gate_parts))
    in_parts, gate_parts, out_parts, grad_proj = tie(in_parts, gate_parts, out_parts, grad_proj)
    in_parts = sent(in_parts, in_grads, -1)
    out_parts = sent(out_parts, out_grads, -2)
    gate_parts = sent(gate_parts, feed_grads, 0)
    grad_tokens, sums = mixer_first(ids, grad_proj, tokens, grad_hidden, sums, consts, in_pieces, in_stacks)
    in_parts, out_parts, sums, gate_parts, up_parts, feed_send = tie(
        in_parts, out_parts, sums, gate_parts, up_parts, feed_send
    )
    sum_steps = core + ys + xs + zs[::-1]
    for step in sum_steps[:1]:
        sums = sums + swap(sums, step)
    in_parts, out_parts, up_parts = fold_all(in_parts), fold_all(out_parts), joined(fold_all(up_parts))
    in_parts, out_parts, up_parts, sums = tie(in_parts, out_parts, up_parts, sums)
    in_parts = sent(in_parts, in_grads, -2)
    sums = (sums, swap(sums, sum_steps[1]))
    in_parts, out_parts, up_parts, sums, feed_send = tie(in_parts, out_parts, up_parts, sums, feed_send)
    in_parts, sums = fold_all(in_parts), sums[0] + sums[1]
    in_parts, out_parts, up_parts, sums = tie(in_parts, out_parts, up_parts, sums)
    in_parts = sent(in_parts, in_grads, -3)
    out_parts = sent(out_parts, out_grads, -3)
    up_parts = sent(up_parts, feed_grads, 0)
    sums = (sums, swap(sums, sum_steps[2]))
    in_parts, out_parts, up_parts, sums, feed_send = tie(in_parts, out_parts, up_parts, sums, feed_send)
    in_parts, out_parts, sums = fold_all(in_parts), fold_all(out_parts), sums[0] + sums[1]
    in_parts, out_parts, sums = tie(in_parts, out_parts, sums)
    in_parts = sent(in_parts, in_grads, -4)
    out_parts = sent(out_parts, out_grads, -4)
    sums = (sums, swap(sums, sum_steps[3]))
    feed_more = swap(feed_send, core[0])
    in_parts, out_parts, sums, feed_more, own_down = tie(in_parts, out_parts, sums, feed_more, own_down)
    sums = sums[0] + sums[1]
    for step in sum_steps[4:]:
        sums = sums + swap(sums, step)
    own_down = own_down.astype(jnp.float32)

    def rest(parts, piece, done):
        parts = folded(parts)
        for place in range(len(piece.steps) - done - 1, -1, -1):
            parts = folded(exchanged(parts, piece.steps[place]))
        return parts

    own_in = [rest(v, p, 4) for v, p in zip(in_parts, in_grads)]
    own_in = jnp.concatenate(own_in, axis=1)
    own_out = rest(out_parts[0], out_grads[0], 4)
    own_gate = folded(gate_parts[0])
    own_up = folded(up_parts[0])
    own_sums = lax.dynamic_slice(sums, (0, own_seq * small_cols), (8, small_cols))
    feed_out = jnp.concatenate(feed_low + feed_high, axis=0).astype(jnp.float32)
    feed_out = feed_out + feed_near.astype(jnp.float32) + feed_more.astype(jnp.float32)
    output = (live_mask * (hidden + feed_out)).astype(jnp.bfloat16)
    return (
        output,
        grad_tokens,
        own_sums[0],
        own_in,
        own_sums[2:5],
        own_out,
        own_sums[1],
        own_gate,
        own_up,
        own_down,
    )


def solution(mesh):
    in_specs = (
        P(("dp", "seq"), None),
        P("seq"),
        P("seq", "dp"),
        P(None, "seq"),
        P("seq", "dp"),
        P("seq"),
        P("seq", "dp"),
        P("seq", "dp"),
        P("seq", "dp"),
        P("dp", None),
        P(("dp", "seq"), None),
    )
    out_specs = (
        P(("dp", "seq"), None),
        P(("dp", "seq"), None),
        P("seq"),
        P("seq", "dp"),
        P(None, "seq"),
        P("seq", "dp"),
        P("seq"),
        P("seq", "dp"),
        P("seq", "dp"),
        P("seq", "dp"),
    )
    return jax.shard_map(
        per_device, mesh=mesh, in_specs=in_specs, out_specs=out_specs, check_vma=False
    )
```

```python
from typing import NamedTuple

import jax
import jax.numpy as jnp
from jax import lax
from jax.experimental import pallas as pl
from jax.experimental.pallas import tpu as pltpu
from jax.sharding import PartitionSpec as P

SLOT_MAX = 8192
HALO = 16
SMALL_ROWS = 16
VMEM_BYTES = 56 << 20
TILE = 256
KERNEL_COST = pl.CostEstimate(flops=1 << 36, bytes_accessed=1 << 20, transcendentals=0)

norm_eps = 1e-05


def multiply(left_side, right_side):
    return jnp.dot(left_side, right_side, preferred_element_type=jnp.float32)


def against(left_side, right_side):
    return lax.dot_general(
        left_side, right_side, (((1,), (1,)), ((), ())), preferred_element_type=jnp.float32
    )


def outer_sum(left_side, right_side):
    return lax.dot_general(
        left_side, right_side, (((0,), (0,)), ((), ())), preferred_element_type=jnp.float32
    )


def tie(*values):
    return lax.optimization_barrier(values)


def swap(shard, step):
    axis, bit = step
    count = lax.axis_size(axis)
    return lax.ppermute(shard, axis, [(i, i ^ bit) for i in range(count)])


def gather_steps(stack, steps):
    for step in steps:
        stack = jnp.concatenate([stack, swap(stack, step)], axis=0)
    return stack


def last_step(stack, step):
    return [stack, swap(stack, step)]


def exchanged(parts, step):
    keep, send = parts
    return keep, swap(send, step)


def folded(parts):
    keep, come = parts
    total = keep.astype(jnp.float32) + come.astype(jnp.float32)
    half = total.shape[0] // 2
    if not half:
        return total[0]
    return total[:half].astype(jnp.bfloat16), total[half:].astype(jnp.bfloat16)


def masks_at(position, steps):
    masks = {"dp": 0, "seq": 0}
    for place, (axis, bit) in enumerate(steps):
        masks[axis] = masks[axis] + ((position >> place) & 1) * bit
    return masks["dp"], masks["seq"]


def tile_of(ref, row, rows, col, cols):
    return ref.at[pl.ds(pl.multiple_of(row * rows, rows), rows), pl.ds(pl.multiple_of(col * cols, cols), cols)]


def dp_gather(block, steps):
    blocks = [block]
    for step in steps:
        blocks = blocks + [swap(b, step) for b in blocks]
    return blocks


def dp_scatter(parts, steps):
    for step in reversed(steps):
        half = len(parts) // 2
        moved = [swap(send.astype(jnp.bfloat16), step) for send in parts[half:]]
        parts = [
            new if keep is None else keep.astype(jnp.float32) + new.astype(jnp.float32)
            for keep, new in zip(parts[:half], moved)
        ]
    return parts


class Piece(NamedTuple):
    steps: list
    block: tuple
    view: object


def start_loads(ids_ref, refs, pieces, into, sem):
    for place, piece in enumerate(pieces):
        first = 0
        for part in refs[2 * place : 2 * place + 2]:

            def start(position, carry, part=part, first=first, piece=piece):
                mask_dp, mask_seq = masks_at(position + first, piece.steps)
                pltpu.make_async_copy(
                    part.at[position],
                    piece.view(into, ids_ref[0] ^ mask_dp, ids_ref[1] ^ mask_seq),
                    sem,
                ).start()
                return carry

            lax.fori_loop(0, part.shape[0], start, 0)
            first += part.shape[0]


def start_stores(ids_ref, whole, pieces, outs, sem):
    each = len(outs) // len(pieces)
    for place, piece in enumerate(pieces):
        size = 2 ** len(piece.steps) // each
        for part in range(each):

            def start(position, carry, first=part * size, out=outs[each * place + part], piece=piece):
                mask_dp, mask_seq = masks_at(position + first, piece.steps)
                source = piece.view(whole, ids_ref[0] ^ mask_dp, ids_ref[1] ^ mask_seq)
                pltpu.make_async_copy(source, out.at[position], sem).start()
                return carry

            lax.fori_loop(0, size, start, 0)


def start_row_stores(ids_ref, whole, pieces, outs, sem, first, count):
    each = len(outs) // len(pieces)
    for step in range(count):
        seq = first + step
        mask = seq ^ ids_ref[1]
        for place, piece in enumerate(pieces):
            size = 2 ** len(piece.steps) // each
            position = sum(
                ((mask >> (bit.bit_length() - 1)) & 1) << at for at, (_, bit) in enumerate(piece.steps)
            )
            for part in range(each):

                @pl.when(jnp.logical_and(position >= part * size, position < (part + 1) * size))
                def _(part=part, position=position, seq=seq, piece=piece, place=place, size=size):
                    pltpu.make_async_copy(
                        piece.view(whole, ids_ref[0], seq),
                        outs[each * place + part].at[position - part * size],
                        sem,
                    ).start()


def wait_whole(ref, sem):
    pltpu.make_async_copy(ref, ref, sem).wait()


def fetch_block(blocks, buffers, sems):
    i = pl.program_id(0)

    rows = buffers.shape[1]

    def copy(place):
        slot = place % 2
        source = blocks[place // 2].at[pl.ds(place % 2 * rows, rows)]
        return pltpu.make_async_copy(source, buffers.at[slot], sems.at[slot])

    for place in range(2 * len(blocks)):

        @pl.when(i == place)
        def _(place=place):
            if place == 0:
                copy(0).start()
            if place + 1 < 2 * len(blocks):
                copy(place + 1).start()
            copy(place).wait()

    return buffers[i % 2]


def token_call(kernel, ids, blocks, tiled, stacks, outs, apart, scratch):
    rows, width = blocks[0].shape
    rows, count, steps = rows // 2, len(blocks), 2 * len(blocks)
    return pl.pallas_call(
        kernel,
        out_shape=[jax.ShapeDtypeStruct((rows * steps, n), t) for n, t in outs]
        + [jax.ShapeDtypeStruct((rows * 2, n), t) for n, t in apart for _ in range(count)],
        grid_spec=pltpu.PrefetchScalarGridSpec(
            num_scalar_prefetch=1,
            grid=(steps,),
            in_specs=[pl.BlockSpec(memory_space=pl.ANY)] * count
            + [pl.BlockSpec((rows, v.shape[1]), lambda i, ids: (i, 0)) for v in tiled]
            + [pl.BlockSpec(memory_space=pl.ANY)] * len(stacks),
            out_specs=[pl.BlockSpec((rows, n), lambda i, ids: (i, 0)) for n, _ in outs]
            + [pl.BlockSpec(memory_space=pl.ANY)] * (len(apart) * count),
            scratch_shapes=[
                pltpu.VMEM((2, rows, width), jnp.bfloat16),
                pltpu.SemaphoreType.DMA((2,)),
                *scratch,
            ],
        ),
        compiler_params=pltpu.CompilerParams(vmem_limit_bytes=VMEM_BYTES),
        cost_estimate=KERNEL_COST,
    )(ids, *blocks, *tiled, *stacks)


def feed_up(ids, normed, gate, gate_stacks, up, up_stacks, shape):
    count = len(normed)

    def kernel(ids_ref, *refs):
        blocks, stacks, refs = refs[:count], refs[count:-9], refs[-9:]
        act, slope, silu, whole, buffers, block_sems, gate_v, up_v, sems = refs

        @pl.when(pl.program_id(0) == 0)
        def _():
            start_loads(ids_ref, stacks[: 2 * len(gate)], gate, gate_v, sems.at[0])
            start_loads(ids_ref, stacks[2 * len(gate) :], up, up_v, sems.at[1])

        x = fetch_block(blocks, buffers, block_sems)

        @pl.when(pl.program_id(0) == 0)
        def _():
            wait_whole(gate_v, sems.at[0])
            wait_whole(up_v, sems.at[1])

        whole[...] = x
        gate_val = multiply(x, gate_v[...])
        up_val = multiply(x, up_v[...])
        sigmoid = jax.nn.sigmoid(gate_val)
        silu_gate = gate_val * sigmoid
        act[...] = (silu_gate * up_val).astype(jnp.bfloat16)
        slope[...] = (up_val * sigmoid * (1.0 + gate_val * (1.0 - sigmoid))).astype(jnp.bfloat16)
        silu[...] = silu_gate.astype(jnp.bfloat16)

    n = shape[1]
    return token_call(
        kernel,
        ids,
        normed,
        [],
        [*gate_stacks, *up_stacks],
        [(n, jnp.bfloat16)] * 3 + [(shape[0], jnp.bfloat16)],
        [],
        [pltpu.VMEM(shape, jnp.bfloat16)] * 2 + [pltpu.SemaphoreType.DMA((2,))],
    )


def feed_back(ids, final, activated, slope, silu, gate, gate_stacks, up, up_stacks, down, down_stacks, shape):
    count = len(final)
    ends = [2 * len(gate), 2 * len(gate) + 2 * len(up)]

    def kernel(ids_ref, *refs):
        blocks, (act_ref, slope_ref, silu_ref) = refs[:count], refs[count : count + 3]
        parts = 2 * count
        stacks, refs = refs[count + 3 : -10 - parts], refs[-10 - parts :]
        grad_gate, grad_up, buffers, block_sems, gate_v, up_v, down_v, sems = refs[:2] + refs[2 + parts : -2]
        tiles, store_sems = refs[-2:]
        i = pl.program_id(0)
        slot = i % 2
        norm_parts, out_parts = refs[2 : 2 + count], refs[2 + count : 2 + parts]

        @pl.when(pl.program_id(0) == 0)
        def _():
            start_loads(ids_ref, stacks[ends[1] :], down, down_v, sems.at[2])
            start_loads(ids_ref, stacks[: ends[0]], gate, gate_v, sems.at[0])
            start_loads(ids_ref, stacks[ends[0] : ends[1]], up, up_v, sems.at[1])

        f = fetch_block(blocks, buffers, block_sems)

        @pl.when(pl.program_id(0) == 0)
        def _():
            wait_whole(down_v, sems.at[2])
            wait_whole(gate_v, sems.at[0])
            wait_whole(up_v, sems.at[1])

        grad_act = against(f, down_v[...])
        gg = (grad_act * slope_ref[...].astype(jnp.float32)).astype(jnp.bfloat16)
        gu = (grad_act * silu_ref[...].astype(jnp.float32)).astype(jnp.bfloat16)
        grad_gate[...] = gg
        grad_up[...] = gu
        @pl.when(i >= 2)
        def _():
            wait_whole(tiles.at[slot], store_sems.at[slot])

        tiles[slot, 0] = multiply(act_ref[...], down_v[...]).astype(jnp.bfloat16)
        tiles[slot, 1] = (against(gg, gate_v[...]) + against(gu, up_v[...])).astype(jnp.bfloat16)
        rows = tiles.shape[2]
        for place in range(count):

            @pl.when(i // 2 == place)
            def _(place=place):
                at = pl.ds(pl.multiple_of(slot * rows, rows), rows)
                for kind, target in ((0, out_parts[place]), (1, norm_parts[place])):
                    pltpu.make_async_copy(tiles.at[slot, kind], target.at[at], store_sems.at[slot]).start()

        @pl.when(i == 2 * count - 1)
        def _():
            wait_whole(tiles.at[0], store_sems.at[0])
            wait_whole(tiles.at[1], store_sems.at[1])

    features, n = shape
    return token_call(
        kernel,
        ids,
        final,
        [activated, slope, silu],
        [*gate_stacks, *up_stacks, *down_stacks],
        [(n, jnp.bfloat16)] * 2,
        [(features, jnp.bfloat16)] * 2,
        [
            pltpu.VMEM(shape, jnp.bfloat16),
            pltpu.VMEM(shape, jnp.bfloat16),
            pltpu.VMEM((n, features), jnp.bfloat16),
            pltpu.SemaphoreType.DMA((3,)),
            pltpu.VMEM((2, 2, final[0].shape[0] // 2, features), jnp.bfloat16),
            pltpu.SemaphoreType.DMA((2,)),
        ],
    )


def stack_shapes(pieces, each=2):
    shapes = []
    for piece in pieces:
        size = 2 ** len(piece.steps) // each
        shapes += [jax.ShapeDtypeStruct((size, *piece.block), jnp.bfloat16)] * each
    return shapes


def paired(parts, each=2):
    return [tuple(parts[i : i + each]) for i in range(0, len(parts), each)]


def weight_gradient(ids, lefts, rights, pieces, each=2, by_rows=False):
    rows, columns = lefts[0].shape[1], rights[0].shape[1]
    step = min(v.shape[0] for v in (*lefts, *rights))
    tile = next((t for t in (512, 384, 256, 128) if rows % t == 0), rows)
    count = rows // tile
    shapes = stack_shapes(pieces, each)

    def kernel(ids_ref, *refs):
        sides, refs = refs[: len(lefts) + len(rights)], refs[len(lefts) + len(rights) :]
        outs, (whole, sems) = refs[:-2], refs[-2:]
        i = pl.program_id(0)
        left_rows, right_rows = [
            [v[at : at + step] for v in side for at in range(0, v.shape[0], step)]
            for side in (sides[: len(lefts)], sides[len(lefts) :])
        ]
        total = sum(outer_sum(a, b) for a, b in zip(left_rows, right_rows))
        whole[pl.ds(pl.multiple_of(i * tile, tile), tile)] = total.astype(jnp.bfloat16)

        if by_rows:
            seqs = 2 ** len(pieces[0].steps) // count
            start_row_stores(ids_ref, whole, pieces, outs, sems.at[0], i * seqs, seqs)

        @pl.when(i == count - 1)
        def _():
            if not by_rows:
                start_stores(ids_ref, whole, pieces, outs, sems.at[0])
            wait_whole(whole, sems.at[0])

    parts = pl.pallas_call(
        kernel,
        out_shape=shapes,
        grid_spec=pltpu.PrefetchScalarGridSpec(
            num_scalar_prefetch=1,
            grid=(count,),
            in_specs=[
                *(pl.BlockSpec((v.shape[0], tile), lambda i, ids: (0, i)) for v in lefts),
                *(pl.BlockSpec((v.shape[0], columns), lambda i, ids: (0, 0)) for v in rights),
            ],
            out_specs=[pl.BlockSpec(memory_space=pl.ANY)] * len(shapes),
            scratch_shapes=[
                pltpu.VMEM((rows, columns), jnp.bfloat16),
                pltpu.SemaphoreType.DMA((1,)),
            ],
        ),
        compiler_params=pltpu.CompilerParams(vmem_limit_bytes=VMEM_BYTES),
        cost_estimate=KERNEL_COST,
    )(ids, *lefts, *rights)
    return paired(parts, each)


def mixer_forward(ids, extended, consts, in_pieces, in_stacks, out_pieces, out_stacks, slot_size):
    rows, features = extended.shape
    rows = rows - HALO
    tile = rows // 2
    count = len(in_stacks)
    wide = 3 * features

    def kernel(ids_ref, ext_ref, const_ref, *refs):
        stacks, refs = refs[: count + len(out_stacks)], refs[count + len(out_stacks) :]
        normed_one, b_out, c_out, x_out, mixed_out, gated_out, hidden_out, normed_two = refs[:8]
        in_v, out_v, mixed_s, sems = refs[8:]
        i = pl.program_id(0)

        @pl.when(i == 0)
        def _():
            start_loads(ids_ref, stacks[:count], in_pieces, in_v, sems.at[0])
            start_loads(ids_ref, stacks[count:], out_pieces, out_v, sems.at[1])

        at = pl.multiple_of(i * tile, HALO)
        x = ext_ref[pl.ds(at, HALO + tile)].astype(jnp.float32)
        scale = lax.rsqrt(jnp.mean(x * x, axis=1, keepdims=True) + norm_eps)
        normed = (x * scale * const_ref[0:1]).astype(jnp.bfloat16)
        normed_one[...] = normed[HALO:]

        @pl.when(i == 0)
        def _():
            wait_whole(in_v, sems.at[0])
            wait_whole(out_v, sems.at[1])

        b_part = multiply(normed, in_v[:, :features])
        x_part = multiply(normed, in_v[:, 2 * features :])
        b_out[...] = b_part[HALO:].astype(jnp.bfloat16)
        x_out[...] = x_part[HALO:].astype(jnp.bfloat16)
        mixed = (b_part * x_part).astype(jnp.bfloat16)
        mixed_s[...] = mixed.astype(jnp.float32)
        base = lax.rem(ids_ref[1] * rows, slot_size)

        @pl.when(jnp.logical_and(i == 0, base == 0))
        def _():
            mixed_s[0:HALO] = jnp.zeros((HALO, features), jnp.float32)

        mixed_out[pl.ds(at, HALO)] = mixed_s[0:HALO].astype(jnp.bfloat16)
        mixed_out[pl.ds(pl.multiple_of(at + HALO, HALO), tile)] = mixed[HALO:]
        conv = sum(
            const_ref[2 + k : 3 + k] * mixed_s[HALO - 2 + k : HALO - 2 + k + tile] for k in range(3)
        )
        c_part = multiply(normed[HALO:], in_v[:, features : 2 * features])
        c_out[...] = c_part.astype(jnp.bfloat16)
        gated = (c_part * conv).astype(jnp.bfloat16)
        gated_out[...] = gated
        hidden = x[HALO:] + multiply(gated, out_v[...])
        hidden_out[...] = hidden
        scale = lax.rsqrt(jnp.mean(hidden * hidden, axis=1, keepdims=True) + norm_eps)
        normed_two[...] = (hidden * scale * const_ref[1:2]).astype(jnp.bfloat16)

    f32, bf16 = jnp.float32, jnp.bfloat16
    kinds = [bf16, bf16, bf16, bf16, bf16, bf16, f32, bf16]
    shapes = [(rows + (HALO if i == 4 else 0), features) for i in range(8)]
    whole = pl.BlockSpec((rows + HALO, features), lambda i, ids: (0, 0))
    part = pl.BlockSpec((tile, features), lambda i, ids: (i, 0))
    return pl.pallas_call(
        kernel,
        out_shape=[jax.ShapeDtypeStruct(s, t) for s, t in zip(shapes, kinds)],
        grid_spec=pltpu.PrefetchScalarGridSpec(
            num_scalar_prefetch=1,
            grid=(2,),
            in_specs=[whole, pl.BlockSpec(consts.shape, lambda i, ids: (0, 0))]
            + [pl.BlockSpec(memory_space=pl.ANY)] * (count + len(out_stacks)),
            out_specs=[whole if i == 4 else part for i in range(8)],
            scratch_shapes=[
                pltpu.VMEM((features, wide), bf16),
                pltpu.VMEM((features, features), bf16),
                pltpu.VMEM((tile + HALO, features), f32),
                pltpu.SemaphoreType.DMA((2,)),
            ],
        ),
        compiler_params=pltpu.CompilerParams(vmem_limit_bytes=VMEM_BYTES),
        cost_estimate=KERNEL_COST,
    )(ids, extended, consts, *in_stacks, *out_stacks)


def mixer_back(ids, tiled, far, mixed, consts, out_pieces, out_stacks, out_grads, slot_size):
    rows, features = tiled[0].shape
    tile = rows // 2
    shapes = stack_shapes(out_grads)

    def kernel(ids_ref, *refs):
        near_ref, more_ref, final_ref, hidden_ref, c_ref, gated_ref = refs[:6]
        low_ref, high_ref, mixed_ref, const_ref = refs[6:10]
        refs = refs[10:]
        stacks, refs = refs[: len(out_stacks)], refs[len(out_stacks) :]
        grad_hidden, grad_c, grad_mixed, head, sums = refs[:5]
        outs, (out_v, whole, mixed_s, conv_s, sems) = refs[5:-5], refs[-5:]
        i = pl.program_id(0)

        @pl.when(i == 0)
        def _():
            start_loads(ids_ref, stacks, out_pieces, out_v, sems.at[0])
            sums[...] = jnp.zeros(sums.shape, jnp.float32)
            conv_s[tile:] = jnp.zeros((8, features), jnp.float32)

        @pl.when(i > 0)
        def _():
            conv_s[tile:] = conv_s[0:8]

        normed_grad = near_ref[...].astype(jnp.float32) + more_ref[...].astype(jnp.float32)
        normed_grad += jnp.where(i == 0, high_ref[...].astype(jnp.float32), low_ref[...].astype(jnp.float32))
        h = hidden_ref[...]
        scale = lax.rsqrt(jnp.mean(h * h, axis=1, keepdims=True) + norm_eps)
        weighted = normed_grad * const_ref[1:2]
        inner = jnp.mean(weighted * h, axis=1, keepdims=True)
        sums[1:2] += jnp.sum(normed_grad * h * scale, axis=0, keepdims=True)
        total = final_ref[...].astype(jnp.float32) + scale * weighted - h * (scale * scale * scale * inner)
        grad_hidden[...] = total
        branch = total.astype(jnp.bfloat16)
        outer = outer_sum(gated_ref[...], branch)

        @pl.when(i == 0)
        def _():
            wait_whole(out_v, sems.at[0])

        grad_gated = against(branch, out_v[...])
        at = pl.multiple_of((1 - i) * tile, HALO)
        mixed_s[...] = mixed_ref[pl.ds(at, HALO + tile)].astype(jnp.float32)
        conv = sum(
            const_ref[2 + k : 3 + k] * mixed_s[HALO - 2 + k : HALO - 2 + k + tile] for k in range(3)
        )
        grad_c[...] = (grad_gated * conv).astype(jnp.bfloat16)
        grad_conv = grad_gated * c_ref[...].astype(jnp.float32)
        conv_s[0:tile] = grad_conv
        for k in range(3):
            sums[2 + k : 3 + k] += jnp.sum(
                grad_conv * mixed_s[HALO - 2 + k : HALO - 2 + k + tile], axis=0, keepdims=True
            )
        grad_mixed[...] = sum(const_ref[2 + k : 3 + k] * conv_s[2 - k : 2 - k + tile] for k in range(3))

        @pl.when(i == 1)
        def _():
            live = jnp.where(lax.rem(ids_ref[1] * rows, slot_size) > 0, 1.0, 0.0)
            head[...] = jnp.zeros(head.shape, jnp.float32)
            head[0:1] = live * const_ref[2:3] * conv_s[0:1]
            head[1:2] = live * (const_ref[2:3] * conv_s[1:2] + const_ref[3:4] * conv_s[0:1])
            out_v[...] = (whole[...] + outer).astype(jnp.bfloat16)
            start_stores(ids_ref, out_v, out_grads, outs, sems.at[0])
            wait_whole(out_v, sems.at[0])

        @pl.when(i == 0)
        def _():
            whole[...] = outer

    f32, bf16 = jnp.float32, jnp.bfloat16
    part = pl.BlockSpec((tile, features), lambda i, ids: (1 - i, 0))
    once = pl.BlockSpec((8, features), lambda i, ids: (0, 0))
    parts = pl.pallas_call(
        kernel,
        out_shape=[jax.ShapeDtypeStruct((rows, features), t) for t in (f32, bf16, f32)]
        + [jax.ShapeDtypeStruct((8, features), f32)] * 2
        + shapes,
        grid_spec=pltpu.PrefetchScalarGridSpec(
            num_scalar_prefetch=1,
            grid=(2,),
            in_specs=[part] * 6
            + [pl.BlockSpec((tile, features), lambda i, ids: (0, 0))] * 2
            + [pl.BlockSpec((rows + HALO, features), lambda i, ids: (0, 0)), once]
            + [pl.BlockSpec(memory_space=pl.ANY)] * len(out_stacks),
            out_specs=[part] * 3 + [once] * 2 + [pl.BlockSpec(memory_space=pl.ANY)] * len(shapes),
            scratch_shapes=[
                pltpu.VMEM((features, features), bf16),
                pltpu.VMEM((features, features), f32),
                pltpu.VMEM((tile + HALO, features), f32),
                pltpu.VMEM((tile + 8, features), f32),
                pltpu.SemaphoreType.DMA((1,)),
            ],
        ),
        compiler_params=pltpu.CompilerParams(vmem_limit_bytes=VMEM_BYTES),
        cost_estimate=KERNEL_COST,
    )(ids, *tiled, *far, mixed, consts, *out_stacks)
    return [*parts[:5], paired(parts[5:])]


def projection_gradient(ids, normed, grad_mixed, returned, grad_c, b_part, x_part, pieces):
    rows, features = normed.shape
    tile = features // 4
    shapes = stack_shapes(pieces)

    def kernel(ids_ref, normed_ref, mixed_ref, back_ref, c_ref, b_ref, x_ref, proj, *refs):
        outs, (whole, mixed_s, sems) = refs[:-3], refs[-3:]
        i = pl.program_id(0)

        @pl.when(i == 0)
        def _():
            mixed_s[...] = mixed_ref[...]
            mixed_s[rows - 2 :] += back_ref[0:2]
            grad = mixed_s[...]
            proj[:, :features] = (grad * x_ref[...].astype(jnp.float32)).astype(jnp.bfloat16)
            proj[:, features : 2 * features] = c_ref[...]
            proj[:, 2 * features :] = (grad * b_ref[...].astype(jnp.float32)).astype(jnp.bfloat16)

        whole[pl.ds(pl.multiple_of(i * tile, tile), tile)] = outer_sum(
            normed_ref[...], proj[...]
        ).astype(jnp.bfloat16)

        @pl.when(i == 3)
        def _():
            start_stores(ids_ref, whole, pieces, outs, sems.at[0])
            wait_whole(whole, sems.at[0])

    def same(n, width):
        return pl.BlockSpec((n, width), lambda i, ids: (0, 0))

    parts = pl.pallas_call(
        kernel,
        out_shape=[jax.ShapeDtypeStruct((rows, 3 * features), jnp.bfloat16), *shapes],
        grid_spec=pltpu.PrefetchScalarGridSpec(
            num_scalar_prefetch=1,
            grid=(4,),
            in_specs=[
                pl.BlockSpec((rows, tile), lambda i, ids: (0, i)),
                same(rows, features),
                same(8, features),
                same(rows, features),
                same(rows, features),
                same(rows, features),
            ],
            out_specs=[same(rows, 3 * features)] + [pl.BlockSpec(memory_space=pl.ANY)] * len(shapes),
            scratch_shapes=[
                pltpu.VMEM((features, 3 * features), jnp.bfloat16),
                pltpu.VMEM((rows, features), jnp.float32),
                pltpu.SemaphoreType.DMA((1,)),
            ],
        ),
        compiler_params=pltpu.CompilerParams(vmem_limit_bytes=VMEM_BYTES),
        cost_estimate=KERNEL_COST,
    )(ids, normed, grad_mixed, returned, grad_c, b_part, x_part)
    return parts[0], paired(parts[1:])


def mixer_first(ids, proj, tokens, grad_hidden, sums, consts, in_pieces, in_stacks):
    rows, features = tokens.shape
    tile = rows // 2

    def kernel(ids_ref, proj_ref, x_ref, hidden_ref, sums_ref, const_ref, *refs):
        stacks, (grad_tokens, sums_out, in_v, sems) = refs[:-4], refs[-4:]

        @pl.when(pl.program_id(0) == 0)
        def _():
            start_loads(ids_ref, stacks, in_pieces, in_v, sems.at[0])
            sums_out[...] = sums_ref[...]
            wait_whole(in_v, sems.at[0])

        normed_grad = against(proj_ref[...], in_v[...])
        x = x_ref[...].astype(jnp.float32)
        scale = lax.rsqrt(jnp.mean(x * x, axis=1, keepdims=True) + norm_eps)
        weighted = normed_grad * const_ref[0:1]
        inner = jnp.mean(weighted * x, axis=1, keepdims=True)
        sums_out[0:1] += jnp.sum(normed_grad * x * scale, axis=0, keepdims=True)
        grad_tokens[...] = (
            hidden_ref[...] + scale * weighted - x * (scale * scale * scale * inner)
        ).astype(jnp.bfloat16)

    part = pl.BlockSpec((tile, features), lambda i, ids: (i, 0))
    once = pl.BlockSpec((8, features), lambda i, ids: (0, 0))
    return pl.pallas_call(
        kernel,
        out_shape=[
            jax.ShapeDtypeStruct((rows, features), jnp.bfloat16),
            jax.ShapeDtypeStruct((8, features), jnp.float32),
        ],
        grid_spec=pltpu.PrefetchScalarGridSpec(
            num_scalar_prefetch=1,
            grid=(2,),
            in_specs=[pl.BlockSpec((tile, 3 * features), lambda i, ids: (i, 0)), part, part, once, once]
            + [pl.BlockSpec(memory_space=pl.ANY)] * len(in_stacks),
            out_specs=[part, once],
            scratch_shapes=[
                pltpu.VMEM((features, 3 * features), jnp.bfloat16),
                pltpu.SemaphoreType.DMA((1,)),
            ],
        ),
        compiler_params=pltpu.CompilerParams(vmem_limit_bytes=VMEM_BYTES),
        cost_estimate=KERNEL_COST,
    )(ids, proj, tokens, grad_hidden, sums, consts, *in_stacks)


def bits_below(count):
    return [1 << i for i in range(count.bit_length() - 1)]


def per_device(
    tokens,
    mixer_gain,
    in_weight,
    conv_weight,
    out_weight,
    feed_gain,
    gate_weight,
    up_weight,
    down_weight,
    lengths,
    cotangent,
):
    n_dp, n_seq = lax.axis_size("dp"), lax.axis_size("seq")
    tok_rows, features = tokens.shape
    slot_size = min(SLOT_MAX, tok_rows * n_seq)
    own_dp, own_seq = lax.axis_index("dp"), lax.axis_index("seq")
    ids = jnp.stack([own_dp, own_seq]).astype(jnp.int32)

    seq_bits = bits_below(n_seq)
    along_y = seq_bits[: len(seq_bits) // 2]
    ys = [("seq", b) for b in reversed(along_y)]
    zs = [("seq", b) for b in reversed(seq_bits[len(along_y) :])]
    core = [("dp", 1)]
    xs = [("dp", b) for b in reversed(bits_below(n_dp)[1:])]
    in_orders = [zs + xs + ys + core, zs[::-1] + ys + xs + core]
    out_order = zs[:1] + xs + ys + zs[1:] + core
    far_order, near_order = zs[:1] + ys + zs[1:], zs + ys
    token_order = xs + core

    position = own_seq * tok_rows + jnp.arange(tok_rows, dtype=jnp.int32)
    in_slot = position % slot_size
    slot_index = position // slot_size
    slot_ids = jnp.arange(lengths.shape[1], dtype=jnp.int32)
    slot_length = jnp.sum(
        jnp.where(slot_index[:, None] == slot_ids[None, :], lengths[0][None, :], 0), axis=1
    )
    live_mask = (in_slot < slot_length).astype(jnp.float32)[:, None]

    in_rows, in_cols = in_weight.shape
    out_rows, out_cols = out_weight.shape
    in_cut = (in_cols // 128 + 1) // 2 * 128
    in_cuts = [0, in_cut, in_cols]
    third = in_cols // 3
    small_cols = mixer_gain.shape[0]
    small = jnp.concatenate([mixer_gain[None], feed_gain[None], conv_weight], axis=0)
    small = jnp.pad(small, ((0, SMALL_ROWS - small.shape[0]), (0, -small_cols % 128)))
    small_order = zs + ys
    mixer = [in_weight[None, :, :in_cut], in_weight[None, :, in_cut:], out_weight[None]]
    orders = [*in_orders, out_order]
    hidden_units = gate_weight.shape[1]
    gate_rows = gate_weight.shape[0]
    down_rows, down_cols = down_weight.shape
    ratio = n_seq // n_dp
    turned = [(e % 2) * (n_dp // 2) + e // 2 for e in range(n_dp)]
    home = [
        (e * n_seq + s, (s // ratio) * n_seq + turned[e] * ratio + s % ratio)
        for e in range(n_dp)
        for s in range(n_seq)
    ]
    cuts = [0, -(-down_rows // 32) * 16, down_rows]

    def gate_view(ref, dp, seq):
        return ref.at[pl.ds(pl.multiple_of(seq * gate_rows, gate_rows), gate_rows)]

    def down_view(cut):
        low, high = cuts[cut], cuts[cut + 1]

        def view(ref, dp, seq):
            row = pl.multiple_of((seq % ratio) * down_rows + low, 16)
            place = seq // ratio
            place = place % (n_dp // 2) * 2 + place // (n_dp // 2)
            col = pl.multiple_of(place * down_cols, down_cols)
            return ref.at[pl.ds(row, high - low), pl.ds(col, down_cols)]

        return view

    gate = [Piece(near_order, gate_weight.shape, gate_view)]
    up = [Piece(far_order, up_weight.shape, gate_view)]
    down = [
        Piece(order, (cuts[i + 1] - cuts[i], down_cols), down_view(i))
        for i, order in enumerate((near_order, far_order))
    ]

    def with_core(blocks):
        return blocks + [swap(v, core[0]) for v in blocks]

    grad_final = (live_mask * cotangent.astype(jnp.float32)).astype(jnp.bfloat16)
    middle = len(orders[0]) // 2
    z_first, last = 1, len(zs) + len(ys) - 1
    mixer = [gather_steps(v, order[:1]) for v, order in zip(mixer, orders)]
    mixer, small, tokens = tie(mixer, small, tokens)
    mixer = [gather_steps(v, order[1:middle]) for v, order in zip(mixer, orders)]
    before = lax.ppermute(
        tokens[tok_rows - HALO :], "seq", [(i, i + 1) for i in range(n_seq - 1)]
    )
    small = gather_steps(small[None], small_order)
    mixer, gate_weight, up_weight = tie(mixer, gate_weight, up_weight)
    mixer = [gather_steps(v, order[middle:-1]) for v, order in zip(mixer, orders)]
    gate_up = [
        gather_steps(v[None], p.steps[:z_first])
        for v, p in zip((gate_weight, up_weight), (*gate, *up))
    ]
    extended = jnp.concatenate([before, tokens], axis=0)
    places = jnp.stack([jnp.int32(masks_at(p, small_order)[1]) for p in range(n_seq)])
    chosen = (own_seq ^ jnp.arange(n_seq))[:, None] == places[None]
    consts = jnp.einsum(
        "sp,pkc->ksc",
        chosen.astype(jnp.bfloat16),
        small[:, :8, :small_cols],
        preferred_element_type=jnp.float32,
    ).reshape(8, features)
    mixer, gate_up, consts, extended, down_weight, grad_final = tie(
        mixer, gate_up, consts, extended, down_weight, grad_final
    )
    stacks = [last_step(v, order[-1]) for v, order in zip(mixer, orders)]
    stacks, gate_up, down_weight, grad_final = tie(stacks, gate_up, down_weight, grad_final)

    def in_view(low, high):

        def view(ref, dp, seq):
            row = pl.multiple_of(seq * in_rows, in_rows)
            col = pl.multiple_of(dp * in_cols + low, 128)
            return ref.at[pl.ds(row, in_rows), pl.ds(col, high - low)]

        return view

    def out_view(ref, dp, seq):
        return tile_of(ref, seq, out_rows, dp, out_cols)

    in_pieces = [
        Piece(order, (in_rows, in_cuts[i + 1] - in_cuts[i]), in_view(in_cuts[i], in_cuts[i + 1]))
        for i, order in enumerate(in_orders)
    ]
    half_block = gate_rows // 2

    def half_view(low):
        def view(ref, dp, seq):
            row = pl.multiple_of(seq * gate_rows + low, half_block)
            return ref.at[pl.ds(row, half_block)]

        return view

    feed_grads = [
        Piece(order, (half_block, hidden_units), half_view(low))
        for order, low in ((near_order, 0), (far_order, half_block))
    ]
    in_grads = [
        Piece(order, (in_rows, third), in_view(i * third, (i + 1) * third))
        for i, order in enumerate((in_orders[0], ys + zs + xs + core, out_order))
    ]
    out_grads = [Piece(zs + xs + ys + core, out_weight.shape, out_view)]
    out_pieces = [Piece(out_order, out_weight.shape, out_view)]
    in_stacks, out_stacks = stacks[0] + stacks[1], stacks[2]

    gate_up = [gather_steps(v, p.steps[z_first:last]) for v, p in zip(gate_up, (*gate, *up))]
    down_shard = lax.ppermute(down_weight, ("dp", "seq"), home)
    final_there = dp_gather(grad_final, xs)[1:]
    final_near = swap(grad_final, core[0])
    forward = mixer_forward(
        ids, extended, consts, in_pieces, in_stacks, out_pieces, out_stacks, slot_size
    )
    forward, gate_up, down_shard, grad_final, final_near, final_there = tie(
        forward, gate_up, down_shard, grad_final, final_near, final_there
    )
    normed_one, b_part, c_part, x_part, mixed, gated, hidden, normed_two = forward

    wide = (features, hidden_units)
    gate_stacks, up_stacks = [last_step(v, p.steps[-1]) for v, p in zip(gate_up, (*gate, *up))]
    down_stack = gather_steps(down_shard[None], near_order[:z_first])
    normed_there = dp_gather(normed_two, xs)[1:]
    final_blocks = [grad_final, final_near] + with_core(final_there)
    normed_two, normed_there, gate_stacks, up_stacks, down_stack, final_blocks = tie(
        normed_two, normed_there, gate_stacks, up_stacks, down_stack, final_blocks
    )
    downs = [down_stack[:, a:b] for a, b in zip(cuts, cuts[1:])]
    normed_blocks = with_core([normed_two]) + with_core(normed_there)
    normed_blocks, downs, gate_stacks, up_stacks = tie(normed_blocks, downs, gate_stacks, up_stacks)
    downs = [gather_steps(v, p.steps[z_first:last]) for v, p in zip(downs, down)]
    activated, slope, silu, normed_all = feed_up(ids, normed_blocks, gate, gate_stacks, up, up_stacks, wide)
    activated, downs = tie(activated, downs)
    down_stacks = [v for stack, p in zip(downs, down) for v in last_step(stack, p.steps[-1])]
    down_parts = weight_gradient(ids, [activated], final_blocks, down)
    down_parts, down_stacks = tie(down_parts, down_stacks)

    def sent(parts, pieces, place):
        return [exchanged(v, p.steps[place]) for v, p in zip(parts, pieces)]

    def fold_all(parts):
        return [folded(v) for v in parts]

    def sent_on(parts, pieces):
        count = len(pieces[0].steps)
        for place in range(count - 2, 0, -1):
            parts = sent(fold_all(parts) if place < count - 2 else parts, pieces, place)
        return parts

    def joined(parts):
        return [tuple(jnp.concatenate(v, axis=1) for v in zip(*parts))]

    def core_halves(v):
        near, far = v[:2], v[2:]
        half = len(far) // 2
        return near[0], near[1], far[:half], far[half:]

    def far_added(keep, come):
        return [
            (a.astype(jnp.float32) + b.astype(jnp.float32)).astype(jnp.bfloat16)
            for a, b in zip(keep, come)
        ]

    down_parts = sent(down_parts, down, -1)
    grad_gate, grad_up, *back = feed_back(
        ids, final_blocks, activated, slope, silu, gate, gate_stacks, up, up_stacks, down, down_stacks, wide
    )
    back, feed = back[:n_dp], back[n_dp:]
    back, feed, grad_gate, grad_up, down_parts = tie(back, feed, grad_gate, grad_up, down_parts)
    near, near_send, far, far_send = core_halves(back)
    far_come = [swap(v, core[0]) for v in far_send]
    down_parts = sent_on(fold_all(down_parts), down)
    far, far_come, near, near_send, grad_gate, grad_up, feed, down_parts = tie(
        far, far_come, near, near_send, grad_gate, grad_up, feed, down_parts
    )
    far = far_added(far, far_come)
    half_rows = tok_rows // 2
    far_low, far_high = [v[:half_rows] for v in far], [v[half_rows:] for v in far]
    down_parts = joined(fold_all(down_parts))
    far_low, far_high, down_parts, near, near_send, grad_gate, grad_up, feed = tie(
        far_low, far_high, down_parts, near, near_send, grad_gate, grad_up, feed
    )
    far_low = dp_scatter([None] + far_low, xs)
    near_more = swap(near_send, core[0])
    down_parts = sent(down_parts, down, 0)
    gate_parts = weight_gradient(ids, [normed_all], [grad_gate], feed_grads, by_rows=True)
    gate_parts, far_low, far_high, grad_up, near, near_more, down_parts, feed = tie(
        gate_parts, far_low, far_high, grad_up, near, near_more, down_parts, feed
    )
    own_down = folded(down_parts[0]).astype(jnp.bfloat16)
    feed_near, feed_send, feed_far, feed_come = core_halves(feed)
    own_down, gate_parts, feed_far, feed_come, grad_up, far_low, far_high = tie(
        own_down, gate_parts, feed_far, feed_come, grad_up, far_low, far_high
    )
    far_high = dp_scatter([None] + far_high, xs)
    gate_parts = sent(gate_parts, feed_grads, -1)
    feed_come = [swap(v, core[0]) for v in feed_come]
    up_parts = weight_gradient(ids, [normed_all], [grad_up], feed_grads, by_rows=True)
    up_parts, far_low, far_high, gate_parts, feed_far, feed_come, own_down = tie(
        up_parts, far_low, far_high, gate_parts, feed_far, feed_come, own_down
    )

    feed_far = far_added(feed_far, feed_come)
    feed_low, feed_high = [v[:half_rows] for v in feed_far], [v[half_rows:] for v in feed_far]
    feed_low, feed_high, up_parts, gate_parts, far_low, far_high, own_down = tie(
        feed_low, feed_high, up_parts, gate_parts, far_low, far_high, own_down
    )
    up_parts = sent(up_parts, feed_grads, -1)
    feed_low = dp_scatter([None] + feed_low, xs)
    own_down = lax.ppermute(own_down, ("dp", "seq"), [(b, a) for a, b in home])
    grad_hidden, grad_c, grad_mixed, first_rows, sums, out_parts = mixer_back(
        ids,
        [near, near_more, grad_final, hidden, c_part, gated],
        far_low + far_high,
        mixed,
        consts,
        out_pieces,
        out_stacks,
        out_grads,
        slot_size,
    )
    out_parts, grad_mixed, first_rows, gate_parts, up_parts, feed_low, feed_high, own_down = tie(
        out_parts, grad_mixed, first_rows, gate_parts, up_parts, feed_low, feed_high, own_down
    )
    returned = lax.ppermute(first_rows, "seq", [(i + 1, i) for i in range(n_seq - 1)])
    out_parts = fold_all(sent(out_parts, out_grads, -1))
    gate_parts, up_parts = fold_all(gate_parts), fold_all(up_parts)
    returned, out_parts, up_parts, gate_parts, feed_high = tie(
        returned, out_parts, up_parts, gate_parts, feed_high
    )
    gate_parts = sent_on(gate_parts, feed_grads)
    up_parts = sent_on(up_parts, feed_grads)
    feed_high = dp_scatter([None] + feed_high, xs)
    grad_proj, in_parts = projection_gradient(
        ids, normed_one, grad_mixed, returned, grad_c, b_part, x_part, in_grads
    )
    in_parts, up_parts, gate_parts, grad_proj, out_parts, feed_high = tie(
        in_parts, up_parts, gate_parts, grad_proj, out_parts, feed_high
    )
    gate_parts = joined(fold_all(gate_parts))
    in_parts, gate_parts, out_parts, grad_proj = tie(in_parts, gate_parts, out_parts, grad_proj)
    in_parts = sent(in_parts, in_grads, -1)
    out_parts = sent(out_parts, out_grads, -2)
    gate_parts = sent(gate_parts, feed_grads, 0)
    grad_tokens, sums = mixer_first(ids, grad_proj, tokens, grad_hidden, sums, consts, in_pieces, in_stacks)
    in_parts, out_parts, sums, gate_parts, up_parts, feed_send = tie(
        in_parts, out_parts, sums, gate_parts, up_parts, feed_send
    )
    sum_steps = core + ys + xs + zs[::-1]
    for step in sum_steps[:1]:
        sums = sums + swap(sums, step)
    in_parts, out_parts, up_parts = fold_all(in_parts), fold_all(out_parts), joined(fold_all(up_parts))
    in_parts, out_parts, up_parts, sums = tie(in_parts, out_parts, up_parts, sums)
    in_parts = sent(in_parts, in_grads, -2)
    sums = (sums, swap(sums, sum_steps[1]))
    in_parts, out_parts, up_parts, sums, feed_send = tie(in_parts, out_parts, up_parts, sums, feed_send)
    in_parts, sums = fold_all(in_parts), sums[0] + sums[1]
    in_parts, out_parts, up_parts, sums = tie(in_parts, out_parts, up_parts, sums)
    in_parts = sent(in_parts, in_grads, -3)
    out_parts = sent(out_parts, out_grads, -3)
    up_parts = sent(up_parts, feed_grads, 0)
    sums = (sums, swap(sums, sum_steps[2]))
    in_parts, out_parts, up_parts, sums, feed_send = tie(in_parts, out_parts, up_parts, sums, feed_send)
    in_parts, out_parts, sums = fold_all(in_parts), fold_all(out_parts), sums[0] + sums[1]
    in_parts, out_parts, sums = tie(in_parts, out_parts, sums)
    in_parts = sent(in_parts, in_grads, -4)
    out_parts = sent(out_parts, out_grads, -4)
    sums = (sums, swap(sums, sum_steps[3]))
    feed_more = swap(feed_send, core[0])
    in_parts, out_parts, sums, feed_more, own_down = tie(in_parts, out_parts, sums, feed_more, own_down)
    sums = sums[0] + sums[1]
    for step in sum_steps[4:]:
        sums = sums + swap(sums, step)
    own_down = own_down.astype(jnp.float32)

    def rest(parts, piece, done):
        parts = folded(parts)
        for place in range(len(piece.steps) - done - 1, -1, -1):
            parts = folded(exchanged(parts, piece.steps[place]))
        return parts

    own_in = [rest(v, p, 4) for v, p in zip(in_parts, in_grads)]
    own_in = jnp.concatenate(own_in, axis=1)
    own_out = rest(out_parts[0], out_grads[0], 4)
    own_gate = folded(gate_parts[0])
    own_up = folded(up_parts[0])
    own_sums = lax.dynamic_slice(sums, (0, own_seq * small_cols), (8, small_cols))
    feed_out = jnp.concatenate(feed_low + feed_high, axis=0).astype(jnp.float32)
    feed_out = feed_out + feed_near.astype(jnp.float32) + feed_more.astype(jnp.float32)
    output = (live_mask * (hidden + feed_out)).astype(jnp.bfloat16)
    return (
        output,
        grad_tokens,
        own_sums[0],
        own_in,
        own_sums[2:5],
        own_out,
        own_sums[1],
        own_gate,
        own_up,
        own_down,
    )


def solution(mesh):
    in_specs = (
        P(("dp", "seq"), None),
        P("seq"),
        P("seq", "dp"),
        P(None, "seq"),
        P("seq", "dp"),
        P("seq"),
        P("seq", "dp"),
        P("seq", "dp"),
        P("seq", "dp"),
        P("dp", None),
        P(("dp", "seq"), None),
    )
    out_specs = (
        P(("dp", "seq"), None),
        P(("dp", "seq"), None),
        P("seq"),
        P("seq", "dp"),
        P(None, "seq"),
        P("seq", "dp"),
        P("seq"),
        P("seq", "dp"),
        P("seq", "dp"),
        P("seq", "dp"),
    )
    return jax.shard_map(
        per_device, mesh=mesh, in_specs=in_specs, out_specs=out_specs, check_vma=False
    )
```

```python
from typing import NamedTuple

import jax
import jax.numpy as jnp
from jax import lax
from jax.experimental import pallas as pl
from jax.experimental.pallas import tpu as pltpu
from jax.sharding import PartitionSpec as P

SLOT_MAX = 8192
HALO = 16
SMALL_ROWS = 16
VMEM_BYTES = 56 << 20
TILE = 256
KERNEL_COST = pl.CostEstimate(flops=1 << 36, bytes_accessed=1 << 20, transcendentals=0)

norm_eps = 1e-05


def multiply(left_side, right_side):
    return jnp.dot(left_side, right_side, preferred_element_type=jnp.float32)


def against(left_side, right_side):
    return lax.dot_general(
        left_side, right_side, (((1,), (1,)), ((), ())), preferred_element_type=jnp.float32
    )


def outer_sum(left_side, right_side):
    return lax.dot_general(
        left_side, right_side, (((0,), (0,)), ((), ())), preferred_element_type=jnp.float32
    )


def tie(*values):
    return lax.optimization_barrier(values)


def swap(shard, step):
    axis, bit = step
    count = lax.axis_size(axis)
    return lax.ppermute(shard, axis, [(i, i ^ bit) for i in range(count)])


def gather_steps(stack, steps):
    for step in steps:
        stack = jnp.concatenate([stack, swap(stack, step)], axis=0)
    return stack


def last_step(stack, step):
    return [stack, swap(stack, step)]


def exchanged(parts, step):
    keep, send = parts
    return keep, swap(send, step)


def folded(parts):
    keep, come = parts
    total = keep.astype(jnp.float32) + come.astype(jnp.float32)
    half = total.shape[0] // 2
    if not half:
        return total[0]
    return total[:half].astype(jnp.bfloat16), total[half:].astype(jnp.bfloat16)


def masks_at(position, steps):
    masks = {"dp": 0, "seq": 0}
    for place, (axis, bit) in enumerate(steps):
        masks[axis] = masks[axis] + ((position >> place) & 1) * bit
    return masks["dp"], masks["seq"]


def tile_of(ref, row, rows, col, cols):
    return ref.at[pl.ds(pl.multiple_of(row * rows, rows), rows), pl.ds(pl.multiple_of(col * cols, cols), cols)]


def dp_gather(block, steps):
    blocks = [block]
    for step in steps:
        blocks = blocks + [swap(b, step) for b in blocks]
    return blocks


def dp_scatter(parts, steps):
    for step in reversed(steps):
        half = len(parts) // 2
        moved = [swap(send.astype(jnp.bfloat16), step) for send in parts[half:]]
        parts = [
            new if keep is None else keep.astype(jnp.float32) + new.astype(jnp.float32)
            for keep, new in zip(parts[:half], moved)
        ]
    return parts


class Piece(NamedTuple):
    steps: list
    block: tuple
    view: object


def start_loads(ids_ref, refs, pieces, into, sem):
    for place, piece in enumerate(pieces):
        first = 0
        for part in refs[2 * place : 2 * place + 2]:

            def start(position, carry, part=part, first=first, piece=piece):
                mask_dp, mask_seq = masks_at(position + first, piece.steps)
                pltpu.make_async_copy(
                    part.at[position],
                    piece.view(into, ids_ref[0] ^ mask_dp, ids_ref[1] ^ mask_seq),
                    sem,
                ).start()
                return carry

            lax.fori_loop(0, part.shape[0], start, 0)
            first += part.shape[0]


def start_stores(ids_ref, whole, pieces, outs, sem):
    each = len(outs) // len(pieces)
    for place, piece in enumerate(pieces):
        size = 2 ** len(piece.steps) // each
        for part in range(each):

            def start(position, carry, first=part * size, out=outs[each * place + part], piece=piece):
                mask_dp, mask_seq = masks_at(position + first, piece.steps)
                source = piece.view(whole, ids_ref[0] ^ mask_dp, ids_ref[1] ^ mask_seq)
                pltpu.make_async_copy(source, out.at[position], sem).start()
                return carry

            lax.fori_loop(0, size, start, 0)


def start_row_stores(ids_ref, whole, pieces, outs, sem, first, count):
    each = len(outs) // len(pieces)
    for step in range(count):
        seq = first + step
        mask = seq ^ ids_ref[1]
        for place, piece in enumerate(pieces):
            size = 2 ** len(piece.steps) // each
            position = sum(
                ((mask >> (bit.bit_length() - 1)) & 1) << at for at, (_, bit) in enumerate(piece.steps)
            )
            for part in range(each):

                @pl.when(jnp.logical_and(position >= part * size, position < (part + 1) * size))
                def _(part=part, position=position, seq=seq, piece=piece, place=place, size=size):
                    pltpu.make_async_copy(
                        piece.view(whole, ids_ref[0], seq),
                        outs[each * place + part].at[position - part * size],
                        sem,
                    ).start()


def wait_whole(ref, sem):
    pltpu.make_async_copy(ref, ref, sem).wait()


def fetch_block(blocks, buffers, sems):
    i = pl.program_id(0)

    rows = buffers.shape[1]

    def copy(place):
        slot = place % 2
        source = blocks[place // 2].at[pl.ds(place % 2 * rows, rows)]
        return pltpu.make_async_copy(source, buffers.at[slot], sems.at[slot])

    for place in range(2 * len(blocks)):

        @pl.when(i == place)
        def _(place=place):
            if place == 0:
                copy(0).start()
            if place + 1 < 2 * len(blocks):
                copy(place + 1).start()
            copy(place).wait()

    return buffers[i % 2]


def token_call(kernel, ids, blocks, tiled, stacks, outs, apart, scratch):
    rows, width = blocks[0].shape
    rows, count, steps = rows // 2, len(blocks), 2 * len(blocks)
    return pl.pallas_call(
        kernel,
        out_shape=[jax.ShapeDtypeStruct((rows * steps, n), t) for n, t in outs]
        + [jax.ShapeDtypeStruct((rows * 2, n), t) for n, t in apart for _ in range(count)],
        grid_spec=pltpu.PrefetchScalarGridSpec(
            num_scalar_prefetch=1,
            grid=(steps,),
            in_specs=[pl.BlockSpec(memory_space=pl.ANY)] * count
            + [pl.BlockSpec((rows, v.shape[1]), lambda i, ids: (i, 0)) for v in tiled]
            + [pl.BlockSpec(memory_space=pl.ANY)] * len(stacks),
            out_specs=[pl.BlockSpec((rows, n), lambda i, ids: (i, 0)) for n, _ in outs]
            + [pl.BlockSpec(memory_space=pl.ANY)] * (len(apart) * count),
            scratch_shapes=[
                pltpu.VMEM((2, rows, width), jnp.bfloat16),
                pltpu.SemaphoreType.DMA((2,)),
                *scratch,
            ],
        ),
        compiler_params=pltpu.CompilerParams(vmem_limit_bytes=VMEM_BYTES),
        cost_estimate=KERNEL_COST,
    )(ids, *blocks, *tiled, *stacks)


def feed_up(ids, normed, gate, gate_stacks, up, up_stacks, shape):
    count = len(normed)

    def kernel(ids_ref, *refs):
        blocks, stacks, refs = refs[:count], refs[count:-9], refs[-9:]
        act, slope, silu, whole, buffers, block_sems, gate_v, up_v, sems = refs

        @pl.when(pl.program_id(0) == 0)
        def _():
            start_loads(ids_ref, stacks[: 2 * len(gate)], gate, gate_v, sems.at[0])
            start_loads(ids_ref, stacks[2 * len(gate) :], up, up_v, sems.at[1])

        x = fetch_block(blocks, buffers, block_sems)

        @pl.when(pl.program_id(0) == 0)
        def _():
            wait_whole(gate_v, sems.at[0])
            wait_whole(up_v, sems.at[1])

        whole[...] = x
        gate_val = multiply(x, gate_v[...])
        up_val = multiply(x, up_v[...])
        sigmoid = jax.nn.sigmoid(gate_val)
        silu_gate = gate_val * sigmoid
        act[...] = (silu_gate * up_val).astype(jnp.bfloat16)
        slope[...] = (up_val * sigmoid * (1.0 + gate_val * (1.0 - sigmoid))).astype(jnp.bfloat16)
        silu[...] = silu_gate.astype(jnp.bfloat16)

    n = shape[1]
    return token_call(
        kernel,
        ids,
        normed,
        [],
        [*gate_stacks, *up_stacks],
        [(n, jnp.bfloat16)] * 3 + [(shape[0], jnp.bfloat16)],
        [],
        [pltpu.VMEM(shape, jnp.bfloat16)] * 2 + [pltpu.SemaphoreType.DMA((2,))],
    )


def feed_back(ids, final, activated, slope, silu, gate, gate_stacks, up, up_stacks, down, down_stacks, shape):
    count = len(final)
    ends = [2 * len(gate), 2 * len(gate) + 2 * len(up)]

    def kernel(ids_ref, *refs):
        blocks, (act_ref, slope_ref, silu_ref) = refs[:count], refs[count : count + 3]
        parts = 2 * count
        stacks, refs = refs[count + 3 : -10 - parts], refs[-10 - parts :]
        grad_gate, grad_up, buffers, block_sems, gate_v, up_v, down_v, sems = refs[:2] + refs[2 + parts : -2]
        tiles, store_sems = refs[-2:]
        i = pl.program_id(0)
        slot = i % 2
        norm_parts, out_parts = refs[2 : 2 + count], refs[2 + count : 2 + parts]

        @pl.when(pl.program_id(0) == 0)
        def _():
            start_loads(ids_ref, stacks[ends[1] :], down, down_v, sems.at[2])
            start_loads(ids_ref, stacks[: ends[0]], gate, gate_v, sems.at[0])
            start_loads(ids_ref, stacks[ends[0] : ends[1]], up, up_v, sems.at[1])

        f = fetch_block(blocks, buffers, block_sems)

        @pl.when(pl.program_id(0) == 0)
        def _():
            wait_whole(down_v, sems.at[2])
            wait_whole(gate_v, sems.at[0])
            wait_whole(up_v, sems.at[1])

        grad_act = against(f, down_v[...])
        gg = (grad_act * slope_ref[...].astype(jnp.float32)).astype(jnp.bfloat16)
        gu = (grad_act * silu_ref[...].astype(jnp.float32)).astype(jnp.bfloat16)
        grad_gate[...] = gg
        grad_up[...] = gu
        @pl.when(i >= 2)
        def _():
            wait_whole(tiles.at[slot], store_sems.at[slot])

        tiles[slot, 0] = multiply(act_ref[...], down_v[...]).astype(jnp.bfloat16)
        tiles[slot, 1] = (against(gg, gate_v[...]) + against(gu, up_v[...])).astype(jnp.bfloat16)
        rows = tiles.shape[2]
        for place in range(count):

            @pl.when(i // 2 == place)
            def _(place=place):
                at = pl.ds(pl.multiple_of(slot * rows, rows), rows)
                for kind, target in ((0, out_parts[place]), (1, norm_parts[place])):
                    pltpu.make_async_copy(tiles.at[slot, kind], target.at[at], store_sems.at[slot]).start()

        @pl.when(i == 2 * count - 1)
        def _():
            wait_whole(tiles.at[0], store_sems.at[0])
            wait_whole(tiles.at[1], store_sems.at[1])

    features, n = shape
    return token_call(
        kernel,
        ids,
        final,
        [activated, slope, silu],
        [*gate_stacks, *up_stacks, *down_stacks],
        [(n, jnp.bfloat16)] * 2,
        [(features, jnp.bfloat16)] * 2,
        [
            pltpu.VMEM(shape, jnp.bfloat16),
            pltpu.VMEM(shape, jnp.bfloat16),
            pltpu.VMEM((n, features), jnp.bfloat16),
            pltpu.SemaphoreType.DMA((3,)),
            pltpu.VMEM((2, 2, final[0].shape[0] // 2, features), jnp.bfloat16),
            pltpu.SemaphoreType.DMA((2,)),
        ],
    )


def stack_shapes(pieces, each=2):
    shapes = []
    for piece in pieces:
        size = 2 ** len(piece.steps) // each
        shapes += [jax.ShapeDtypeStruct((size, *piece.block), jnp.bfloat16)] * each
    return shapes


def paired(parts, each=2):
    return [tuple(parts[i : i + each]) for i in range(0, len(parts), each)]


def weight_gradient(ids, lefts, rights, pieces, each=2, by_rows=False):
    rows, columns = lefts[0].shape[1], rights[0].shape[1]
    step = min(v.shape[0] for v in (*lefts, *rights))
    tile = next((t for t in (512, 384, 256, 128) if rows % t == 0), rows)
    count = rows // tile
    shapes = stack_shapes(pieces, each)

    def kernel(ids_ref, *refs):
        sides, refs = refs[: len(lefts) + len(rights)], refs[len(lefts) + len(rights) :]
        outs, (whole, sems) = refs[:-2], refs[-2:]
        i = pl.program_id(0)
        left_rows, right_rows = [
            [v[at : at + step] for v in side for at in range(0, v.shape[0], step)]
            for side in (sides[: len(lefts)], sides[len(lefts) :])
        ]
        total = sum(outer_sum(a, b) for a, b in zip(left_rows, right_rows))
        whole[pl.ds(pl.multiple_of(i * tile, tile), tile)] = total.astype(jnp.bfloat16)

        if by_rows:
            seqs = 2 ** len(pieces[0].steps) // count
            start_row_stores(ids_ref, whole, pieces, outs, sems.at[0], i * seqs, seqs)

        @pl.when(i == count - 1)
        def _():
            if not by_rows:
                start_stores(ids_ref, whole, pieces, outs, sems.at[0])
            wait_whole(whole, sems.at[0])

    parts = pl.pallas_call(
        kernel,
        out_shape=shapes,
        grid_spec=pltpu.PrefetchScalarGridSpec(
            num_scalar_prefetch=1,
            grid=(count,),
            in_specs=[
                *(pl.BlockSpec((v.shape[0], tile), lambda i, ids: (0, i)) for v in lefts),
                *(pl.BlockSpec((v.shape[0], columns), lambda i, ids: (0, 0)) for v in rights),
            ],
            out_specs=[pl.BlockSpec(memory_space=pl.ANY)] * len(shapes),
            scratch_shapes=[
                pltpu.VMEM((rows, columns), jnp.bfloat16),
                pltpu.SemaphoreType.DMA((1,)),
            ],
        ),
        compiler_params=pltpu.CompilerParams(vmem_limit_bytes=VMEM_BYTES),
        cost_estimate=KERNEL_COST,
    )(ids, *lefts, *rights)
    return paired(parts, each)


def mixer_forward(ids, extended, consts, in_pieces, in_stacks, out_pieces, out_stacks, slot_size):
    rows, features = extended.shape
    rows = rows - HALO
    tile = rows // 2
    count = len(in_stacks)
    wide = 3 * features

    def kernel(ids_ref, ext_ref, const_ref, *refs):
        stacks, refs = refs[: count + len(out_stacks)], refs[count + len(out_stacks) :]
        normed_one, b_out, c_out, x_out, mixed_out, gated_out, hidden_out, normed_two = refs[:8]
        in_v, out_v, mixed_s, sems = refs[8:]
        i = pl.program_id(0)

        @pl.when(i == 0)
        def _():
            start_loads(ids_ref, stacks[:count], in_pieces, in_v, sems.at[0])
            start_loads(ids_ref, stacks[count:], out_pieces, out_v, sems.at[1])

        at = pl.multiple_of(i * tile, HALO)
        x = ext_ref[pl.ds(at, HALO + tile)].astype(jnp.float32)
        scale = lax.rsqrt(jnp.mean(x * x, axis=1, keepdims=True) + norm_eps)
        normed = (x * scale * const_ref[0:1]).astype(jnp.bfloat16)
        normed_one[...] = normed[HALO:]

        @pl.when(i == 0)
        def _():
            wait_whole(in_v, sems.at[0])
            wait_whole(out_v, sems.at[1])

        b_part = multiply(normed, in_v[:, :features])
        x_part = multiply(normed, in_v[:, 2 * features :])
        b_out[...] = b_part[HALO:].astype(jnp.bfloat16)
        x_out[...] = x_part[HALO:].astype(jnp.bfloat16)
        mixed = (b_part * x_part).astype(jnp.bfloat16)
        mixed_s[...] = mixed.astype(jnp.float32)
        base = lax.rem(ids_ref[1] * rows, slot_size)

        @pl.when(jnp.logical_and(i == 0, base == 0))
        def _():
            mixed_s[0:HALO] = jnp.zeros((HALO, features), jnp.float32)

        mixed_out[pl.ds(at, HALO)] = mixed_s[0:HALO].astype(jnp.bfloat16)
        mixed_out[pl.ds(pl.multiple_of(at + HALO, HALO), tile)] = mixed[HALO:]
        conv = sum(
            const_ref[2 + k : 3 + k] * mixed_s[HALO - 2 + k : HALO - 2 + k + tile] for k in range(3)
        )
        c_part = multiply(normed[HALO:], in_v[:, features : 2 * features])
        c_out[...] = c_part.astype(jnp.bfloat16)
        gated = (c_part * conv).astype(jnp.bfloat16)
        gated_out[...] = gated
        hidden = x[HALO:] + multiply(gated, out_v[...])
        hidden_out[...] = hidden
        scale = lax.rsqrt(jnp.mean(hidden * hidden, axis=1, keepdims=True) + norm_eps)
        normed_two[...] = (hidden * scale * const_ref[1:2]).astype(jnp.bfloat16)

    f32, bf16 = jnp.float32, jnp.bfloat16
    kinds = [bf16, bf16, bf16, bf16, bf16, bf16, f32, bf16]
    shapes = [(rows + (HALO if i == 4 else 0), features) for i in range(8)]
    whole = pl.BlockSpec((rows + HALO, features), lambda i, ids: (0, 0))
    part = pl.BlockSpec((tile, features), lambda i, ids: (i, 0))
    return pl.pallas_call(
        kernel,
        out_shape=[jax.ShapeDtypeStruct(s, t) for s, t in zip(shapes, kinds)],
        grid_spec=pltpu.PrefetchScalarGridSpec(
            num_scalar_prefetch=1,
            grid=(2,),
            in_specs=[whole, pl.BlockSpec(consts.shape, lambda i, ids: (0, 0))]
            + [pl.BlockSpec(memory_space=pl.ANY)] * (count + len(out_stacks)),
            out_specs=[whole if i == 4 else part for i in range(8)],
            scratch_shapes=[
                pltpu.VMEM((features, wide), bf16),
                pltpu.VMEM((features, features), bf16),
                pltpu.VMEM((tile + HALO, features), f32),
                pltpu.SemaphoreType.DMA((2,)),
            ],
        ),
        compiler_params=pltpu.CompilerParams(vmem_limit_bytes=VMEM_BYTES),
        cost_estimate=KERNEL_COST,
    )(ids, extended, consts, *in_stacks, *out_stacks)


def mixer_back(ids, tiled, far, mixed, consts, out_pieces, out_stacks, out_grads, slot_size):
    rows, features = tiled[0].shape
    tile = rows // 2
    shapes = stack_shapes(out_grads)

    def kernel(ids_ref, *refs):
        near_ref, more_ref, final_ref, hidden_ref, c_ref, gated_ref = refs[:6]
        low_ref, high_ref, mixed_ref, const_ref = refs[6:10]
        refs = refs[10:]
        stacks, refs = refs[: len(out_stacks)], refs[len(out_stacks) :]
        grad_hidden, grad_c, grad_mixed, head, sums = refs[:5]
        outs, (out_v, whole, mixed_s, conv_s, sems) = refs[5:-5], refs[-5:]
        i = pl.program_id(0)

        @pl.when(i == 0)
        def _():
            start_loads(ids_ref, stacks, out_pieces, out_v, sems.at[0])
            sums[...] = jnp.zeros(sums.shape, jnp.float32)
            conv_s[tile:] = jnp.zeros((8, features), jnp.float32)

        @pl.when(i > 0)
        def _():
            conv_s[tile:] = conv_s[0:8]

        normed_grad = near_ref[...].astype(jnp.float32) + more_ref[...].astype(jnp.float32)
        normed_grad += jnp.where(i == 0, high_ref[...].astype(jnp.float32), low_ref[...].astype(jnp.float32))
        h = hidden_ref[...]
        scale = lax.rsqrt(jnp.mean(h * h, axis=1, keepdims=True) + norm_eps)
        weighted = normed_grad * const_ref[1:2]
        inner = jnp.mean(weighted * h, axis=1, keepdims=True)
        sums[1:2] += jnp.sum(normed_grad * h * scale, axis=0, keepdims=True)
        total = final_ref[...].astype(jnp.float32) + scale * weighted - h * (scale * scale * scale * inner)
        grad_hidden[...] = total
        branch = total.astype(jnp.bfloat16)
        outer = outer_sum(gated_ref[...], branch)

        @pl.when(i == 0)
        def _():
            wait_whole(out_v, sems.at[0])

        grad_gated = against(branch, out_v[...])
        at = pl.multiple_of((1 - i) * tile, HALO)
        mixed_s[...] = mixed_ref[pl.ds(at, HALO + tile)].astype(jnp.float32)
        conv = sum(
            const_ref[2 + k : 3 + k] * mixed_s[HALO - 2 + k : HALO - 2 + k + tile] for k in range(3)
        )
        grad_c[...] = (grad_gated * conv).astype(jnp.bfloat16)
        grad_conv = grad_gated * c_ref[...].astype(jnp.float32)
        conv_s[0:tile] = grad_conv
        for k in range(3):
            sums[2 + k : 3 + k] += jnp.sum(
                grad_conv * mixed_s[HALO - 2 + k : HALO - 2 + k + tile], axis=0, keepdims=True
            )
        grad_mixed[...] = sum(const_ref[2 + k : 3 + k] * conv_s[2 - k : 2 - k + tile] for k in range(3))

        @pl.when(i == 1)
        def _():
            live = jnp.where(lax.rem(ids_ref[1] * rows, slot_size) > 0, 1.0, 0.0)
            head[...] = jnp.zeros(head.shape, jnp.float32)
            head[0:1] = live * const_ref[2:3] * conv_s[0:1]
            head[1:2] = live * (const_ref[2:3] * conv_s[1:2] + const_ref[3:4] * conv_s[0:1])
            out_v[...] = (whole[...] + outer).astype(jnp.bfloat16)
            start_stores(ids_ref, out_v, out_grads, outs, sems.at[0])
            wait_whole(out_v, sems.at[0])

        @pl.when(i == 0)
        def _():
            whole[...] = outer

    f32, bf16 = jnp.float32, jnp.bfloat16
    part = pl.BlockSpec((tile, features), lambda i, ids: (1 - i, 0))
    once = pl.BlockSpec((8, features), lambda i, ids: (0, 0))
    parts = pl.pallas_call(
        kernel,
        out_shape=[jax.ShapeDtypeStruct((rows, features), t) for t in (f32, bf16, f32)]
        + [jax.ShapeDtypeStruct((8, features), f32)] * 2
        + shapes,
        grid_spec=pltpu.PrefetchScalarGridSpec(
            num_scalar_prefetch=1,
            grid=(2,),
            in_specs=[part] * 6
            + [pl.BlockSpec((tile, features), lambda i, ids: (0, 0))] * 2
            + [pl.BlockSpec((rows + HALO, features), lambda i, ids: (0, 0)), once]
            + [pl.BlockSpec(memory_space=pl.ANY)] * len(out_stacks),
            out_specs=[part] * 3 + [once] * 2 + [pl.BlockSpec(memory_space=pl.ANY)] * len(shapes),
            scratch_shapes=[
                pltpu.VMEM((features, features), bf16),
                pltpu.VMEM((features, features), f32),
                pltpu.VMEM((tile + HALO, features), f32),
                pltpu.VMEM((tile + 8, features), f32),
                pltpu.SemaphoreType.DMA((1,)),
            ],
        ),
        compiler_params=pltpu.CompilerParams(vmem_limit_bytes=VMEM_BYTES),
        cost_estimate=KERNEL_COST,
    )(ids, *tiled, *far, mixed, consts, *out_stacks)
    return [*parts[:5], paired(parts[5:])]


def projection_gradient(ids, normed, grad_mixed, returned, grad_c, b_part, x_part, pieces):
    rows, features = normed.shape
    tile = features // 4
    shapes = stack_shapes(pieces)

    def kernel(ids_ref, normed_ref, mixed_ref, back_ref, c_ref, b_ref, x_ref, proj, *refs):
        outs, (whole, mixed_s, sems) = refs[:-3], refs[-3:]
        i = pl.program_id(0)

        @pl.when(i == 0)
        def _():
            mixed_s[...] = mixed_ref[...]
            mixed_s[rows - 2 :] += back_ref[0:2]
            grad = mixed_s[...]
            proj[:, :features] = (grad * x_ref[...].astype(jnp.float32)).astype(jnp.bfloat16)
            proj[:, features : 2 * features] = c_ref[...]
            proj[:, 2 * features :] = (grad * b_ref[...].astype(jnp.float32)).astype(jnp.bfloat16)

        whole[pl.ds(pl.multiple_of(i * tile, tile), tile)] = outer_sum(
            normed_ref[...], proj[...]
        ).astype(jnp.bfloat16)

        @pl.when(i == 3)
        def _():
            start_stores(ids_ref, whole, pieces, outs, sems.at[0])
            wait_whole(whole, sems.at[0])

    def same(n, width):
        return pl.BlockSpec((n, width), lambda i, ids: (0, 0))

    parts = pl.pallas_call(
        kernel,
        out_shape=[jax.ShapeDtypeStruct((rows, 3 * features), jnp.bfloat16), *shapes],
        grid_spec=pltpu.PrefetchScalarGridSpec(
            num_scalar_prefetch=1,
            grid=(4,),
            in_specs=[
                pl.BlockSpec((rows, tile), lambda i, ids: (0, i)),
                same(rows, features),
                same(8, features),
                same(rows, features),
                same(rows, features),
                same(rows, features),
            ],
            out_specs=[same(rows, 3 * features)] + [pl.BlockSpec(memory_space=pl.ANY)] * len(shapes),
            scratch_shapes=[
                pltpu.VMEM((features, 3 * features), jnp.bfloat16),
                pltpu.VMEM((rows, features), jnp.float32),
                pltpu.SemaphoreType.DMA((1,)),
            ],
        ),
        compiler_params=pltpu.CompilerParams(vmem_limit_bytes=VMEM_BYTES),
        cost_estimate=KERNEL_COST,
    )(ids, normed, grad_mixed, returned, grad_c, b_part, x_part)
    return parts[0], paired(parts[1:])


def mixer_first(ids, proj, tokens, grad_hidden, sums, consts, in_pieces, in_stacks):
    rows, features = tokens.shape
    tile = rows // 2

    def kernel(ids_ref, proj_ref, x_ref, hidden_ref, sums_ref, const_ref, *refs):
        stacks, (grad_tokens, sums_out, in_v, sems) = refs[:-4], refs[-4:]

        @pl.when(pl.program_id(0) == 0)
        def _():
            start_loads(ids_ref, stacks, in_pieces, in_v, sems.at[0])
            sums_out[...] = sums_ref[...]
            wait_whole(in_v, sems.at[0])

        normed_grad = against(proj_ref[...], in_v[...])
        x = x_ref[...].astype(jnp.float32)
        scale = lax.rsqrt(jnp.mean(x * x, axis=1, keepdims=True) + norm_eps)
        weighted = normed_grad * const_ref[0:1]
        inner = jnp.mean(weighted * x, axis=1, keepdims=True)
        sums_out[0:1] += jnp.sum(normed_grad * x * scale, axis=0, keepdims=True)
        grad_tokens[...] = (
            hidden_ref[...] + scale * weighted - x * (scale * scale * scale * inner)
        ).astype(jnp.bfloat16)

    part = pl.BlockSpec((tile, features), lambda i, ids: (i, 0))
    once = pl.BlockSpec((8, features), lambda i, ids: (0, 0))
    return pl.pallas_call(
        kernel,
        out_shape=[
            jax.ShapeDtypeStruct((rows, features), jnp.bfloat16),
            jax.ShapeDtypeStruct((8, features), jnp.float32),
        ],
        grid_spec=pltpu.PrefetchScalarGridSpec(
            num_scalar_prefetch=1,
            grid=(2,),
            in_specs=[pl.BlockSpec((tile, 3 * features), lambda i, ids: (i, 0)), part, part, once, once]
            + [pl.BlockSpec(memory_space=pl.ANY)] * len(in_stacks),
            out_specs=[part, once],
            scratch_shapes=[
                pltpu.VMEM((features, 3 * features), jnp.bfloat16),
                pltpu.SemaphoreType.DMA((1,)),
            ],
        ),
        compiler_params=pltpu.CompilerParams(vmem_limit_bytes=VMEM_BYTES),
        cost_estimate=KERNEL_COST,
    )(ids, proj, tokens, grad_hidden, sums, consts, *in_stacks)


def bits_below(count):
    return [1 << i for i in range(count.bit_length() - 1)]


def per_device(
    tokens,
    mixer_gain,
    in_weight,
    conv_weight,
    out_weight,
    feed_gain,
    gate_weight,
    up_weight,
    down_weight,
    lengths,
    cotangent,
):
    n_dp, n_seq = lax.axis_size("dp"), lax.axis_size("seq")
    tok_rows, features = tokens.shape
    slot_size = min(SLOT_MAX, tok_rows * n_seq)
    own_dp, own_seq = lax.axis_index("dp"), lax.axis_index("seq")
    ids = jnp.stack([own_dp, own_seq]).astype(jnp.int32)

    seq_bits = bits_below(n_seq)
    along_y = seq_bits[: len(seq_bits) // 2]
    ys = [("seq", b) for b in reversed(along_y)]
    zs = [("seq", b) for b in reversed(seq_bits[len(along_y) :])]
    core = [("dp", 1)]
    xs = [("dp", b) for b in reversed(bits_below(n_dp)[1:])]
    in_orders = [zs + xs + ys + core, zs[::-1] + ys + xs + core]
    out_order = zs[:1] + xs + ys + zs[1:] + core
    far_order, near_order = zs[:1] + ys + zs[1:], zs + ys
    token_order = xs + core

    position = own_seq * tok_rows + jnp.arange(tok_rows, dtype=jnp.int32)
    in_slot = position % slot_size
    slot_index = position // slot_size
    slot_ids = jnp.arange(lengths.shape[1], dtype=jnp.int32)
    slot_length = jnp.sum(
        jnp.where(slot_index[:, None] == slot_ids[None, :], lengths[0][None, :], 0), axis=1
    )
    live_mask = (in_slot < slot_length).astype(jnp.float32)[:, None]

    in_rows, in_cols = in_weight.shape
    out_rows, out_cols = out_weight.shape
    in_cut = (in_cols // 128 + 1) // 2 * 128
    in_cuts = [0, in_cut, in_cols]
    third = in_cols // 3
    small_cols = mixer_gain.shape[0]
    small = jnp.concatenate([mixer_gain[None], feed_gain[None], conv_weight], axis=0)
    small = jnp.pad(small, ((0, SMALL_ROWS - small.shape[0]), (0, -small_cols % 128)))
    small_order = zs + ys
    mixer = [in_weight[None, :, :in_cut], in_weight[None, :, in_cut:], out_weight[None]]
    orders = [*in_orders, out_order]
    hidden_units = gate_weight.shape[1]
    gate_rows = gate_weight.shape[0]
    down_rows, down_cols = down_weight.shape
    ratio = n_seq // n_dp
    turned = [(e % 2) * (n_dp // 2) + e // 2 for e in range(n_dp)]
    home = [
        (e * n_seq + s, (s // ratio) * n_seq + turned[e] * ratio + s % ratio)
        for e in range(n_dp)
        for s in range(n_seq)
    ]
    cuts = [0, -(-down_rows // 32) * 16, down_rows]

    def gate_view(ref, dp, seq):
        return ref.at[pl.ds(pl.multiple_of(seq * gate_rows, gate_rows), gate_rows)]

    def down_view(cut):
        low, high = cuts[cut], cuts[cut + 1]

        def view(ref, dp, seq):
            row = pl.multiple_of((seq % ratio) * down_rows + low, 16)
            place = seq // ratio
            place = place % (n_dp // 2) * 2 + place // (n_dp // 2)
            col = pl.multiple_of(place * down_cols, down_cols)
            return ref.at[pl.ds(row, high - low), pl.ds(col, down_cols)]

        return view

    gate = [Piece(near_order, gate_weight.shape, gate_view)]
    up = [Piece(far_order, up_weight.shape, gate_view)]
    down = [
        Piece(order, (cuts[i + 1] - cuts[i], down_cols), down_view(i))
        for i, order in enumerate((near_order, far_order))
    ]

    def with_core(blocks):
        return blocks + [swap(v, core[0]) for v in blocks]

    grad_final = (live_mask * cotangent.astype(jnp.float32)).astype(jnp.bfloat16)
    middle = len(orders[0]) // 2
    z_first, last = 1, len(zs) + len(ys) - 1
    mixer = [gather_steps(v, order[:1]) for v, order in zip(mixer, orders)]
    mixer, small, tokens = tie(mixer, small, tokens)
    mixer = [gather_steps(v, order[1:middle]) for v, order in zip(mixer, orders)]
    before = lax.ppermute(
        tokens[tok_rows - HALO :], "seq", [(i, i + 1) for i in range(n_seq - 1)]
    )
    small = gather_steps(small[None], small_order)
    mixer, gate_weight, up_weight = tie(mixer, gate_weight, up_weight)
    mixer = [gather_steps(v, order[middle:-1]) for v, order in zip(mixer, orders)]
    gate_up = [
        gather_steps(v[None], p.steps[:z_first])
        for v, p in zip((gate_weight, up_weight), (*gate, *up))
    ]
    extended = jnp.concatenate([before, tokens], axis=0)
    places = jnp.stack([jnp.int32(masks_at(p, small_order)[1]) for p in range(n_seq)])
    chosen = (own_seq ^ jnp.arange(n_seq))[:, None] == places[None]
    consts = jnp.einsum(
        "sp,pkc->ksc",
        chosen.astype(jnp.bfloat16),
        small[:, :8, :small_cols],
        preferred_element_type=jnp.float32,
    ).reshape(8, features)
    mixer, gate_up, consts, extended, down_weight, grad_final = tie(
        mixer, gate_up, consts, extended, down_weight, grad_final
    )
    stacks = [last_step(v, order[-1]) for v, order in zip(mixer, orders)]
    stacks, gate_up, down_weight, grad_final = tie(stacks, gate_up, down_weight, grad_final)

    def in_view(low, high):

        def view(ref, dp, seq):
            row = pl.multiple_of(seq * in_rows, in_rows)
            col = pl.multiple_of(dp * in_cols + low, 128)
            return ref.at[pl.ds(row, in_rows), pl.ds(col, high - low)]

        return view

    def out_view(ref, dp, seq):
        return tile_of(ref, seq, out_rows, dp, out_cols)

    in_pieces = [
        Piece(order, (in_rows, in_cuts[i + 1] - in_cuts[i]), in_view(in_cuts[i], in_cuts[i + 1]))
        for i, order in enumerate(in_orders)
    ]
    half_block = gate_rows // 2

    def half_view(low):
        def view(ref, dp, seq):
            row = pl.multiple_of(seq * gate_rows + low, half_block)
            return ref.at[pl.ds(row, half_block)]

        return view

    feed_grads = [
        Piece(order, (half_block, hidden_units), half_view(low))
        for order, low in ((near_order, 0), (far_order, half_block))
    ]
    in_grads = [
        Piece(order, (in_rows, third), in_view(i * third, (i + 1) * third))
        for i, order in enumerate((in_orders[0], ys + zs + xs + core, out_order))
    ]
    out_grads = [Piece(zs + xs + ys + core, out_weight.shape, out_view)]
    out_pieces = [Piece(out_order, out_weight.shape, out_view)]
    in_stacks, out_stacks = stacks[0] + stacks[1], stacks[2]

    gate_up = [gather_steps(v, p.steps[z_first:last]) for v, p in zip(gate_up, (*gate, *up))]
    down_shard = lax.ppermute(down_weight, ("dp", "seq"), home)
    final_there = dp_gather(grad_final, xs)[1:]
    final_near = swap(grad_final, core[0])
    forward = mixer_forward(
        ids, extended, consts, in_pieces, in_stacks, out_pieces, out_stacks, slot_size
    )
    forward, gate_up, down_shard, grad_final, final_near, final_there = tie(
        forward, gate_up, down_shard, grad_final, final_near, final_there
    )
    normed_one, b_part, c_part, x_part, mixed, gated, hidden, normed_two = forward

    wide = (features, hidden_units)
    gate_stacks, up_stacks = [last_step(v, p.steps[-1]) for v, p in zip(gate_up, (*gate, *up))]
    down_stack = gather_steps(down_shard[None], near_order[:z_first])
    normed_there = dp_gather(normed_two, xs)[1:]
    final_blocks = [grad_final, final_near] + with_core(final_there)
    normed_two, normed_there, gate_stacks, up_stacks, down_stack, final_blocks = tie(
        normed_two, normed_there, gate_stacks, up_stacks, down_stack, final_blocks
    )
    downs = [down_stack[:, a:b] for a, b in zip(cuts, cuts[1:])]
    normed_blocks = with_core([normed_two]) + with_core(normed_there)
    normed_blocks, downs, gate_stacks, up_stacks = tie(normed_blocks, downs, gate_stacks, up_stacks)
    downs = [gather_steps(v, p.steps[z_first:last]) for v, p in zip(downs, down)]
    activated, slope, silu, normed_all = feed_up(ids, normed_blocks, gate, gate_stacks, up, up_stacks, wide)
    activated, downs = tie(activated, downs)
    down_stacks = [v for stack, p in zip(downs, down) for v in last_step(stack, p.steps[-1])]
    down_parts = weight_gradient(ids, [activated], final_blocks, down)
    down_parts, down_stacks = tie(down_parts, down_stacks)

    def sent(parts, pieces, place):
        return [exchanged(v, p.steps[place]) for v, p in zip(parts, pieces)]

    def fold_all(parts):
        return [folded(v) for v in parts]

    def sent_on(parts, pieces):
        count = len(pieces[0].steps)
        for place in range(count - 2, 0, -1):
            parts = sent(fold_all(parts) if place < count - 2 else parts, pieces, place)
        return parts

    def joined(parts):
        return [tuple(jnp.concatenate(v, axis=1) for v in zip(*parts))]

    def core_halves(v):
        near, far = v[:2], v[2:]
        half = len(far) // 2
        return near[0], near[1], far[:half], far[half:]

    def far_added(keep, come):
        return [
            (a.astype(jnp.float32) + b.astype(jnp.float32)).astype(jnp.bfloat16)
            for a, b in zip(keep, come)
        ]

    down_parts = sent(down_parts, down, -1)
    grad_gate, grad_up, *back = feed_back(
        ids, final_blocks, activated, slope, silu, gate, gate_stacks, up, up_stacks, down, down_stacks, wide
    )
    back, feed = back[:n_dp], back[n_dp:]
    back, feed, grad_gate, grad_up, down_parts = tie(back, feed, grad_gate, grad_up, down_parts)
    near, near_send, far, far_send = core_halves(back)
    far_come = [swap(v, core[0]) for v in far_send]
    down_parts = sent_on(fold_all(down_parts), down)
    far, far_come, near, near_send, grad_gate, grad_up, feed, down_parts = tie(
        far, far_come, near, near_send, grad_gate, grad_up, feed, down_parts
    )
    far = far_added(far, far_come)
    half_rows = tok_rows // 2
    far_low, far_high = [v[:half_rows] for v in far], [v[half_rows:] for v in far]
    down_parts = joined(fold_all(down_parts))
    far_low, far_high, down_parts, near, near_send, grad_gate, grad_up, feed = tie(
        far_low, far_high, down_parts, near, near_send, grad_gate, grad_up, feed
    )
    far_low = dp_scatter([None] + far_low, xs)
    near_more = swap(near_send, core[0])
    down_parts = sent(down_parts, down, 0)
    gate_parts = weight_gradient(ids, [normed_all], [grad_gate], feed_grads, by_rows=True)
    gate_parts, far_low, far_high, grad_up, near, near_more, down_parts, feed = tie(
        gate_parts, far_low, far_high, grad_up, near, near_more, down_parts, feed
    )
    own_down = folded(down_parts[0]).astype(jnp.bfloat16)
    feed_near, feed_send, feed_far, feed_come = core_halves(feed)
    own_down, gate_parts, feed_far, feed_come, grad_up, far_low, far_high = tie(
        own_down, gate_parts, feed_far, feed_come, grad_up, far_low, far_high
    )
    far_high = dp_scatter([None] + far_high, xs)
    gate_parts = sent(gate_parts, feed_grads, -1)
    feed_come = [swap(v, core[0]) for v in feed_come]
    up_parts = weight_gradient(ids, [normed_all], [grad_up], feed_grads, by_rows=True)
    up_parts, far_low, far_high, gate_parts, feed_far, feed_come, own_down = tie(
        up_parts, far_low, far_high, gate_parts, feed_far, feed_come, own_down
    )

    feed_far = far_added(feed_far, feed_come)
    feed_low, feed_high = [v[:half_rows] for v in feed_far], [v[half_rows:] for v in feed_far]
    feed_low, feed_high, up_parts, gate_parts, far_low, far_high, own_down = tie(
        feed_low, feed_high, up_parts, gate_parts, far_low, far_high, own_down
    )
    up_parts = sent(up_parts, feed_grads, -1)
    feed_low = dp_scatter([None] + feed_low, xs)
    own_down = lax.ppermute(own_down, ("dp", "seq"), [(b, a) for a, b in home])
    grad_hidden, grad_c, grad_mixed, first_rows, sums, out_parts = mixer_back(
        ids,
        [near, near_more, grad_final, hidden, c_part, gated],
        far_low + far_high,
        mixed,
        consts,
        out_pieces,
        out_stacks,
        out_grads,
        slot_size,
    )
    out_parts, grad_mixed, first_rows, gate_parts, up_parts, feed_low, feed_high, own_down = tie(
        out_parts, grad_mixed, first_rows, gate_parts, up_parts, feed_low, feed_high, own_down
    )
    returned = lax.ppermute(first_rows, "seq", [(i + 1, i) for i in range(n_seq - 1)])
    out_parts = fold_all(sent(out_parts, out_grads, -1))
    gate_parts, up_parts = fold_all(gate_parts), fold_all(up_parts)
    returned, out_parts, up_parts, gate_parts, feed_high = tie(
        returned, out_parts, up_parts, gate_parts, feed_high
    )
    gate_parts = sent_on(gate_parts, feed_grads)
    up_parts = sent_on(up_parts, feed_grads)
    feed_high = dp_scatter([None] + feed_high, xs)
    grad_proj, in_parts = projection_gradient(
        ids, normed_one, grad_mixed, returned, grad_c, b_part, x_part, in_grads
    )
    in_parts, up_parts, gate_parts, grad_proj, out_parts, feed_high = tie(
        in_parts, up_parts, gate_parts, grad_proj, out_parts, feed_high
    )
    gate_parts = joined(fold_all(gate_parts))
    in_parts, gate_parts, out_parts, grad_proj = tie(in_parts, gate_parts, out_parts, grad_proj)
    in_parts = sent(in_parts, in_grads, -1)
    out_parts = sent(out_parts, out_grads, -2)
    gate_parts = sent(gate_parts, feed_grads, 0)
    grad_tokens, sums = mixer_first(ids, grad_proj, tokens, grad_hidden, sums, consts, in_pieces, in_stacks)
    in_parts, out_parts, sums, gate_parts, up_parts, feed_send = tie(
        in_parts, out_parts, sums, gate_parts, up_parts, feed_send
    )
    sum_steps = core + xs + ys + zs[::-1]
    for step in sum_steps[:1]:
        sums = sums + swap(sums, step)
    in_parts, out_parts, up_parts = fold_all(in_parts), fold_all(out_parts), joined(fold_all(up_parts))
    in_parts, out_parts, up_parts, sums = tie(in_parts, out_parts, up_parts, sums)
    in_parts = sent(in_parts, in_grads, -2)
    sums = (sums, swap(sums, sum_steps[1]))
    in_parts, out_parts, up_parts, sums, feed_send = tie(in_parts, out_parts, up_parts, sums, feed_send)
    in_parts, sums = fold_all(in_parts), sums[0] + sums[1]
    in_parts, out_parts, up_parts, sums = tie(in_parts, out_parts, up_parts, sums)
    in_parts = sent(in_parts, in_grads, -3)
    out_parts = sent(out_parts, out_grads, -3)
    up_parts = sent(up_parts, feed_grads, 0)
    sums = (sums, swap(sums, sum_steps[2]))
    in_parts, out_parts, up_parts, sums, feed_send = tie(in_parts, out_parts, up_parts, sums, feed_send)
    in_parts, out_parts, sums = fold_all(in_parts), fold_all(out_parts), sums[0] + sums[1]
    in_parts, out_parts, sums = tie(in_parts, out_parts, sums)
    in_parts = sent(in_parts, in_grads, -4)
    out_parts = sent(out_parts, out_grads, -4)
    sums = (sums, swap(sums, sum_steps[3]))
    feed_more = swap(feed_send, core[0])
    in_parts, out_parts, sums, feed_more, own_down = tie(in_parts, out_parts, sums, feed_more, own_down)
    sums = sums[0] + sums[1]
    for step in sum_steps[4:]:
        sums = sums + swap(sums, step)
    own_down = own_down.astype(jnp.float32)

    def rest(parts, piece, done):
        parts = folded(parts)
        for place in range(len(piece.steps) - done - 1, -1, -1):
            parts = folded(exchanged(parts, piece.steps[place]))
        return parts

    own_in = [rest(v, p, 4) for v, p in zip(in_parts, in_grads)]
    own_in = jnp.concatenate(own_in, axis=1)
    own_out = rest(out_parts[0], out_grads[0], 4)
    own_gate = folded(gate_parts[0])
    own_up = folded(up_parts[0])
    own_sums = lax.dynamic_slice(sums, (0, own_seq * small_cols), (8, small_cols))
    feed_out = jnp.concatenate(feed_low + feed_high, axis=0).astype(jnp.float32)
    feed_out = feed_out + feed_near.astype(jnp.float32) + feed_more.astype(jnp.float32)
    output = (live_mask * (hidden + feed_out)).astype(jnp.bfloat16)
    return (
        output,
        grad_tokens,
        own_sums[0],
        own_in,
        own_sums[2:5],
        own_out,
        own_sums[1],
        own_gate,
        own_up,
        own_down,
    )


def solution(mesh):
    in_specs = (
        P(("dp", "seq"), None),
        P("seq"),
        P("seq", "dp"),
        P(None, "seq"),
        P("seq", "dp"),
        P("seq"),
        P("seq", "dp"),
        P("seq", "dp"),
        P("seq", "dp"),
        P("dp", None),
        P(("dp", "seq"), None),
    )
    out_specs = (
        P(("dp", "seq"), None),
        P(("dp", "seq"), None),
        P("seq"),
        P("seq", "dp"),
        P(None, "seq"),
        P("seq", "dp"),
        P("seq"),
        P("seq", "dp"),
        P("seq", "dp"),
        P("seq", "dp"),
    )
    return jax.shard_map(
        per_device, mesh=mesh, in_specs=in_specs, out_specs=out_specs, check_vma=False
    )
```
